32 devices in a mesh: inst: 4 (over x, core), axial: 8 (over z, y).
Axes of the slice: x: 2, y: 2, z: 4, core: 2. Of those that a mesh axis runs over, the one named last changes fastest.
Arguments:
- flow_state: float32 [16, 128, 320], P('inst', 'axial'), may hold values from -6 to 6
- forcing: float32 [16, 128, 320], P('inst', 'axial'), may hold values from -6 to 6
- tile_inverse: bfloat16 [128, 320, 320], P('axial')
- coupling: bfloat16 [128, 320, 320], P('axial')
- sweep_order: int32 [128], P('axial'), may hold values from 0 to 15, as said below
Outputs:
- final_state: float32 [16, 128, 320], P('inst', 'axial')
The draws below stay inside these ranges and needn't reach their ends.
Inputs may be any that keep to these rules, and one draw needn't show every extreme that they name: `sweep_order`: the 16 entries of each axial group form a permutation of 0 to 15.
All inputs are finite; a program needn't handle non-finite values.
Results may differ from the reference program's by a relative error of at most 0.0003.
Values sent between devices are 32-bit elements; how exact they have to be, the bound alone decides.
No kernel may reach another device: no remote copies, remote signals or barrier semaphores. Data moves between devices by JAX's collectives and lax.ppermute only.
A program may use at most 128 MiB of HBM per device.

```python
import math
import jax
import jax.numpy as jnp
from jax import lax

B = 320
INSTANCES = 16
TILES_DEV = 16
SLAB_TILE_COUNT = 128
ITERS = 2
N_AXIAL = 8


def draw_tile_inverse(key, part):
    noise = jax.random.normal(key, (SLAB_TILE_COUNT, B, B), jnp.float32)
    eye_block = jnp.eye(B, dtype=jnp.float32)
    return (0.5 * eye_block[None] + 0.02 / math.sqrt(B) * noise).astype(jnp.bfloat16)


def draw_coupling(key, part):
    key_rates = jax.random.fold_in(key, 11)
    pulse_group_key = jax.random.fold_in(key, 13)
    key_noise = jax.random.fold_in(key, 17)
    upper = math.log(max(SLAB_TILE_COUNT / 30.0, 0.5))
    decay = jnp.exp(jax.random.uniform(key_rates, (B,), jnp.float32, math.log(0.1), upper))
    relaxation_rates = 2.0 * jnp.exp(-decay / SLAB_TILE_COUNT)
    pulse_group = jax.random.randint(pulse_group_key, (SLAB_TILE_COUNT, 1), 0, SLAB_TILE_COUNT) < 3
    per_tile_relaxation = relaxation_rates[None, :] * jnp.where(pulse_group, 0.6, 1.0)
    noise = jax.random.normal(key_noise, (SLAB_TILE_COUNT, B, B), jnp.float32)
    eye_block = jnp.eye(B, dtype=jnp.float32)
    blocks = -(eye_block[None] * per_tile_relaxation[:, None, :]) + 0.04 / math.sqrt(B) * noise
    return blocks.astype(jnp.bfloat16)


def draw_sweep_order(key, part):
    scores = jax.random.randint(key, (N_AXIAL, TILES_DEV), 0, 1 << 20) * TILES_DEV
    scores = scores + jnp.arange(TILES_DEV, dtype=jnp.int32)[None, :]
    ranks = jnp.argsort(scores, axis=1, stable=True).astype(jnp.int32)
    return ranks.reshape(SLAB_TILE_COUNT)


def block_levels(key, extent, cuts, low, high):
    gain = 1.0
    for dim, shards_of in cuts:
        heights = jax.random.uniform(jax.random.fold_in(jax.random.fold_in(key, 6), dim), (shards_of,), jnp.float32, low / len(cuts), high / len(cuts))
        gain = gain * jnp.repeat(jnp.exp(heights), extent[dim] // shards_of).reshape((-1,) + (1,) * (len(extent) - 1 - dim))
    return gain


def scatter_about(stream_key, extent, scale, bound, pieces=(), held_as=jnp.bfloat16):
    factor_of = block_levels(stream_key, extent, pieces, -0.22, 0.18) if pieces else 1.0
    result = jax.random.normal(stream_key, extent, jnp.float32) * scale * factor_of
    return jnp.minimum(jnp.maximum(result, -bound), bound).astype(held_as)


def setup_inputs(seed: int = 0) -> dict:
    keys = jax.random.split(jax.random.key(seed), 6)
    flow_state = scatter_about(keys[0], (INSTANCES, SLAB_TILE_COUNT, B), 1.0, 6.0, ((0, 4), (1, 8)), jnp.float32)
    forcing = scatter_about(keys[1], (INSTANCES, SLAB_TILE_COUNT, B), 1.0, 6.0, ((0, 4), (1, 8)), jnp.float32)
    tile_inverse = draw_tile_inverse(jax.random.fold_in(keys[5], 71), 0)
    coupling = draw_coupling(jax.random.fold_in(keys[5], 71), 0)
    sweep_order = draw_sweep_order(jax.random.fold_in(keys[5], 71), 0)
    return {"flow_state": flow_state, "forcing": forcing, "tile_inverse": tile_inverse, "coupling": coupling, "sweep_order": sweep_order}


highest = lax.Precision.HIGHEST
spectral_gain = 2.0


def spectral_rows(row_ids, col_ids, period):
    distance = row_ids[:, None] - col_ids[None, :]
    parity = 1.0 - 2.0 * jnp.mod(distance, 2).astype(jnp.float32)
    angles = jnp.pi * distance.astype(jnp.float32) / period
    on_diag = distance == 0
    sine_safe = jnp.where(on_diag, 1.0, jnp.sin(angles))
    return jnp.where(on_diag, 0.0, 0.5 * parity * jnp.cos(angles) / sine_safe)


def visit_tile(upstream, tile_items):
    right_side, inverse, couple_tile = tile_items
    collapsed_result = right_side - jnp.dot(upstream, couple_tile.astype(jnp.float32).T, precision=highest)
    updated = jnp.dot(collapsed_result, inverse.astype(jnp.float32).T, precision=highest)
    return updated, updated


def reference(flow_state, forcing, tile_inverse, coupling, sweep_order):
    period = flow_state.shape[0]
    total_tiles = flow_state.shape[1]
    width = flow_state.shape[2]
    positions = jnp.arange(total_tiles, dtype=jnp.int32)
    visit_ids = (positions // TILES_DEV) * TILES_DEV + sweep_order.astype(jnp.int32)
    inst_ids = jnp.arange(period, dtype=jnp.int32)
    derivative = spectral_rows(inst_ids, inst_ids, period) * (spectral_gain / period)
    inverse_seq = tile_inverse[visit_ids]
    couple_seq = coupling[visit_ids]
    for repeat in range(ITERS):
        source_term = jnp.einsum("ij,jtb->itb", derivative, flow_state, precision=highest)
        right_side = forcing - source_term - flow_state
        ordered = jnp.swapaxes(right_side[:, visit_ids], 0, 1)
        start_zero = jnp.zeros((period, width), jnp.float32)
        _, updates = lax.scan(visit_tile, start_zero, (ordered, inverse_seq, couple_seq))
        increment = jnp.zeros_like(flow_state).at[:, visit_ids].set(jnp.swapaxes(updates, 0, 1))
        flow_state = flow_state + increment
    return flow_state
```

```python
import functools

import jax
import jax.numpy as jnp
import numpy as np
from jax import lax
from jax.experimental import pallas as pl
from jax.experimental.pallas import tpu as pltpu
from jax.sharding import PartitionSpec as P

NT = (((1,), (1,)), ((), ()))
NN = (((1,), (0,)), ((), ()))
bf16 = jnp.bfloat16
f32 = jnp.float32


def mixing_matrices(period):
    distance = np.arange(period)[:, None] - np.arange(period)[None, :]
    angles = np.pi * distance / period
    sine = np.where(distance == 0, 1.0, np.sin(angles))
    parity = 1.0 - 2.0 * (distance % 2)
    derivative = np.where(distance == 0, 0.0, 0.5 * parity * np.cos(angles) / sine)
    mix = derivative * (2.0 / period) + np.eye(period)
    return mix, mix @ mix


def split(value):
    high = value.astype(bf16)
    return high, (value - high.astype(f32)).astype(bf16)


def tall_dot(value, matrix):
    rows = value.shape[0]
    high, low = split(value)
    both = lax.dot_general(jnp.concatenate([high, low], 0), matrix, NT, preferred_element_type=f32)
    return both[:rows] + both[rows:]


def twin_dot(value, matrix):
    rows = value.shape[0]
    high = value.astype(bf16).astype(f32)
    upper = lax.broadcasted_iota(jnp.int32, value.shape, 0) < rows // 2
    parts = jnp.where(upper, high, value - high).astype(bf16)
    both = lax.dot_general(parts, matrix, NT, preferred_element_type=f32)
    return both + pltpu.roll(both, rows // 2, 0)


def map_kernel(order, inverse, coupling, p_out, q_out):
    tiles, width, _ = inverse.shape
    ids = lax.broadcasted_iota(jnp.int32, (width, width), 0)
    cols = lax.broadcasted_iota(jnp.int32, (width, width), 1)
    p_out[...] = (ids == cols).astype(f32)
    q_out[...] = jnp.zeros((width, width), f32)

    def step(k, carry):
        tile = order[k]
        p = p_out[...]
        q = q_out[...]
        p = -tall_dot(tall_dot(p, coupling[tile]), inverse[tile])
        p_out[...] = p
        q_out[...] = -tall_dot(p + tall_dot(q, coupling[tile]), inverse[tile])
        return carry

    lax.fori_loop(0, tiles, step, 0)


def group_maps(order, inverse, coupling):
    width = inverse.shape[1]
    shape = jax.ShapeDtypeStruct((width, width), f32)
    return pl.pallas_call(
        map_kernel,
        out_shape=(shape, shape),
        in_specs=[
            pl.BlockSpec(memory_space=pltpu.SMEM),
            pl.BlockSpec(memory_space=pltpu.VMEM),
            pl.BlockSpec(memory_space=pltpu.VMEM),
        ],
        name="group_maps",
        compiler_params=pltpu.CompilerParams(vmem_limit_bytes=56 << 20),
    )(order, inverse, coupling)


def sweep_kernel(all_tiles, order, inverse, coupling, right, inflow, out):
    tiles, width, _ = inverse.shape
    rows = inflow.shape[0] // 2
    a = inflow[:rows]
    w = inflow[rows:]
    for k in range(tiles):
        tile = order[k]
        a = twin_dot(right[tile, :rows] - twin_dot(a, coupling[tile]), inverse[tile])
        w = twin_dot(right[tile, rows:] - a - twin_dot(w, coupling[tile]), inverse[tile])
        if all_tiles:
            out[tile] = w
    if not all_tiles:
        out[:rows] = a
        out[rows:] = w


def sweep(all_tiles, order, inverse, coupling, right, inflow):
    tiles, rows, width = right.shape
    shape = (tiles, rows // 2, width) if all_tiles else (rows, width)
    vmem = pl.BlockSpec(memory_space=pltpu.VMEM)
    return pl.pallas_call(
        functools.partial(sweep_kernel, all_tiles),
        out_shape=jax.ShapeDtypeStruct(shape, f32),
        in_specs=[pl.BlockSpec(memory_space=pltpu.SMEM), vmem, vmem, vmem, vmem],
        name="sweep_all" if all_tiles else "sweep_last",
        compiler_params=pltpu.CompilerParams(vmem_limit_bytes=56 << 20),
    )(order, inverse, coupling, right, inflow)


def full_dot(value, matrix):
    high, low = split(value)
    matrix_high, matrix_low = split(matrix)
    rows = value.shape[0]
    both = lax.dot_general(jnp.concatenate([high, low], 0), matrix_high, NN, preferred_element_type=f32)
    return both[:rows] + both[rows:] + lax.dot_general(high, matrix_low, NN, preferred_element_type=f32)


def carried(value, p, q):
    rows = value.shape[0] // 2
    moved = full_dot(value, p)
    return moved + jnp.concatenate([jnp.zeros_like(value[:rows]), full_dot(value[:rows], q)], 0)


def carry_kernel(count, value, *refs):
    maps, start, out = refs[: 2 * count], refs[2 * count], refs[2 * count + 1]
    moved = value[...]
    for i in range(count):
        moved = carried(moved, maps[2 * i][...], maps[2 * i + 1][...])
    out[...] = moved + start[...]


def carry(value, maps, start):
    return pl.pallas_call(
        functools.partial(carry_kernel, len(maps)),
        out_shape=jax.ShapeDtypeStruct(value.shape, f32),
        name="carry",
    )(value, *[part for pair in maps for part in pair], start)


def compose_kernel(p_first, q_first, p_then, q_then, p_out, q_out):
    p = p_first[...]
    p_out[...] = full_dot(p, p_then[...])
    q_out[...] = full_dot(p, q_then[...]) + full_dot(q_first[...], p_then[...])


def compose(first, then):
    shape = jax.ShapeDtypeStruct(first[0].shape, f32)
    return pl.pallas_call(compose_kernel, out_shape=(shape, shape), name="compose")(*first, *then)


def on_device(flow_state, forcing, tile_inverse, coupling, sweep_order):
    local, tiles, width = flow_state.shape
    groups = lax.axis_size("axial")
    period = lax.axis_size("inst") * local
    mix, mix_twice = mixing_matrices(period)
    eye = np.eye(period)
    first = np.concatenate([-mix_twice, mix], 1)
    second = np.concatenate([-2.0 * mix, 2.0 * eye], 1)
    mine = lax.axis_index("inst") * local
    first = lax.dynamic_slice_in_dim(jnp.asarray(first, f32), mine, local, 0)
    second = lax.dynamic_slice_in_dim(jnp.asarray(second, f32), mine, local, 0)
    weights = jnp.concatenate([first, first, second, second], 0)

    both = jnp.stack([flow_state, forcing], 0)
    both = lax.all_gather(both, "inst", axis=1, tiled=True).reshape(2 * period, tiles, width)
    own_map = group_maps(sweep_order, tile_inverse, coupling)
    right = jnp.einsum("ij,jtb->tib", weights, both, precision=lax.Precision.HIGHEST)
    nothing = jnp.zeros((4 * local, width), f32)
    ends = sweep(False, sweep_order, tile_inverse, coupling, right, nothing)
    ends = jnp.concatenate([ends[:local], ends[2 * local : 3 * local]], 0)

    inflow = jnp.zeros_like(ends)
    ahead = []
    through = own_map
    step = 1
    while step < groups:
        pairs = [(g, g + step) for g in range(groups - step)]
        arrived = lax.ppermute(ends, "axial", pairs)
        inflow = carry(arrived, ahead, inflow) if ahead else arrived
        if 2 * step < groups:
            arrived_map = tuple(lax.ppermute(part, "axial", pairs) for part in through)
            ahead = [arrived_map] + ahead
            ends = carry(arrived, [through], ends)
            if 4 * step < groups:
                through = compose(arrived_map, through)
        step *= 2
    a, w = inflow[:local], inflow[local:]
    inflow = jnp.concatenate([a, a, w, w], 0)
    updates = sweep(True, sweep_order, tile_inverse, coupling, right, inflow)
    return flow_state + jnp.swapaxes(updates[:, :local], 0, 1)


def solution(mesh):
    return jax.shard_map(
        on_device,
        mesh=mesh,
        in_specs=(
            P("inst", "axial", None),
            P("inst", "axial", None),
            P("axial", None, None),
            P("axial", None, None),
            P("axial"),
        ),
        out_specs=P("inst", "axial", None),
        check_vma=False,
    )
```

```python
import functools

import jax
import jax.numpy as jnp
import numpy as np
from jax import lax
from jax.experimental import pallas as pl
from jax.experimental.pallas import tpu as pltpu
from jax.sharding import PartitionSpec as P

NT = (((1,), (1,)), ((), ()))
NN = (((1,), (0,)), ((), ()))
bf16 = jnp.bfloat16
f32 = jnp.float32
SMEM = pl.BlockSpec(memory_space=pltpu.SMEM)
VMEM = pl.BlockSpec(memory_space=pltpu.VMEM)
CORES = 2


def params():
    return pltpu.CompilerParams(vmem_limit_bytes=48 << 20)


def mixing_table(devices, local):
    period = devices * local
    distance = np.arange(period)[:, None] - np.arange(period)[None, :]
    angles = np.pi * distance / period
    sine = np.where(distance == 0, 1.0, np.sin(angles))
    parity = 1.0 - 2.0 * (distance % 2)
    derivative = np.where(distance == 0, 0.0, 0.5 * parity * np.cos(angles) / sine)
    eye = np.eye(period)
    mix = derivative * (2.0 / period) + eye
    of_state = np.stack([-mix @ mix, -2.0 * mix])
    of_forcing = np.stack([mix, 2.0 * eye])
    table = []
    for i in range(devices):
        rows = np.arange(CORES * local) + (i // CORES) * CORES * local
        blocks = []
        for s in range(devices):
            columns = np.arange(local) + (i ^ s) * local
            for part in (of_state, of_forcing):
                blocks.append(part[:, rows][:, :, columns].reshape(-1, local))
        table.append(np.concatenate(blocks, 1))
    table = np.stack(table).astype(np.float32)
    high = table.astype(bf16)
    low = (table - high.astype(np.float32)).astype(bf16)
    return np.concatenate([high, low, high], 2)


def split(value):
    high = value.astype(bf16)
    return high, (value - high.astype(f32)).astype(bf16)


def wide_dot(value, matrix):
    parts = jnp.concatenate(split(value), 1)
    return lax.dot_general(parts, jnp.concatenate([matrix, matrix], 1), NT, preferred_element_type=f32)


def tall_dot(value, matrix):
    rows = value.shape[0]
    both = lax.dot_general(jnp.concatenate(split(value), 0), matrix, NT, preferred_element_type=f32)
    return both[:rows] + both[rows:]


def full_dot(value, matrix):
    high, low = split(value)
    matrix_high, matrix_low = split(matrix)
    rows = value.shape[0]
    both = lax.dot_general(jnp.concatenate([high, low], 0), matrix_high, NN, preferred_element_type=f32)
    return both[:rows] + both[rows:] + lax.dot_general(high, matrix_low, NN, preferred_element_type=f32)


def pack_kernel(order, core, state, forcing, mine, other):
    local, tiles, _ = state.shape
    half = tiles // CORES
    for out, start in ((mine, core[0] * half), (other, (1 - core[0]) * half)):
        for k in range(half):
            tile = order[start + k]
            for i in range(local):
                out[k, pl.ds(i, 1), :] = state[i, pl.ds(tile, 1), :]
                out[k, pl.ds(local + i, 1), :] = forcing[i, pl.ds(tile, 1), :]


def pack(order, core, state, forcing):
    local, tiles, width = state.shape
    shape = jax.ShapeDtypeStruct((tiles // CORES, 2 * local, width), f32)
    return pl.pallas_call(
        pack_kernel,
        out_shape=(shape, shape),
        in_specs=[SMEM, SMEM, VMEM, VMEM],
        name="pack",
    )(order, core, state, forcing)


def map_kernel(order, core, inverse, coupling, out, both):
    tiles, width, _ = inverse.shape
    half = tiles // CORES
    start = core[0] * half
    tile = order[start]
    p = -lax.dot_general(coupling[tile], inverse[tile], (((0,), (1,)), ((), ())), preferred_element_type=f32)
    both[:width] = p
    both[width:] = -wide_dot(p, inverse[tile])

    def step(k, carry):
        tile = order[start + k]
        turned = wide_dot(both[...], coupling[tile])
        p = -wide_dot(turned[:width], inverse[tile])
        both[:width] = p
        both[width:] = -wide_dot(p + turned[width:], inverse[tile])
        return carry

    lax.fori_loop(1, half, step, 0)
    out[0] = both[:width]
    out[1] = both[width:]


def half_maps(order, core, inverse, coupling):
    width = inverse.shape[1]
    return pl.pallas_call(
        map_kernel,
        out_shape=jax.ShapeDtypeStruct((2, width, width), f32),
        in_specs=[SMEM, SMEM, VMEM, VMEM],
        scratch_shapes=[pltpu.VMEM((2 * width, width), f32)],
        name="half_maps",
        compiler_params=params(),
    )(order, core, inverse, coupling)


def first_sweep_kernel(order, place, inverse, coupling, table, *refs):
    blocks, (right, ends) = refs[:-2], refs[-2:]
    tiles, width, _ = inverse.shape
    half = tiles // CORES
    start = place[0] * half
    rows = ends.shape[0] // 2
    weights = table[place[1]]
    a = jnp.zeros((rows, width), f32)
    w = jnp.zeros((rows, width), f32)
    for k in range(half):
        tile = order[start + k]
        high, low = split(jnp.concatenate([block[k] for block in blocks], 0))
        here = lax.dot_general(weights, jnp.concatenate([high, high, low], 0), NN, preferred_element_type=f32)
        right[k] = here
        a = tall_dot(here[:rows] - tall_dot(a, coupling[tile]), inverse[tile])
        w = tall_dot(here[rows:] - a - tall_dot(w, coupling[tile]), inverse[tile])
    ends[:rows] = a
    ends[rows:] = w


def first_sweep(order, place, inverse, coupling, table, blocks):
    width = inverse.shape[1]
    half = inverse.shape[0] // CORES
    rows = table.shape[1]
    return pl.pallas_call(
        first_sweep_kernel,
        out_shape=(jax.ShapeDtypeStruct((half, rows, width), f32), jax.ShapeDtypeStruct((rows, width), f32)),
        in_specs=[SMEM, SMEM] + [VMEM] * (3 + len(blocks)),
        name="first_sweep",
        compiler_params=params(),
    )(order, place, inverse, coupling, table, *blocks)


def carried(value, pair):
    p, q = pair
    rows = value.shape[0] // 2
    moved = full_dot(value, p)
    return jnp.concatenate([moved[:rows], moved[rows:] + full_dot(value[:rows], q)], 0)


def joined(mine, theirs, core):
    lower, upper = jnp.where(core == 0, mine[...], theirs[...]), jnp.where(core == 0, theirs[...], mine[...])
    return jnp.concatenate([lower[0], upper[0]], 0), jnp.concatenate([lower[1], upper[1]], 0)


def composed(first, then):
    rows = first.shape[1]
    moved = full_dot(jnp.concatenate([first[0], first[1]], 0), then[0])
    return moved[:rows], moved[rows:] + full_dot(first[0], then[1])


def group_kernel(core, mine, theirs, out):
    c = core[0]
    rows = out.shape[1]
    first = jnp.where(c == 0, mine[:, :rows], theirs[:, rows:])
    then = jnp.where(c == 0, theirs[...], mine[...])
    out[0], out[1] = composed(first, then)


def group_half(core, mine, theirs):
    _, width, _ = mine.shape
    return pl.pallas_call(
        group_kernel,
        out_shape=jax.ShapeDtypeStruct((2, width // CORES, width), f32),
        in_specs=[SMEM, VMEM, VMEM],
        name="group_half",
        compiler_params=params(),
    )(core, mine, theirs)


def pair_kernel(place, own, own_rest, partner, partner_rest, out):
    core, upper = place[0], place[2]
    first = jnp.where(upper == 1, partner[...], own[...])
    mine = jnp.where(upper == 1, own[...], partner[...])
    rest = jnp.where(upper == 1, own_rest[...], partner_rest[...])
    out[0], out[1] = composed(first, joined(mine, rest, core))


def pair_half(place, own, own_rest, partner, partner_rest):
    return pl.pallas_call(
        pair_kernel,
        out_shape=jax.ShapeDtypeStruct(own.shape, f32),
        in_specs=[SMEM] + [VMEM] * 4,
        name="pair_half",
        compiler_params=params(),
    )(place, own, own_rest, partner, partner_rest)


def compose_kernel(place, first, then, then_rest, out):
    out[0], out[1] = composed(first[...], joined(then, then_rest, place[0]))


def compose_half(place, first, then, then_rest):
    return pl.pallas_call(
        compose_kernel,
        out_shape=jax.ShapeDtypeStruct(first.shape, f32),
        in_specs=[SMEM] + [VMEM] * 3,
        name="compose_half",
        compiler_params=params(),
    )(place, first, then, then_rest)


def group_ends_kernel(core, map_mine, map_theirs, ends_mine, ends_theirs, out):
    c = core[0]
    first = jnp.where(c == 0, ends_mine[...], ends_theirs[...])
    last = jnp.where(c == 0, ends_theirs[...], ends_mine[...])
    then = jnp.where(c == 0, map_theirs[...], map_mine[...])
    out[...] = carried(first, then) + last


def group_ends(core, map_mine, map_theirs, ends_mine, ends_theirs):
    return pl.pallas_call(
        group_ends_kernel,
        out_shape=jax.ShapeDtypeStruct(ends_mine.shape, f32),
        in_specs=[SMEM] + [VMEM] * 4,
        name="group_ends",
        compiler_params=params(),
    )(core, map_mine, map_theirs, ends_mine, ends_theirs)


def pair_ends_kernel(place, own, own_rest, partner, partner_rest, ends, ends_partner, out):
    core, upper = place[0], place[2]
    mine = jnp.where(upper == 1, own[...], partner[...])
    rest = jnp.where(upper == 1, own_rest[...], partner_rest[...])
    first = jnp.where(upper == 1, ends_partner[...], ends[...])
    last = jnp.where(upper == 1, ends[...], ends_partner[...])
    out[...] = carried(first, joined(mine, rest, core)) + last


def pair_ends(place, own, own_rest, partner, partner_rest, ends, ends_partner):
    return pl.pallas_call(
        pair_ends_kernel,
        out_shape=jax.ShapeDtypeStruct(ends.shape, f32),
        in_specs=[SMEM] + [VMEM] * 6,
        name="pair_ends",
        compiler_params=params(),
    )(place, own, own_rest, partner, partner_rest, ends, ends_partner)


def carry_kernel(place, value, *refs):
    maps, start, out = refs[:-2], refs[-2], refs[-1]
    moved = value[...]
    for mine, rest in zip(maps[::2], maps[1::2]):
        moved = carried(moved, joined(mine, rest, place[0]))
    out[...] = moved + start[...]


def carry(place, value, maps, start):
    flat = [part for pair in maps for part in pair]
    return pl.pallas_call(
        carry_kernel,
        out_shape=jax.ShapeDtypeStruct(value.shape, f32),
        in_specs=[SMEM] + [VMEM] * (2 + len(flat)),
        name="carry",
        compiler_params=params(),
    )(place, value, *flat, start)


def last_sweep_kernel(order, place, inverse, coupling, right, inflow, partner, partner_rest, ends_partner,
                      map_mine, map_theirs, ends_mine, ends_theirs, out, at_group, at_half):
    tiles, width, _ = inverse.shape
    half = tiles // CORES
    core, upper = place[0], place[2]
    start = core * half
    rows = inflow.shape[0] // 2
    at_group[...] = inflow[...]

    @pl.when(upper == 1)
    def _():
        at_group[...] = carried(inflow[...], joined(partner, partner_rest, core)) + ends_partner[...]

    at_half[...] = at_group[...]

    @pl.when(core == 1)
    def _():
        at_half[...] = carried(at_group[...], map_theirs[...]) + ends_theirs[...]

    a = at_half[:rows]
    w = at_half[rows:]
    for k in range(half):
        tile = order[start + k]
        a = tall_dot(right[k, :rows] - tall_dot(a, coupling[tile]), inverse[tile])
        w = tall_dot(right[k, rows:] - a - tall_dot(w, coupling[tile]), inverse[tile])
        out[k] = w


def last_sweep(order, place, inverse, coupling, right, *rest):
    half, rows, width = right.shape
    return pl.pallas_call(
        last_sweep_kernel,
        out_shape=jax.ShapeDtypeStruct((half, rows // 2, width), f32),
        in_specs=[SMEM, SMEM] + [VMEM] * (3 + len(rest)),
        scratch_shapes=[pltpu.VMEM((rows, width), f32), pltpu.VMEM((rows, width), f32)],
        name="last_sweep",
        compiler_params=params(),
    )(order, place, inverse, coupling, right, *rest)


def finish_kernel(order, place, state, mine, theirs, out):
    local, tiles, _ = state.shape
    half = tiles // CORES
    core = place[0]
    for update, offset, start in ((mine, core * local, core * half), (theirs, 0, (1 - core) * half)):
        for k in range(half):
            tile = order[start + k]
            for i in range(local):
                out[i, pl.ds(tile, 1), :] = state[i, pl.ds(tile, 1), :] + update[k, pl.ds(offset + i, 1), :]


def finish(order, place, state, mine, theirs):
    return pl.pallas_call(
        finish_kernel,
        out_shape=jax.ShapeDtypeStruct(state.shape, f32),
        in_specs=[SMEM, SMEM] + [VMEM] * 3,
        name="finish",
    )(order, place, state, mine, theirs)


def on_device(state, forcing, inverse, coupling, order):
    local, tiles, width = state.shape
    groups = lax.axis_size("axial")
    devices = lax.axis_size("inst")
    me = lax.axis_index("inst")
    core = me % CORES
    place = jnp.stack([core, me, lax.axis_index("axial") % 2]).astype(jnp.int32)
    table = jnp.asarray(mixing_table(devices, local))

    def partnered(value, axis, bit):
        return lax.ppermute(value, axis, [(i, i ^ bit) for i in range(lax.axis_size(axis))])

    def passed(value, step):
        return lax.ppermute(value, "axial", [(g, g + step) for g in range(groups - step)])

    mine, other = pack(order, place, state, forcing)
    blocks = [mine] + [partnered(other if s % CORES else mine, "inst", s) for s in range(1, devices)]
    map_mine = half_maps(order, place, inverse, coupling)
    map_theirs = partnered(map_mine, "inst", 1)
    right, ends_mine = first_sweep(order, place, inverse, coupling, table, blocks)
    ends_theirs = partnered(ends_mine, "inst", 1)

    own = group_half(place, map_mine, map_theirs)
    own_rest = partnered(own, "inst", 1)
    partner = partnered(own, "axial", 1)
    partner_rest = partnered(partner, "inst", 1)
    through = pair_half(place, own, own_rest, partner, partner_rest)
    through_rest = partnered(through, "inst", 1)

    ends = group_ends(place, map_mine, map_theirs, ends_mine, ends_theirs)
    ends_partner = partnered(ends, "axial", 1)
    total = pair_ends(place, own, own_rest, partner, partner_rest, ends, ends_partner)
    inflow = jnp.zeros_like(total)
    ahead = []
    step = 2
    while step < groups:
        arrived = passed(total, step)
        inflow = carry(place, arrived, ahead, inflow) if ahead else arrived
        if 2 * step < groups:
            total = carry(place, arrived, [(through, through_rest)], total)
            arrived_map = passed(through, step)
            ahead = [(arrived_map, partnered(arrived_map, "inst", 1))] + ahead
            if 4 * step < groups:
                through = compose_half(place, arrived_map, through, through_rest)
                through_rest = partnered(through, "inst", 1)
        step *= 2

    updates = last_sweep(order, place, inverse, coupling, right, inflow, partner, partner_rest, ends_partner,
                         map_mine, map_theirs, ends_mine, ends_theirs)
    theirs = lax.dynamic_slice_in_dim(updates, (1 - core) * local, local, 1)
    return finish(order, place, state, updates, partnered(theirs, "inst", 1))


def solution(mesh):
    return jax.shard_map(
        on_device,
        mesh=mesh,
        in_specs=(
            P("inst", "axial", None),
            P("inst", "axial", None),
            P("axial", None, None),
            P("axial", None, None),
            P("axial"),
        ),
        out_specs=P("inst", "axial", None),
        check_vma=False,
    )
```

```python
import functools

import jax
import jax.numpy as jnp
import numpy as np
from jax import lax
from jax.experimental import pallas as pl
from jax.experimental.pallas import tpu as pltpu
from jax.sharding import PartitionSpec as P

NT = (((1,), (1,)), ((), ()))
NN = (((1,), (0,)), ((), ()))
bf16 = jnp.bfloat16
f32 = jnp.float32
SMEM = pl.BlockSpec(memory_space=pltpu.SMEM)
VMEM = pl.BlockSpec(memory_space=pltpu.VMEM)
HBM = pl.BlockSpec(memory_space=pltpu.HBM)
CORES = 2


def params():
    return pltpu.CompilerParams(vmem_limit_bytes=48 << 20)


def mixing(period):
    distance = np.arange(period)[:, None] - np.arange(period)[None, :]
    angles = np.pi * distance / period
    sine = np.where(distance == 0, 1.0, np.sin(angles))
    parity = 1.0 - 2.0 * (distance % 2)
    derivative = np.where(distance == 0, 0.0, 0.5 * parity * np.cos(angles) / sine)
    mix = derivative * (2.0 / period) + np.eye(period)
    return mix, mix @ mix


def mixing_tables(devices, local):
    period = devices * local
    mix, twice = mixing(period)
    eye, none = np.eye(period), np.zeros((period, period))
    rights, chains = [], []
    for i in range(devices):
        rows = np.arange(local) + i * local
        right, chain = [], []
        for s in range(devices):
            columns = np.arange(local) + (i ^ s) * local
            cut = lambda upper, lower: np.concatenate([upper[rows][:, columns], lower[rows][:, columns]], 0)
            right += [cut(mix, 2 * eye), cut(-twice, -2 * mix)]
            chain += [cut(mix, 2 * eye), cut(-twice, -2 * mix), cut(none, -mix), cut(none, twice)]
        rights.append(np.concatenate(right, 1))
        chains.append(np.concatenate(chain, 1))
    return np.stack(rights).astype(np.float32), np.stack(chains).astype(np.float32)


def split(value):
    high = value.astype(bf16)
    return high, (value - high.astype(f32)).astype(bf16)


def wide_dot(value, matrix):
    parts = jnp.concatenate(split(value), 1)
    return lax.dot_general(parts, jnp.concatenate([matrix, matrix], 1), NT, preferred_element_type=f32)


def tall_dot(value, matrix):
    rows = value.shape[0]
    both = lax.dot_general(jnp.concatenate(split(value), 0), matrix, NT, preferred_element_type=f32)
    return both[:rows] + both[rows:]


def full_dot(value, matrix):
    high, low = split(value)
    matrix_high, matrix_low = split(matrix)
    rows = value.shape[0]
    both = lax.dot_general(jnp.concatenate([high, low], 0), matrix_high, NN, preferred_element_type=f32)
    return both[:rows] + both[rows:] + lax.dot_general(high, matrix_low, NN, preferred_element_type=f32)


def chain_kernel(order, place, inverse_hbm, coupling_hbm, state, forcing, whole, middle, ends,
                 inverse, coupling, both, inverse_sem, coupling_sem):
    tiles, width, _ = inverse.shape
    local = state.shape[0]
    part = width // CORES
    rows = part + 2 * local

    def fetch(k):
        tile = order[k]
        return (
            pltpu.make_async_copy(coupling_hbm.at[tile], coupling.at[k], coupling_sem.at[k]),
            pltpu.make_async_copy(inverse_hbm.at[tile], inverse.at[k], inverse_sem.at[k]),
        )

    def arrive(k):
        for copy in fetch(k):
            copy.wait()

    for k in range(tiles):
        for copy in fetch(k):
            copy.start()

    def with_terms(k, turned):
        tile = order[k]
        terms = [array[i, pl.ds(tile, 1), :] for array in (forcing, state) for i in range(local)]
        return jnp.concatenate([-turned[:part], jnp.concatenate(terms, 0) - turned[part:]], 0)

    def keep(out, first):
        out[0] = both[:part]
        out[1] = both[rows : rows + part]
        ends[first : first + 2 * local] = both[part:rows]
        ends[first + 2 * local : first + 4 * local] = both[rows + part :]

    ids = lax.broadcasted_iota(jnp.int32, (rows, width), 0)
    columns = lax.broadcasted_iota(jnp.int32, (rows, width), 1)
    both[:rows] = jnp.where((ids < part) & (columns == ids + place[0] * part), 1.0, 0.0)
    both[rows:] = jnp.zeros((rows, width), f32)

    def step(k, carry):
        arrive(k)
        turned = wide_dot(both[...], coupling[k])
        first = wide_dot(with_terms(k, turned[:rows]), inverse[k])
        both[:rows] = first
        both[rows:] = wide_dot(first - turned[rows:], inverse[k])
        return carry

    lax.fori_loop(0, tiles // 2, step, 0, unroll=2)
    keep(middle, 4 * local)
    lax.fori_loop(tiles // 2, tiles, step, 0, unroll=2)
    keep(whole, 0)


def chain(order, place, inverse, coupling, state, forcing):
    local, tiles, width = state.shape
    part = width // CORES
    half = jax.ShapeDtypeStruct((2, part, width), f32)
    return pl.pallas_call(
        chain_kernel,
        out_shape=(half, half, jax.ShapeDtypeStruct((8 * local, width), f32)),
        in_specs=[SMEM, SMEM, HBM, HBM, VMEM, VMEM],
        scratch_shapes=[
            pltpu.VMEM((tiles, width, width), bf16),
            pltpu.VMEM((tiles, width, width), bf16),
            pltpu.VMEM((2 * (part + 2 * local), width), f32),
            pltpu.SemaphoreType.DMA((tiles,)),
            pltpu.SemaphoreType.DMA((tiles,)),
        ],
        name="chain",
        compiler_params=params(),
    )(order, place, inverse, coupling, state, forcing)


def carried(value, pair):
    p, q = pair
    rows = value.shape[0] // 2
    moved = full_dot(value, p)
    return jnp.concatenate([moved[:rows], moved[rows:] - full_dot(value[:rows], q)], 0)


def joined(mine, theirs, core):
    lower, upper = jnp.where(core == 0, mine[...], theirs[...]), jnp.where(core == 0, theirs[...], mine[...])
    return jnp.concatenate([lower[0], upper[0]], 0), jnp.concatenate([lower[1], upper[1]], 0)


def pick(flag, when_set, otherwise):
    return jnp.where(flag == 1, when_set[...], otherwise[...])


def pair_kernel(place, table, own, own_rest, partner, partner_rest, *refs):
    blocks, (total, beside, middle) = refs[:-3], refs[-3:]
    core, upper, me = place[0], place[1], place[2]
    weights = table[me]
    rows = total.shape[0]
    chains = 2 * rows

    def mixed(first):
        picked = [block[first + c * 2 * chains : first + c * 2 * chains + chains] for block in chosen for c in order_of]
        return jnp.dot(weights, jnp.concatenate(picked, 0), precision=lax.Precision.HIGHEST, preferred_element_type=f32)

    order_of = range(CORES)
    chosen = blocks[: len(blocks) // 2]
    mine = mixed(0)
    middle[...] = mixed(chains)
    chosen = blocks[len(blocks) // 2 :]
    other = mixed(0)
    beside[...] = other
    first = jnp.where(upper == 1, other, mine)
    last = jnp.where(upper == 1, mine, other)
    then = joined(pick(upper, own, partner), pick(upper, own_rest, partner_rest), core)
    total[...] = carried(first, then) + last


def pair_total(place, table, maps, blocks):
    rows, width = blocks[0].shape[0] // 8, blocks[0].shape[1]
    shape = jax.ShapeDtypeStruct((rows, width), f32)
    return pl.pallas_call(
        pair_kernel,
        out_shape=(shape, shape, shape),
        in_specs=[SMEM] + [VMEM] * (1 + len(maps) + len(blocks)),
        name="pair_total",
        compiler_params=params(),
    )(place, table, *maps, *blocks)


def carry_kernel(place, value, *refs):
    maps, start, out = refs[:-2], refs[-2], refs[-1]
    moved = value[...]
    for mine, rest in zip(maps[::2], maps[1::2]):
        moved = carried(moved, joined(mine, rest, place[0]))
    out[...] = moved + start[...]


def carry_pair_kernel(place, value, own, own_rest, partner, partner_rest, start, out):
    core, upper = place[0], place[1]
    moved = carried(value[...], joined(pick(upper, partner, own), pick(upper, partner_rest, own_rest), core))
    moved = carried(moved, joined(pick(upper, own, partner), pick(upper, own_rest, partner_rest), core))
    out[...] = moved + start[...]


def carry(place, value, maps, start, pair=False):
    return pl.pallas_call(
        carry_pair_kernel if pair else carry_kernel,
        out_shape=jax.ShapeDtypeStruct(value.shape, f32),
        in_specs=[SMEM] + [VMEM] * (2 + len(maps)),
        name="carry_pair" if pair else "carry",
        compiler_params=params(),
    )(place, value, *maps, start)


def composed(first, then, out):
    p, q = first
    rows = p.shape[0]
    moved = full_dot(jnp.concatenate([p, q], 0), then[0])
    out[0] = moved[:rows]
    out[1] = moved[rows:] + full_dot(p, then[1])


def compose_kernel(place, first, then, then_rest, out):
    composed((first[0], first[1]), joined(then, then_rest, place[0]), out)


def compose_pair_kernel(place, own, own_rest, partner, partner_rest, out):
    core, upper = place[0], place[1]
    first = pick(upper, partner, own)
    composed((first[0], first[1]), joined(pick(upper, own, partner), pick(upper, own_rest, partner_rest), core), out)


def compose(place, *maps, pair=False):
    return pl.pallas_call(
        compose_pair_kernel if pair else compose_kernel,
        out_shape=jax.ShapeDtypeStruct(maps[0].shape, f32),
        in_specs=[SMEM] + [VMEM] * len(maps),
        name="compose_pair" if pair else "compose",
        compiler_params=params(),
    )(place, *maps)


def sweep_kernel(order, place, inverse_hbm, coupling_hbm, right, state, inflow, partner, partner_rest, beside,
                 middle, middle_rest, middle_ends, out, inverse, coupling, at_group, inverse_sem, coupling_sem):
    tiles, width, _ = inverse.shape
    local = state.shape[0]
    half = tiles // 2
    core, upper = place[0], place[1]

    def fetch(k):
        tile = order[k]
        return (
            pltpu.make_async_copy(coupling_hbm.at[tile], coupling.at[k], coupling_sem.at[k]),
            pltpu.make_async_copy(inverse_hbm.at[tile], inverse.at[k], inverse_sem.at[k]),
        )

    for k in range(half):
        for copy in fetch(k) + fetch(k + half):
            copy.start()

    at_group[...] = inflow[...]

    @pl.when(upper == 1)
    def _():
        at_group[...] = carried(inflow[...], joined(partner, partner_rest, core)) + beside[...]

    starts = [at_group[...]]
    starts.append(carried(starts[0], joined(middle, middle_rest, core)) + middle_ends[...])
    a = [start[:local] for start in starts]
    w = [start[local:] for start in starts]
    for k in range(half):
        for s in range(2):
            j = k + s * half
            for copy in fetch(j):
                copy.wait()
            tile = order[j]
            here = right[tile]
            turned = tall_dot(jnp.concatenate([a[s], w[s]], 0), coupling[j])
            a[s] = tall_dot(here[:local] - turned[:local], inverse[j])
            w[s] = tall_dot(here[local:] - a[s] - turned[local:], inverse[j])
            for i in range(local):
                out[i, pl.ds(tile, 1), :] = state[i, pl.ds(tile, 1), :] + w[s][i : i + 1]


def sweep(order, place, inverse, coupling, right, state, *rest):
    local, tiles, width = state.shape
    return pl.pallas_call(
        sweep_kernel,
        out_shape=jax.ShapeDtypeStruct(state.shape, f32),
        in_specs=[SMEM, SMEM, HBM, HBM] + [VMEM] * (2 + len(rest)),
        scratch_shapes=[
            pltpu.VMEM((tiles, width, width), bf16),
            pltpu.VMEM((tiles, width, width), bf16),
            pltpu.VMEM((2 * local, width), f32),
            pltpu.SemaphoreType.DMA((tiles,)),
            pltpu.SemaphoreType.DMA((tiles,)),
        ],
        name="sweep",
        compiler_params=params(),
    )(order, place, inverse, coupling, right, state, *rest)


def on_device(state, forcing, inverse, coupling, order):
    local, tiles, width = state.shape
    groups = lax.axis_size("axial")
    devices = lax.axis_size("inst")
    me = lax.axis_index("inst")
    place = jnp.stack([me % CORES, lax.axis_index("axial") % 2, me]).astype(jnp.int32)
    right_table, chain_table = mixing_tables(devices, local)

    def over_inst(value, bit):
        return lax.ppermute(value, "inst", [(i, i ^ bit) for i in range(devices)])

    def over_both(value, inst_bit, axial_bit):
        pairs = [(i * groups + g, (i ^ inst_bit) * groups + (g ^ axial_bit)) for i in range(devices) for g in range(groups)]
        return lax.ppermute(value, ("inst", "axial"), pairs)

    def passed(value, step, bit=0):
        return lax.ppermute(value, "axial", [(g, (g + step) ^ bit) for g in range(groups - step)])

    def with_rest(value):
        return [value, over_inst(value, 1)]

    whole, middle, ends = chain(order, place, inverse, coupling, state, forcing)

    sibling = over_inst(ends, 1)
    chip = jnp.concatenate([ends, sibling], 0)
    blocks = [
        chip if not (s or y) else over_both(chip, s * CORES, y) for y in range(2) for s in range(devices // CORES)
    ]

    own = with_rest(whole)
    partner = with_rest(over_both(whole, 0, 1))
    if 4 < groups <= 8:
        straight = with_rest(passed(whole, 2))
        crossed = with_rest(passed(whole, 2, 1))
    middle_maps = with_rest(middle)

    both = jnp.stack([forcing, state], 0)
    parts = jnp.stack([both if not s else over_inst(both, s) for s in range(devices)], 0)
    weights = lax.dynamic_index_in_dim(jnp.asarray(right_table), me, 0, keepdims=False)
    weights = weights.reshape(2 * local, devices, 2, local)
    right = jnp.einsum("ispj,spjtb->tib", weights, parts, precision=lax.Precision.HIGHEST)

    total, beside, middle_ends = pair_total(place, jnp.asarray(chain_table), own + partner, blocks)
    inflow = jnp.zeros_like(total)
    ahead, through = [], []
    if groups > 8:
        through = with_rest(compose(place, *own, *partner, pair=True))
    step = 2
    while step < groups:
        arrived = passed(total, step)
        if step == 2:
            inflow = arrived
        else:
            inflow = carry(place, arrived, ahead, inflow, groups <= 8)
        if 2 * step < groups:
            if groups <= 8:
                total = carry(place, arrived, own + partner, total, True)
                ahead = straight + crossed
            else:
                total = carry(place, arrived, through, total)
                before = with_rest(passed(through[0], step))
                ahead = before + ahead
                through = with_rest(compose(place, before[0], *through))
        step *= 2
    return sweep(order, place, inverse, coupling, right, state, inflow, *partner, beside, *middle_maps, middle_ends)


def solution(mesh):
    return jax.shard_map(
        on_device,
        mesh=mesh,
        in_specs=(
            P("inst", "axial", None),
            P("inst", "axial", None),
            P("axial", None, None),
            P("axial", None, None),
            P("axial"),
        ),
        out_specs=P("inst", "axial", None),
        check_vma=False,
    )
```

```python
import functools

import jax
import jax.numpy as jnp
import numpy as np
from jax import lax
from jax.experimental import pallas as pl
from jax.experimental.pallas import tpu as pltpu
from jax.sharding import PartitionSpec as P

NT = (((1,), (1,)), ((), ()))
NN = (((1,), (0,)), ((), ()))
bf16 = jnp.bfloat16
f32 = jnp.float32
SMEM = pl.BlockSpec(memory_space=pltpu.SMEM)
VMEM = pl.BlockSpec(memory_space=pltpu.VMEM)
HBM = pl.BlockSpec(memory_space=pltpu.HBM)
CORES = 2


def params(mebibytes):
    return pltpu.CompilerParams(vmem_limit_bytes=mebibytes << 20)


def batches(count):
    edges = [0]
    while edges[-1] < count:
        edges.append(min(count, max(1, 2 * edges[-1])))
    return dict(zip(edges, edges[1:]))


def mixing(period):
    distance = np.arange(period)[:, None] - np.arange(period)[None, :]
    angles = np.pi * distance / period
    sine = np.where(distance == 0, 1.0, np.sin(angles))
    parity = 1.0 - 2.0 * (distance % 2)
    derivative = np.where(distance == 0, 0.0, 0.5 * parity * np.cos(angles) / sine)
    mix = derivative * (2.0 / period) + np.eye(period)
    return mix, mix @ mix


def mixing_tables(devices, local):
    period = devices * local
    mix, twice = mixing(period)
    eye, none = np.eye(period), np.zeros((period, period))
    rights, chains = [], []
    for i in range(devices):
        rows = np.arange(local) + i * local
        right, chain = [], []
        for s in range(devices):
            columns = np.arange(local) + (i ^ s) * local
            cut = lambda upper, lower: np.concatenate([upper[rows][:, columns], lower[rows][:, columns]], 0)
            right += [cut(mix, 2 * eye), cut(-twice, -2 * mix)]
            chain += [cut(mix, 2 * eye), cut(-twice, -2 * mix), cut(none, -mix), cut(none, twice)]
        rights.append(np.concatenate(right, 1))
        chains.append(np.concatenate(chain, 1))
    rights, chains = np.stack(rights).astype(np.float32), np.stack(chains).astype(np.float32)
    high = rights.astype(bf16)
    low = (rights - high.astype(np.float32)).astype(bf16)
    return np.concatenate([high, low, high], 2), chains


def split(value):
    high = value.astype(bf16)
    return high, (value - high.astype(f32)).astype(bf16)


def block_dot(value, matrix):
    rows, width = value.shape
    main = width // 256 * 256
    high, low = split(value)
    if not main or 2 * (width - main) > 256:
        return tall_dot(value, matrix)
    both = jnp.concatenate([high[:, :main], low[:, :main]], 0)
    both = lax.dot_general(both, matrix[:, :main], NT, preferred_element_type=f32)
    both = both[:rows] + both[rows:]
    if width == main:
        return both
    rest = jnp.concatenate([high[:, main:], low[:, main:]], 1)
    twice = jnp.concatenate([matrix[:, main:], matrix[:, main:]], 1)
    return both + lax.dot_general(rest, twice, NT, preferred_element_type=f32)


def tall_dot(value, matrix):
    rows = value.shape[0]
    both = lax.dot_general(jnp.concatenate(split(value), 0), matrix, NT, preferred_element_type=f32)
    return both[:rows] + both[rows:]


def full_dot(value, matrix):
    high, low = split(value)
    matrix_high, matrix_low = split(matrix)
    rows = value.shape[0]
    both = lax.dot_general(jnp.concatenate([high, low], 0), matrix_high, NN, preferred_element_type=f32)
    return both[:rows] + both[rows:] + lax.dot_general(high, matrix_low, NN, preferred_element_type=f32)


def chain_kernel(order, place, inverse_hbm, coupling_hbm, state, forcing, whole, middle, ends, packed,
                 inverse, coupling, both, inverse_sem, coupling_sem):
    tiles, width, _ = inverse.shape
    local = state.shape[0]
    part = width // CORES
    rows = part + 2 * local
    half = tiles // 2
    runs = batches(tiles)

    def fetch(k):
        tile = order[k]
        return (
            pltpu.make_async_copy(coupling_hbm.at[tile], coupling.at[k], coupling_sem.at[k]),
            pltpu.make_async_copy(inverse_hbm.at[tile], inverse.at[k], inverse_sem.at[k]),
        )

    for k in range(tiles):
        for copy in fetch(k):
            copy.start()

    def with_terms(k, turned):
        tile = order[k]
        terms = [array[i, pl.ds(tile, 1), :] for array in (forcing, state) for i in range(local)]
        terms = jnp.concatenate(terms, 0)
        packed[tile] = terms
        return jnp.concatenate([-turned[:part], terms - turned[part:]], 0)

    def keep_first(out, offset):
        out[0] = both[:part]
        ends[offset : offset + 2 * local] = both[part:rows]

    def keep_second(out, offset):
        out[1] = both[rows : rows + part]
        ends[offset + 2 * local : offset + 4 * local] = both[rows + part :]

    ids = lax.broadcasted_iota(jnp.int32, (rows, width), 0)
    columns = lax.broadcasted_iota(jnp.int32, (rows, width), 1)
    first = jnp.where((ids < part) & (columns == ids + place[0] * part), 1.0, 0.0)
    second = None
    for k in range(tiles + 1):
        for j in range(k, runs.get(k, k)):
            for copy in fetch(j):
                copy.wait()
        ahead = with_terms(k, block_dot(first, coupling[k])) if k < tiles else None
        behind = None
        if k > 0:
            behind = first if k == 1 else first - block_dot(second, coupling[k - 1])
        if k < tiles:
            first = block_dot(ahead, inverse[k])
            both[:rows] = first
        if k > 0:
            second = block_dot(behind, inverse[k - 1])
            both[rows:] = second
        if k == half - 1:
            keep_first(middle, 4 * local)
        if k == half:
            keep_second(middle, 4 * local)
    keep_first(whole, 0)
    keep_second(whole, 0)


def chain(order, place, inverse, coupling, state, forcing):
    local, tiles, width = state.shape
    part = width // CORES
    half = jax.ShapeDtypeStruct((2, part, width), f32)
    return pl.pallas_call(
        chain_kernel,
        out_shape=(
            half,
            half,
            jax.ShapeDtypeStruct((8 * local, width), f32),
            jax.ShapeDtypeStruct((tiles, 2 * local, width), f32),
        ),
        in_specs=[SMEM, SMEM, HBM, HBM, VMEM, VMEM],
        scratch_shapes=[
            pltpu.VMEM((tiles, width, width), bf16),
            pltpu.VMEM((tiles, width, width), bf16),
            pltpu.VMEM((2 * (part + 2 * local), width), f32),
            pltpu.SemaphoreType.DMA((tiles,)),
            pltpu.SemaphoreType.DMA((tiles,)),
        ],
        name="chain",
        compiler_params=params(60),
    )(order, place, inverse, coupling, state, forcing)


def right_kernel(place, table, *refs):
    blocks, out = refs[:-1], refs[-1]
    weights = table[place[2]]
    for tile in range(out.shape[0]):
        high, low = split(jnp.concatenate([block[tile] for block in blocks], 0))
        out[tile] = lax.dot_general(weights, jnp.concatenate([high, high, low], 0), NN, preferred_element_type=f32)


def right_sides(place, table, blocks):
    return pl.pallas_call(
        right_kernel,
        out_shape=jax.ShapeDtypeStruct(blocks[0].shape, f32),
        in_specs=[SMEM] + [VMEM] * (1 + len(blocks)),
        name="right_sides",
        compiler_params=params(12),
    )(place, table, *blocks)


def carried(value, pair):
    p, q = pair
    rows = value.shape[0] // 2
    moved = full_dot(value, p)
    return jnp.concatenate([moved[:rows], moved[rows:] - full_dot(value[:rows], q)], 0)


def joined(mine, theirs, core):
    lower, upper = jnp.where(core == 0, mine[...], theirs[...]), jnp.where(core == 0, theirs[...], mine[...])
    return jnp.concatenate([lower[0], upper[0]], 0), jnp.concatenate([lower[1], upper[1]], 0)


def pick(flag, when_set, otherwise):
    return jnp.where(flag == 1, when_set[...], otherwise[...])


def pair_kernel(place, table, own, own_rest, partner, partner_rest, ends, ends_partner, total, beside, middle):
    core, upper, me = place[0], place[1], place[2]
    weights = table[me]
    count = 2 * total.shape[0]

    def mixed(blocks, first):
        picked = jnp.concatenate([blocks[i + first : i + first + count] for i in range(0, blocks.shape[0], 2 * count)], 0)
        return jnp.dot(weights, picked, precision=lax.Precision.HIGHEST, preferred_element_type=f32)

    mine = mixed(ends, 0)
    middle[...] = mixed(ends, count)
    other = mixed(ends_partner, 0)
    beside[...] = other
    first = jnp.where(upper == 1, other, mine)
    last = jnp.where(upper == 1, mine, other)
    then = joined(pick(upper, own, partner), pick(upper, own_rest, partner_rest), core)
    total[...] = carried(first, then) + last


def pair_total(place, table, maps, ends):
    shape = jax.ShapeDtypeStruct((table.shape[1], ends[0].shape[1]), f32)
    return pl.pallas_call(
        pair_kernel,
        out_shape=(shape, shape, shape),
        in_specs=[SMEM] + [VMEM] * (1 + len(maps) + len(ends)),
        name="pair_total",
        compiler_params=params(12),
    )(place, table, *maps, *ends)


def carry_kernel(place, value, own, own_rest, partner, partner_rest, start, out):
    core, upper = place[0], place[1]
    moved = carried(value[...], joined(pick(upper, partner, own), pick(upper, partner_rest, own_rest), core))
    moved = carried(moved, joined(pick(upper, own, partner), pick(upper, own_rest, partner_rest), core))
    out[...] = moved + start[...]


def carry(place, value, maps, start):
    return pl.pallas_call(
        carry_kernel,
        out_shape=jax.ShapeDtypeStruct(value.shape, f32),
        in_specs=[SMEM] + [VMEM] * (2 + len(maps)),
        name="carry",
        compiler_params=params(12),
    )(place, value, *maps, start)


def sweep_kernel(order, place, inverse_hbm, coupling_hbm, right, state, partner, partner_rest, beside,
                 middle, middle_rest, middle_ends, *refs):
    arrivals, (out, inverse, coupling, at_group, inverse_sem, coupling_sem) = refs[:-6], refs[-6:]
    tiles, width, _ = inverse.shape
    local = state.shape[0]
    half = tiles // 2
    core, upper = place[0], place[1]

    def fetch(k):
        tile = order[k]
        return (
            pltpu.make_async_copy(coupling_hbm.at[tile], coupling.at[k], coupling_sem.at[k]),
            pltpu.make_async_copy(inverse_hbm.at[tile], inverse.at[k], inverse_sem.at[k]),
        )

    for k in range(half):
        for copy in fetch(k) + fetch(k + half):
            copy.start()

    inflow = jnp.zeros(at_group.shape, f32)
    for i, arrived in enumerate(arrivals):
        inflow = jnp.where(place[3] == i + 1, arrived[...], inflow)
    at_group[...] = inflow

    @pl.when(upper == 1)
    def _():
        at_group[...] = carried(inflow, joined(partner, partner_rest, core)) + beside[...]

    starts = [at_group[...]]
    starts.append(carried(starts[0], joined(middle, middle_rest, core)) + middle_ends[...])
    a = [start[:local] for start in starts]
    w = [start[local:] for start in starts]
    runs = batches(half)
    for k in range(half):
        steps = [k, k + half]
        for j in range(k, runs.get(k, k)):
            for copy in fetch(j) + fetch(j + half):
                copy.wait()
        here = [right[order[j]] for j in steps]
        turned = [tall_dot(jnp.concatenate([a[s], w[s]], 0), coupling[j]) for s, j in enumerate(steps)]
        a = [tall_dot(here[s][:local] - turned[s][:local], inverse[j]) for s, j in enumerate(steps)]
        w = [tall_dot(here[s][local:] - a[s] - turned[s][local:], inverse[j]) for s, j in enumerate(steps)]
        for s, j in enumerate(steps):
            tile = order[j]
            for i in range(local):
                out[i, pl.ds(tile, 1), :] = state[i, pl.ds(tile, 1), :] + w[s][i : i + 1]


def sweep(order, place, inverse, coupling, right, state, *rest):
    local, tiles, width = state.shape
    return pl.pallas_call(
        sweep_kernel,
        out_shape=jax.ShapeDtypeStruct(state.shape, f32),
        in_specs=[SMEM, SMEM, HBM, HBM] + [VMEM] * (2 + len(rest)),
        scratch_shapes=[
            pltpu.VMEM((tiles, width, width), bf16),
            pltpu.VMEM((tiles, width, width), bf16),
            pltpu.VMEM((2 * local, width), f32),
            pltpu.SemaphoreType.DMA((tiles,)),
            pltpu.SemaphoreType.DMA((tiles,)),
        ],
        name="sweep",
        compiler_params=params(24),
    )(order, place, inverse, coupling, right, state, *rest)


def after(value, *others):
    return lax.optimization_barrier((value, *others))[0]


def on_device(state, forcing, inverse, coupling, order):
    local, tiles, width = state.shape
    groups = lax.axis_size("axial")
    devices = lax.axis_size("inst")
    me, group = lax.axis_index("inst"), lax.axis_index("axial")
    place = jnp.stack([me % CORES, group % 2, me, group // 2]).astype(jnp.int32)
    right_table, chain_table = mixing_tables(devices, local)

    def over_inst(value, bit):
        return lax.ppermute(value, "inst", [(i, i ^ bit) for i in range(devices)])

    def over_pair(value):
        return lax.ppermute(value, "axial", [(g, g ^ 1) for g in range(groups)])

    def next_pair(value, hop):
        pairs = groups // 2
        swaps = [(p, p + 1) for p in range(hop % 2, pairs - 1, 2)]
        swaps += [(b, a) for a, b in swaps]
        return lax.ppermute(value, "axial", [(2 * a + y, 2 * b + y) for a, b in swaps for y in range(2)])

    def with_rest(value):
        return [value, over_inst(value, 1)]

    whole, middle, ends, packed = chain(order, place, inverse, coupling, state, forcing)

    own = with_rest(whole)
    partner = over_pair(whole)

    chip = jnp.concatenate([ends, over_inst(ends, 1)], 0)
    blocks = [chip] + [over_inst(chip, s) for s in range(CORES, devices, CORES)]
    blocks = jnp.concatenate(blocks, 0)
    beside = over_pair(blocks)

    packed = after(packed, blocks)
    packs = [packed] + [after(over_inst(packed, s), beside) for s in range(1, devices)]
    right = right_sides(place, jnp.asarray(right_table), packs)
    partner = with_rest(after(partner, right))
    total, beside, middle_ends = pair_total(place, jnp.asarray(chain_table), own + partner, [blocks, beside])

    middle = with_rest(after(middle, total))
    arrivals = []
    leaving = total
    for hop in range(groups // 2 - 1):
        if hop:
            leaving = carry(place, arrivals[-1], own + partner, total)
        arrivals.append(next_pair(leaving, hop))
    return sweep(order, place, inverse, coupling, right, state, *partner, beside, *middle, middle_ends, *arrivals)


def solution(mesh):
    return jax.shard_map(
        on_device,
        mesh=mesh,
        in_specs=(
            P("inst", "axial", None),
            P("inst", "axial", None),
            P("axial", None, None),
            P("axial", None, None),
            P("axial"),
        ),
        out_specs=P("inst", "axial", None),
        check_vma=False,
    )
```

```python
import functools

import jax
import jax.numpy as jnp
import numpy as np
from jax import lax
from jax.experimental import pallas as pl
from jax.experimental.pallas import tpu as pltpu
from jax.sharding import PartitionSpec as P

NT = (((1,), (1,)), ((), ()))
NN = (((1,), (0,)), ((), ()))
bf16 = jnp.bfloat16
f32 = jnp.float32
SMEM = pl.BlockSpec(memory_space=pltpu.SMEM)
VMEM = pl.BlockSpec(memory_space=pltpu.VMEM)
HBM = pl.BlockSpec(memory_space=pltpu.HBM)
CORES = 2


def params(mebibytes):
    return pltpu.CompilerParams(vmem_limit_bytes=mebibytes << 20)


def batches(count):
    edges = [0]
    while edges[-1] < count:
        edges.append(min(count, max(1, 2 * edges[-1])))
    return dict(zip(edges, edges[1:]))


def mixing(period):
    distance = np.arange(period)[:, None] - np.arange(period)[None, :]
    angles = np.pi * distance / period
    sine = np.where(distance == 0, 1.0, np.sin(angles))
    parity = 1.0 - 2.0 * (distance % 2)
    derivative = np.where(distance == 0, 0.0, 0.5 * parity * np.cos(angles) / sine)
    mix = derivative * (2.0 / period) + np.eye(period)
    return mix, mix @ mix


def mixing_tables(devices, local):
    period = devices * local
    mix, twice = mixing(period)
    eye, none = np.eye(period), np.zeros((period, period))
    rights, chains = [], []
    for i in range(devices):
        rows = np.arange(local) + i * local
        right, chain = [], []
        for s in range(devices):
            columns = np.arange(local) + (i ^ s) * local
            cut = lambda upper, lower: np.concatenate([upper[rows][:, columns], lower[rows][:, columns]], 0)
            right += [cut(mix, 2 * eye), cut(-twice, -2 * mix)]
            chain += [cut(mix, 2 * eye), cut(-twice, -2 * mix), cut(none, -mix), cut(none, twice)]
        rights.append(np.concatenate(right, 1))
        chains.append(np.concatenate(chain, 1))
    rights, chains = np.stack(rights).astype(np.float32), np.stack(chains).astype(np.float32)
    high = rights.astype(bf16)
    low = (rights - high.astype(np.float32)).astype(bf16)
    return np.concatenate([high, low, high], 2), chains


def split(value):
    high = value.astype(bf16)
    return high, (value - high.astype(f32)).astype(bf16)


def block_dot(value, matrix):
    rows, width = value.shape
    main = width // 256 * 256
    high, low = split(value)
    if not main or 2 * (width - main) > 256:
        return tall_dot(value, matrix)
    both = jnp.concatenate([high[:, :main], low[:, :main]], 0)
    both = lax.dot_general(both, matrix[:, :main], NT, preferred_element_type=f32)
    both = both[:rows] + both[rows:]
    if width == main:
        return both
    rest = jnp.concatenate([high[:, main:], low[:, main:]], 1)
    twice = jnp.concatenate([matrix[:, main:], matrix[:, main:]], 1)
    return both + lax.dot_general(rest, twice, NT, preferred_element_type=f32)


def tall_dot(value, matrix):
    rows = value.shape[0]
    both = lax.dot_general(jnp.concatenate(split(value), 0), matrix, NT, preferred_element_type=f32)
    return both[:rows] + both[rows:]


def chain_kernel(order, place, inverse_hbm, coupling_hbm, state, forcing, whole, middle, ends, packed,
                 inverse, coupling, both, inverse_sem, coupling_sem):
    tiles, width, _ = inverse.shape
    local = state.shape[0]
    part = width // CORES
    rows = part + 2 * local
    half = tiles // 2
    runs = batches(tiles)

    def fetch(k):
        tile = order[k]
        return (
            pltpu.make_async_copy(coupling_hbm.at[tile], coupling.at[k], coupling_sem.at[k]),
            pltpu.make_async_copy(inverse_hbm.at[tile], inverse.at[k], inverse_sem.at[k]),
        )

    for k in range(tiles):
        for copy in fetch(k):
            copy.start()

    def with_terms(k, turned):
        tile = order[k]
        terms = [array[i, pl.ds(tile, 1), :] for array in (forcing, state) for i in range(local)]
        terms = jnp.concatenate(terms, 0)
        packed[tile] = terms
        return jnp.concatenate([-turned[:part], terms - turned[part:]], 0)

    def keep_first(out, offset):
        out[0] = both[:part]
        ends[offset : offset + 2 * local] = both[part:rows]

    def keep_second(out, offset):
        out[1] = both[rows : rows + part]
        ends[offset + 2 * local : offset + 4 * local] = both[rows + part :]

    ids = lax.broadcasted_iota(jnp.int32, (rows, width), 0)
    columns = lax.broadcasted_iota(jnp.int32, (rows, width), 1)
    first = jnp.where((ids < part) & (columns == ids + place[0] * part), 1.0, 0.0)
    second = None
    for k in range(tiles + 1):
        for j in range(k, runs.get(k, k)):
            for copy in fetch(j):
                copy.wait()
        ahead = with_terms(k, block_dot(first, coupling[k])) if k < tiles else None
        behind = None
        if k > 0:
            behind = first if k == 1 else first - block_dot(second, coupling[k - 1])
        if k < tiles:
            first = block_dot(ahead, inverse[k])
            both[:rows] = first
        if k > 0:
            second = block_dot(behind, inverse[k - 1])
            both[rows:] = second
        if k == half - 1:
            keep_first(middle, 4 * local)
        if k == half:
            keep_second(middle, 4 * local)
    keep_first(whole, 0)
    keep_second(whole, 0)


def chain(order, place, inverse, coupling, state, forcing):
    local, tiles, width = state.shape
    part = width // CORES
    half = jax.ShapeDtypeStruct((2, part, width), f32)
    return pl.pallas_call(
        chain_kernel,
        out_shape=(
            half,
            half,
            jax.ShapeDtypeStruct((8 * local, width), f32),
            jax.ShapeDtypeStruct((tiles, 2 * local, width), f32),
        ),
        in_specs=[SMEM, SMEM, HBM, HBM, VMEM, VMEM],
        scratch_shapes=[
            pltpu.VMEM((tiles, width, width), bf16),
            pltpu.VMEM((tiles, width, width), bf16),
            pltpu.VMEM((2 * (part + 2 * local), width), f32),
            pltpu.SemaphoreType.DMA((tiles,)),
            pltpu.SemaphoreType.DMA((tiles,)),
        ],
        name="chain",
        compiler_params=params(60),
    )(order, place, inverse, coupling, state, forcing)


def right_kernel(place, table, *refs):
    blocks, out = refs[:-1], refs[-1]
    weights = table[place[2]]
    for tile in range(out.shape[0]):
        high, low = split(jnp.concatenate([block[tile] for block in blocks], 0))
        out[tile] = lax.dot_general(weights, jnp.concatenate([high, high, low], 0), NN, preferred_element_type=f32)


def right_sides(place, table, blocks):
    return pl.pallas_call(
        right_kernel,
        out_shape=jax.ShapeDtypeStruct(blocks[0].shape, f32),
        in_specs=[SMEM] + [VMEM] * (1 + len(blocks)),
        name="right_sides",
        compiler_params=params(12),
    )(place, table, *blocks)


def split_map(mine, rest, core, out):
    rows = mine.shape[1]
    for i in range(2):
        for source, start in ((mine, core * rows), (rest, (1 - core) * rows)):
            high, low = split(source[i])
            out[2 * i, pl.ds(pl.multiple_of(start, rows), rows), :] = high
            out[2 * i + 1, pl.ds(pl.multiple_of(start, rows), rows), :] = low


def times(value, high, low):
    upper, lower = split(value)
    rows = value.shape[0]
    both = lax.dot_general(jnp.concatenate([upper, lower], 0), high, NN, preferred_element_type=f32)
    return both[:rows] + both[rows:] + lax.dot_general(upper, low, NN, preferred_element_type=f32)


def carried(value, parts):
    rows = value.shape[0] // 2
    moved = times(value, parts[0], parts[1])
    return jnp.concatenate([moved[:rows], moved[rows:] - times(value[:rows], parts[2], parts[3])], 0)


def prepare_kernel(place, mine, rest, out):
    split_map(mine, rest, place[0], out)


def prepare(place, mine, rest):
    width = mine.shape[2]
    return pl.pallas_call(
        prepare_kernel,
        out_shape=jax.ShapeDtypeStruct((4, width, width), bf16),
        in_specs=[SMEM, VMEM, VMEM],
        name="prepare",
        compiler_params=params(12),
    )(place, mine, rest)


def mix_kernel(place, table, *refs):
    blocks, outs = refs[:-2], refs[-2:]
    weights = table[place[2]]
    count = blocks[0].shape[0] // 2
    for i, out in enumerate(outs):
        rows = jnp.concatenate([block[i * count : i * count + count] for block in blocks], 0)
        out[...] = jnp.dot(weights, rows, precision=lax.Precision.HIGHEST, preferred_element_type=f32)


def mix_ends(place, table, blocks):
    shape = jax.ShapeDtypeStruct((table.shape[1], blocks[0].shape[1]), f32)
    return pl.pallas_call(
        mix_kernel,
        out_shape=(shape, shape),
        in_specs=[SMEM] + [VMEM] * (1 + len(blocks)),
        name="mix_ends",
        compiler_params=params(12),
    )(place, table, *blocks)


def pair_kernel(place, own, partner_mine, partner_rest, ends, beside, total, partner):
    split_map(partner_mine, partner_rest, place[0], partner)

    @pl.when(place[1] == 1)
    def _():
        total[...] = carried(beside[...], own) + ends[...]

    @pl.when(place[1] == 0)
    def _():
        total[...] = carried(ends[...], partner) + beside[...]


def pair_total(place, own, partner, ends, beside):
    return pl.pallas_call(
        pair_kernel,
        out_shape=(jax.ShapeDtypeStruct(ends.shape, f32), jax.ShapeDtypeStruct(own.shape, bf16)),
        in_specs=[SMEM] + [VMEM] * 5,
        name="pair_total",
        compiler_params=params(12),
    )(place, own, *partner, ends, beside)


def carry_kernel(place, value, own, partner, start, out):
    @pl.when(place[1] == 1)
    def _():
        out[...] = carried(carried(value[...], partner), own) + start[...]

    @pl.when(place[1] == 0)
    def _():
        out[...] = carried(carried(value[...], own), partner) + start[...]


def carry(place, value, own, partner, start):
    return pl.pallas_call(
        carry_kernel,
        out_shape=jax.ShapeDtypeStruct(value.shape, f32),
        in_specs=[SMEM] + [VMEM] * 4,
        name="carry",
        compiler_params=params(12),
    )(place, value, own, partner, start)


def sweep_kernel(order, place, inverse, coupling, right, state, partner, beside, middle, middle_ends, *refs):
    arrivals, (out, at_group) = refs[:-2], refs[-2:]
    tiles, width, _ = inverse.shape
    local = state.shape[0]
    half = tiles // 2
    core, upper = place[0], place[1]

    inflow = jnp.zeros(at_group.shape, f32)
    for i, arrived in enumerate(arrivals):
        inflow = jnp.where(place[3] == i + 1, arrived[...], inflow)
    at_group[...] = inflow

    @pl.when(upper == 1)
    def _():
        at_group[...] = carried(inflow, partner) + beside[...]

    starts = [at_group[...]]
    starts.append(carried(starts[0], middle) + middle_ends[...])
    a = [start[:local] for start in starts]
    w = [start[local:] for start in starts]
    for k in range(half):
        steps = [order[k], order[k + half]]
        here = [right[tile] for tile in steps]
        turned = [tall_dot(jnp.concatenate([a[s], w[s]], 0), coupling[tile]) for s, tile in enumerate(steps)]
        a = [tall_dot(here[s][:local] - turned[s][:local], inverse[tile]) for s, tile in enumerate(steps)]
        w = [tall_dot(here[s][local:] - a[s] - turned[s][local:], inverse[tile]) for s, tile in enumerate(steps)]
        for s, tile in enumerate(steps):
            for i in range(local):
                out[i, pl.ds(tile, 1), :] = state[i, pl.ds(tile, 1), :] + w[s][i : i + 1]


def sweep(order, place, inverse, coupling, right, state, *rest):
    local, _, width = state.shape
    return pl.pallas_call(
        sweep_kernel,
        out_shape=jax.ShapeDtypeStruct(state.shape, f32),
        in_specs=[SMEM, SMEM] + [VMEM] * (4 + len(rest)),
        scratch_shapes=[pltpu.VMEM((2 * local, width), f32)],
        name="sweep",
        compiler_params=params(24),
    )(order, place, inverse, coupling, right, state, *rest)


def after(value, *others):
    return lax.optimization_barrier((value, *others))[0]


def on_device(state, forcing, inverse, coupling, order):
    local, tiles, width = state.shape
    groups = lax.axis_size("axial")
    devices = lax.axis_size("inst")
    me, group = lax.axis_index("inst"), lax.axis_index("axial")
    place = jnp.stack([me % CORES, group % 2, me, group // 2]).astype(jnp.int32)
    right_table, chain_table = mixing_tables(devices, local)

    def over_inst(value, bit):
        return lax.ppermute(value, "inst", [(i, i ^ bit) for i in range(devices)])

    def over_pair(value):
        return lax.ppermute(value, "axial", [(g, g ^ 1) for g in range(groups)])

    def next_pair(value, hop):
        pairs = groups // 2
        swaps = [(p, p + 1) for p in range(hop % 2, pairs - 1, 2)]
        swaps += [(b, a) for a, b in swaps]
        return lax.ppermute(value, "axial", [(2 * a + y, 2 * b + y) for a, b in swaps for y in range(2)])

    def with_rest(value):
        return [value, over_inst(value, 1)]

    whole, middle, ends, packed = chain(order, place, inverse, coupling, state, forcing)

    partner = over_pair(whole)
    own = prepare(place, *with_rest(whole))
    blocks = [ends] + [over_inst(ends, s) for s in range(1, devices)]
    packed = after(packed, *blocks)
    packs = [packed] + [over_inst(packed, s) for s in range(CORES, devices, CORES)]
    ends, middle_ends = mix_ends(place, jnp.asarray(chain_table), blocks)
    beside = over_pair(ends)
    partner = with_rest(after(partner, beside, own, *packs))
    total, partner = pair_total(place, own, partner, ends, beside)

    arrivals = []
    leaving = total
    for hop in range(groups // 2 - 1):
        if hop:
            leaving = carry(place, arrivals[-1], own, partner, total)
        arrivals.append(next_pair(leaving, hop))
    packs = [after(pack, total) for pack in packs]
    packs = [block for pack in packs for block in (pack, over_inst(pack, 1))]
    right = right_sides(place, jnp.asarray(right_table), packs)
    middle = prepare(place, *with_rest(after(middle, total)))
    return sweep(order, place, inverse, coupling, right, state, partner, beside, middle, middle_ends, *arrivals)


def solution(mesh):
    return jax.shard_map(
        on_device,
        mesh=mesh,
        in_specs=(
            P("inst", "axial", None),
            P("inst", "axial", None),
            P("axial", None, None),
            P("axial", None, None),
            P("axial"),
        ),
        out_specs=P("inst", "axial", None),
        check_vma=False,
    )
```

```python
import functools

import jax
import jax.numpy as jnp
import numpy as np
from jax import lax
from jax.experimental import pallas as pl
from jax.experimental.pallas import tpu as pltpu
from jax.sharding import PartitionSpec as P

NT = (((1,), (1,)), ((), ()))
NN = (((1,), (0,)), ((), ()))
bf16 = jnp.bfloat16
f32 = jnp.float32
SMEM = pl.BlockSpec(memory_space=pltpu.SMEM)
VMEM = pl.BlockSpec(memory_space=pltpu.VMEM)
HBM = pl.BlockSpec(memory_space=pltpu.HBM)
CORES = 2


def params(mebibytes):
    return pltpu.CompilerParams(vmem_limit_bytes=mebibytes << 20)


def batches(count):
    edges = [0]
    while edges[-1] < count:
        edges.append(min(count, max(1, 2 * edges[-1])))
    return dict(zip(edges, edges[1:]))


def mixing(period):
    distance = np.arange(period)[:, None] - np.arange(period)[None, :]
    angles = np.pi * distance / period
    sine = np.where(distance == 0, 1.0, np.sin(angles))
    parity = 1.0 - 2.0 * (distance % 2)
    derivative = np.where(distance == 0, 0.0, 0.5 * parity * np.cos(angles) / sine)
    mix = derivative * (2.0 / period) + np.eye(period)
    return mix, mix @ mix


def mixing_tables(devices, local):
    period = devices * local
    mix, twice = mixing(period)
    eye, none = np.eye(period), np.zeros((period, period))
    rights, chains = [], []
    for i in range(devices):
        rows = np.arange(local) + i * local
        right, chain = [], []
        for s in range(devices):
            columns = np.arange(local) + (i ^ s) * local
            cut = lambda upper, lower: np.concatenate([upper[rows][:, columns], lower[rows][:, columns]], 0)
            right += [cut(mix, 2 * eye), cut(-twice, -2 * mix)]
            chain += [cut(mix, 2 * eye), cut(-twice, -2 * mix), cut(none, -mix), cut(none, twice)]
        rights.append(np.concatenate(right, 1))
        chains.append(np.concatenate(chain, 1))
    rights, chains = np.stack(rights).astype(np.float32), np.stack(chains).astype(np.float32)
    high = rights.astype(bf16)
    low = (rights - high.astype(np.float32)).astype(bf16)
    return np.concatenate([high, low, high], 2), chains


def split(value):
    high = value.astype(bf16)
    return high, (value - high.astype(f32)).astype(bf16)


def block_dot(value, matrix):
    rows, width = value.shape
    main = width // 256 * 256
    high, low = split(value)
    if not main or 2 * (width - main) > 256:
        return tall_dot(value, matrix)
    both = jnp.concatenate([high[:, :main], low[:, :main]], 0)
    both = lax.dot_general(both, matrix[:, :main], NT, preferred_element_type=f32)
    both = both[:rows] + both[rows:]
    if width == main:
        return both
    rest = jnp.concatenate([high[:, main:], low[:, main:]], 1)
    twice = jnp.concatenate([matrix[:, main:], matrix[:, main:]], 1)
    return both + lax.dot_general(rest, twice, NT, preferred_element_type=f32)


def tall_dot(value, matrix):
    rows = value.shape[0]
    both = lax.dot_general(jnp.concatenate(split(value), 0), matrix, NT, preferred_element_type=f32)
    return both[:rows] + both[rows:]


def chain_kernel(order, place, inverse_hbm, coupling_hbm, state, forcing, whole, middle, ends, packed,
                 inverse, coupling, both, inverse_sem, coupling_sem):
    tiles, width, _ = inverse.shape
    local = state.shape[0]
    part = width // CORES
    rows = part + 2 * local
    half = tiles // 2
    runs = batches(tiles)

    def fetch(k):
        tile = order[k]
        return (
            pltpu.make_async_copy(coupling_hbm.at[tile], coupling.at[k], coupling_sem.at[k]),
            pltpu.make_async_copy(inverse_hbm.at[tile], inverse.at[k], inverse_sem.at[k]),
        )

    for k in range(tiles):
        for copy in fetch(k):
            copy.start()

    def with_terms(k, turned):
        tile = order[k]
        terms = [array[i, pl.ds(tile, 1), :] for array in (forcing, state) for i in range(local)]
        terms = jnp.concatenate(terms, 0)
        packed[tile] = terms
        return jnp.concatenate([-turned[:part], terms - turned[part:]], 0)

    def keep_first(out, offset):
        out[0] = both[:part]
        ends[offset : offset + 2 * local] = both[part:rows]

    def keep_second(out, offset):
        out[1] = both[rows : rows + part]
        ends[offset + 2 * local : offset + 4 * local] = both[rows + part :]

    ids = lax.broadcasted_iota(jnp.int32, (rows, width), 0)
    columns = lax.broadcasted_iota(jnp.int32, (rows, width), 1)
    first = jnp.where((ids < part) & (columns == ids + place[0] * part), 1.0, 0.0)
    second = None
    for k in range(tiles + 1):
        for j in range(k, runs.get(k, k)):
            for copy in fetch(j):
                copy.wait()
        ahead = with_terms(k, block_dot(first, coupling[k])) if k < tiles else None
        behind = None
        if k > 0:
            behind = first if k == 1 else first - block_dot(second, coupling[k - 1])
        if k < tiles:
            first = block_dot(ahead, inverse[k])
            both[:rows] = first
        if k > 0:
            second = block_dot(behind, inverse[k - 1])
            both[rows:] = second
        if k == half - 1:
            keep_first(middle, 4 * local)
        if k == half:
            keep_second(middle, 4 * local)
    keep_first(whole, 0)
    keep_second(whole, 0)


def chain(order, place, inverse, coupling, state, forcing):
    local, tiles, width = state.shape
    part = width // CORES
    half = jax.ShapeDtypeStruct((2, part, width), f32)
    return pl.pallas_call(
        chain_kernel,
        out_shape=(
            half,
            half,
            jax.ShapeDtypeStruct((8 * local, width), f32),
            jax.ShapeDtypeStruct((tiles, 2 * local, width), f32),
        ),
        in_specs=[SMEM, SMEM, HBM, HBM, VMEM, VMEM],
        scratch_shapes=[
            pltpu.VMEM((tiles, width, width), bf16),
            pltpu.VMEM((tiles, width, width), bf16),
            pltpu.VMEM((2 * (part + 2 * local), width), f32),
            pltpu.SemaphoreType.DMA((tiles,)),
            pltpu.SemaphoreType.DMA((tiles,)),
        ],
        name="chain",
        compiler_params=params(60),
    )(order, place, inverse, coupling, state, forcing)


def right_kernel(place, table, *refs):
    blocks, out = refs[:-1], refs[-1]
    weights = table[place[2]]
    for tile in range(out.shape[0]):
        high, low = split(jnp.concatenate([block[tile] for block in blocks], 0))
        out[tile] = lax.dot_general(weights, jnp.concatenate([high, high, low], 0), NN, preferred_element_type=f32)


def right_sides(place, table, blocks):
    return pl.pallas_call(
        right_kernel,
        out_shape=jax.ShapeDtypeStruct(blocks[0].shape, f32),
        in_specs=[SMEM] + [VMEM] * (1 + len(blocks)),
        name="right_sides",
        compiler_params=params(12),
    )(place, table, *blocks)


def split_map(mine, rest, core, out):
    rows = mine.shape[1]
    for i in range(2):
        for source, start in ((mine, core * rows), (rest, (1 - core) * rows)):
            high, low = split(source[i])
            out[2 * i, pl.ds(pl.multiple_of(start, rows), rows), :] = high
            out[2 * i + 1, pl.ds(pl.multiple_of(start, rows), rows), :] = low


def times(value, high, low):
    upper, lower = split(value)
    rows = value.shape[0]
    both = lax.dot_general(jnp.concatenate([upper, lower], 0), high, NN, preferred_element_type=f32)
    return both[:rows] + both[rows:] + lax.dot_general(upper, low, NN, preferred_element_type=f32)


def carried(value, parts):
    rows = value.shape[0] // 2
    moved = times(value, parts[0], parts[1])
    return jnp.concatenate([moved[:rows], moved[rows:] - times(value[:rows], parts[2], parts[3])], 0)


def prepare_kernel(place, mine, rest, out):
    split_map(mine, rest, place[0], out)


def prepare(place, mine, rest):
    width = mine.shape[2]
    return pl.pallas_call(
        prepare_kernel,
        out_shape=jax.ShapeDtypeStruct((4, width, width), bf16),
        in_specs=[SMEM, VMEM, VMEM],
        name="prepare",
        cost_estimate=pl.CostEstimate(flops=5 * 10**9, bytes_accessed=0, transcendentals=0),
        compiler_params=params(12),
    )(place, mine, rest)


def mixed(weights, blocks, start, count):
    rows = jnp.concatenate([block[start : start + count] for block in blocks], 0)
    return jnp.dot(weights, rows, precision=lax.Precision.HIGHEST, preferred_element_type=f32)


def mix_own_kernel(place, table, ends, out):
    count = ends.shape[0] // 2
    weights = table[place[2]][:, :count]
    for i in range(2):
        out[i] = mixed(weights, [ends], i * count, count)


def mix_kernel(place, table, own, *refs):
    blocks, outs = refs[:-2], refs[-2:]
    count = blocks[0].shape[0] // 2
    weights = table[place[2]][:, count:]
    for i, out in enumerate(outs):
        out[...] = own[i] + mixed(weights, blocks, i * count, count)


def mix_ends(place, table, ends, blocks):
    rows, width = table.shape[1], ends.shape[1]
    shape = jax.ShapeDtypeStruct((rows, width), f32)
    own = pl.pallas_call(
        mix_own_kernel,
        out_shape=jax.ShapeDtypeStruct((2, rows, width), f32),
        in_specs=[SMEM, VMEM, VMEM],
        name="mix_own",
        compiler_params=params(12),
    )(place, table, ends)
    return pl.pallas_call(
        mix_kernel,
        out_shape=(shape, shape),
        in_specs=[SMEM] + [VMEM] * (2 + len(blocks)),
        name="mix_ends",
        compiler_params=params(12),
    )(place, table, own, *blocks)


def pair_kernel(place, own, ends, beside, total):
    total[...] = ends[...]

    @pl.when(place[1] == 1)
    def _():
        total[...] = carried(beside[...], own) + ends[...]


def pair_total(place, own, ends, beside):
    return pl.pallas_call(
        pair_kernel,
        out_shape=jax.ShapeDtypeStruct(ends.shape, f32),
        in_specs=[SMEM] + [VMEM] * 3,
        name="pair_total",
        compiler_params=params(12),
    )(place, own, ends, beside)


def carry_kernel(pair, place, value, own, partner, start, out):
    out[...] = start[...]

    @pl.when((place[1] == 1) & (place[3] == pair))
    def _():
        out[...] = carried(carried(value[...], partner), own) + start[...]


def carry(pair, place, value, own, partner, start):
    return pl.pallas_call(
        functools.partial(carry_kernel, pair),
        out_shape=jax.ShapeDtypeStruct(value.shape, f32),
        in_specs=[SMEM] + [VMEM] * 4,
        name="carry",
        compiler_params=params(12),
    )(place, value, own, partner, start)


def sweep_kernel(order, place, inverse, coupling, right, state, partner, beside, middle, middle_ends, *refs):
    arrivals, (out, at_group) = refs[:-2], refs[-2:]
    tiles, width, _ = inverse.shape
    local = state.shape[0]
    half = tiles // 2
    core, upper = place[0], place[1]

    inflow = jnp.zeros(at_group.shape, f32)
    for i in range(len(arrivals) // 2):
        arrived = jnp.where(upper == 1, arrivals[2 * i + 1][...], arrivals[2 * i][...])
        inflow = jnp.where(place[3] == i + 1, arrived, inflow)
    at_group[...] = inflow

    @pl.when(upper == 1)
    def _():
        at_group[...] = carried(inflow, partner) + beside[...]

    starts = [at_group[...]]
    starts.append(carried(starts[0], middle) + middle_ends[...])
    a = [start[:local] for start in starts]
    w = [start[local:] for start in starts]
    for k in range(half):
        steps = [order[k], order[k + half]]
        here = [right[tile] for tile in steps]
        turned = [tall_dot(jnp.concatenate([a[s], w[s]], 0), coupling[tile]) for s, tile in enumerate(steps)]
        a = [tall_dot(here[s][:local] - turned[s][:local], inverse[tile]) for s, tile in enumerate(steps)]
        w = [tall_dot(here[s][local:] - a[s] - turned[s][local:], inverse[tile]) for s, tile in enumerate(steps)]
        for s, tile in enumerate(steps):
            for i in range(local):
                out[i, pl.ds(tile, 1), :] = state[i, pl.ds(tile, 1), :] + w[s][i : i + 1]


def sweep(order, place, inverse, coupling, right, state, *rest):
    local, _, width = state.shape
    return pl.pallas_call(
        sweep_kernel,
        out_shape=jax.ShapeDtypeStruct(state.shape, f32),
        in_specs=[SMEM, SMEM] + [VMEM] * (4 + len(rest)),
        scratch_shapes=[pltpu.VMEM((2 * local, width), f32)],
        name="sweep",
        compiler_params=params(24),
    )(order, place, inverse, coupling, right, state, *rest)


def after(value, *others):
    return lax.optimization_barrier((value, *others))[0]


def on_device(state, forcing, inverse, coupling, order):
    local, tiles, width = state.shape
    groups = lax.axis_size("axial")
    devices = lax.axis_size("inst")
    me, group = lax.axis_index("inst"), lax.axis_index("axial")
    place = jnp.stack([me % CORES, group % 2, me, group // 2]).astype(jnp.int32)
    right_table, chain_table = mixing_tables(devices, local)

    def over_inst(value, bit):
        return lax.ppermute(value, "inst", [(i, i ^ bit) for i in range(devices)])

    def over_pair(value):
        return lax.ppermute(value, "axial", [(g, g ^ 1) for g in range(groups)])

    def next_pair(value, pair, target):
        source, target = 2 * pair + 1, 2 * pair + 2 + target
        return lax.ppermute(value, "axial", [(source, target), (target, source)])

    def with_rest(value):
        return [value, over_inst(value, 1)]

    whole, middle, ends, packed = chain(order, place, inverse, coupling, state, forcing)

    blocks = [over_inst(ends, s) for s in range(1, devices)]
    partner = over_pair(whole)
    own = prepare(place, *with_rest(whole))
    ends, middle_ends = mix_ends(place, jnp.asarray(chain_table), ends, blocks)
    beside = after(over_pair(ends), own)
    packed, middle = after(packed, ends), after(middle, ends)
    packs = [packed] + [over_inst(packed, s) for s in range(CORES, devices, CORES)]
    middle = with_rest(middle)
    total = pair_total(place, own, ends, beside)
    middle = prepare(place, after(middle[0], total), middle[1])
    partner = prepare(place, *with_rest(after(partner, total)))

    arrivals = []
    leaving = total
    for pair in range(groups // 2 - 1):
        if pair:
            leaving = carry(pair, place, arrivals[-1], own, partner, total)
        arrivals += [next_pair(leaving, pair, 0), next_pair(leaving, pair, 1)]
        if not pair:
            arrivals[-1] = after(arrivals[-1], middle, *packs[1:])
        if pair == min(1, groups // 2 - 2):
            packs = [after(pack, leaving) for pack in packs]
            packs = [block for pack in packs for block in (pack, over_inst(pack, 1))]
            right = right_sides(place, jnp.asarray(right_table), packs)
    if groups > 2:
        arrivals[-1] = after(arrivals[-1], right)
    return sweep(order, place, inverse, coupling, right, state, partner, beside, middle, middle_ends, *arrivals)


def solution(mesh):
    return jax.shard_map(
        on_device,
        mesh=mesh,
        in_specs=(
            P("inst", "axial", None),
            P("inst", "axial", None),
            P("axial", None, None),
            P("axial", None, None),
            P("axial"),
        ),
        out_specs=P("inst", "axial", None),
        check_vma=False,
    )
```

```python
import functools

import jax
import jax.numpy as jnp
import numpy as np
from jax import lax
from jax.experimental import pallas as pl
from jax.experimental.pallas import tpu as pltpu
from jax.sharding import PartitionSpec as P

NT = (((1,), (1,)), ((), ()))
NN = (((1,), (0,)), ((), ()))
bf16 = jnp.bfloat16
f32 = jnp.float32
SMEM = pl.BlockSpec(memory_space=pltpu.SMEM)
VMEM = pl.BlockSpec(memory_space=pltpu.VMEM)
HBM = pl.BlockSpec(memory_space=pltpu.HBM)
CORES = 2


def params(mebibytes):
    return pltpu.CompilerParams(vmem_limit_bytes=mebibytes << 20)


def batches(count):
    edges = [0]
    while edges[-1] < count:
        edges.append(min(count, max(1, 2 * edges[-1])))
    return dict(zip(edges, edges[1:]))


def mixing(period):
    distance = np.arange(period)[:, None] - np.arange(period)[None, :]
    angles = np.pi * distance / period
    sine = np.where(distance == 0, 1.0, np.sin(angles))
    parity = 1.0 - 2.0 * (distance % 2)
    derivative = np.where(distance == 0, 0.0, 0.5 * parity * np.cos(angles) / sine)
    mix = derivative * (2.0 / period) + np.eye(period)
    return mix, mix @ mix


def mixing_tables(devices, local):
    period = devices * local
    mix, twice = mixing(period)
    eye, none = np.eye(period), np.zeros((period, period))
    rights, chains = [], []
    for i in range(devices):
        rows = np.arange(local) + i * local
        right, chain = [], []
        for s in range(devices):
            columns = np.arange(local) + (i ^ s) * local
            cut = lambda upper, lower: np.concatenate([upper[rows][:, columns], lower[rows][:, columns]], 0)
            right += [cut(mix, 2 * eye), cut(-twice, -2 * mix)]
            chain += [cut(mix, 2 * eye), cut(-twice, -2 * mix), cut(none, -mix), cut(none, twice)]
        rights.append(np.concatenate(right, 1))
        chains.append(np.concatenate(chain, 1))
    rights, chains = np.stack(rights).astype(np.float32), np.stack(chains).astype(np.float32)
    high = rights.astype(bf16)
    low = (rights - high.astype(np.float32)).astype(bf16)
    return np.concatenate([high, low, high], 2), chains


def split(value):
    high = value.astype(bf16)
    return high, (value - high.astype(f32)).astype(bf16)


def block_dot(value, matrix):
    rows, width = value.shape
    main = width // 256 * 256
    high, low = split(value)
    if not main or 2 * (width - main) > 256:
        return tall_dot(value, matrix)
    both = jnp.concatenate([high[:, :main], low[:, :main]], 0)
    both = lax.dot_general(both, matrix[:, :main], NT, preferred_element_type=f32)
    both = both[:rows] + both[rows:]
    if width == main:
        return both
    rest = jnp.concatenate([high[:, main:], low[:, main:]], 1)
    twice = jnp.concatenate([matrix[:, main:], matrix[:, main:]], 1)
    return both + lax.dot_general(rest, twice, NT, preferred_element_type=f32)


def tall_dot(value, matrix):
    rows = value.shape[0]
    both = lax.dot_general(jnp.concatenate(split(value), 0), matrix, NT, preferred_element_type=f32)
    return both[:rows] + both[rows:]


def chain_kernel(order, place, inverse_hbm, coupling_hbm, state, forcing, whole, whole_p, whole_q, middle, ends, packed,
                 inverse, coupling, both, inverse_sem, coupling_sem):
    tiles, width, _ = inverse.shape
    local = state.shape[0]
    part = width // CORES
    rows = part + 2 * local
    half = tiles // 2
    runs = batches(tiles)

    def fetch(k):
        tile = order[k]
        return (
            pltpu.make_async_copy(coupling_hbm.at[tile], coupling.at[k], coupling_sem.at[k]),
            pltpu.make_async_copy(inverse_hbm.at[tile], inverse.at[k], inverse_sem.at[k]),
        )

    for k in range(tiles):
        for copy in fetch(k):
            copy.start()

    def with_terms(k, turned):
        tile = order[k]
        terms = [array[i, pl.ds(tile, 1), :] for array in (forcing, state) for i in range(local)]
        terms = jnp.concatenate(terms, 0)
        packed[tile] = terms
        return jnp.concatenate([-turned[:part], terms - turned[part:]], 0)

    def keep_first(out, offset):
        out[0] = both[:part]
        ends[offset : offset + 2 * local] = both[part:rows]

    def keep_second(out, offset):
        out[1] = both[rows : rows + part]
        ends[offset + 2 * local : offset + 4 * local] = both[rows + part :]

    ids = lax.broadcasted_iota(jnp.int32, (rows, width), 0)
    columns = lax.broadcasted_iota(jnp.int32, (rows, width), 1)
    first = jnp.where((ids < part) & (columns == ids + place[0] * part), 1.0, 0.0)
    second = None
    for k in range(tiles + 1):
        for j in range(k, runs.get(k, k)):
            for copy in fetch(j):
                copy.wait()
        ahead = with_terms(k, block_dot(first, coupling[k])) if k < tiles else None
        behind = None
        if k > 0:
            behind = first if k == 1 else first - block_dot(second, coupling[k - 1])
        if k < tiles:
            first = block_dot(ahead, inverse[k])
            both[:rows] = first
        if k > 0:
            second = block_dot(behind, inverse[k - 1])
            both[rows:] = second
        if k == half - 1:
            keep_first(middle, 4 * local)
        if k == half:
            keep_second(middle, 4 * local)
    keep_first(whole, 0)
    keep_second(whole, 0)
    whole_p[...] = both[:part]
    whole_q[...] = both[rows : rows + part]


def chain(order, place, inverse, coupling, state, forcing):
    local, tiles, width = state.shape
    part = width // CORES
    half = jax.ShapeDtypeStruct((2, part, width), f32)
    return pl.pallas_call(
        chain_kernel,
        out_shape=(
            half,
            jax.ShapeDtypeStruct((part, width), f32),
            jax.ShapeDtypeStruct((part, width), f32),
            half,
            jax.ShapeDtypeStruct((8 * local, width), f32),
            jax.ShapeDtypeStruct((tiles, 2 * local, width), f32),
        ),
        in_specs=[SMEM, SMEM, HBM, HBM, VMEM, VMEM],
        scratch_shapes=[
            pltpu.VMEM((tiles, width, width), bf16),
            pltpu.VMEM((tiles, width, width), bf16),
            pltpu.VMEM((2 * (part + 2 * local), width), f32),
            pltpu.SemaphoreType.DMA((tiles,)),
            pltpu.SemaphoreType.DMA((tiles,)),
        ],
        name="chain",
        compiler_params=params(60),
    )(order, place, inverse, coupling, state, forcing)


def right_kernel(place, table, *refs):
    blocks, out = refs[:-1], refs[-1]
    weights = table[place[2]]
    for tile in range(out.shape[0]):
        high, low = split(jnp.concatenate([block[tile] for block in blocks], 0))
        out[tile] = lax.dot_general(weights, jnp.concatenate([high, high, low], 0), NN, preferred_element_type=f32)


def right_sides(place, table, blocks):
    return pl.pallas_call(
        right_kernel,
        out_shape=jax.ShapeDtypeStruct(blocks[0].shape, f32),
        in_specs=[SMEM] + [VMEM] * (1 + len(blocks)),
        name="right_sides",
        compiler_params=params(12),
    )(place, table, *blocks)


def split_map(mine, rest, core, out):
    for i in range(2):
        for source, half in ((mine[i], core), (rest[i], 1 - core)):
            rows = source.shape[0]
            high, low = split(source)
            out[2 * i, pl.ds(pl.multiple_of(half * rows, rows), rows), :] = high
            out[2 * i + 1, pl.ds(pl.multiple_of(half * rows, rows), rows), :] = low


def times(value, high, low):
    upper, lower = split(value)
    rows = value.shape[0]
    both = lax.dot_general(jnp.concatenate([upper, lower], 0), high, NN, preferred_element_type=f32)
    return both[:rows] + both[rows:] + lax.dot_general(upper, low, NN, preferred_element_type=f32)


def carried(value, parts):
    rows = value.shape[0] // 2
    moved = times(value, parts[0], parts[1])
    return jnp.concatenate([moved[:rows], moved[rows:] - times(value[:rows], parts[2], parts[3])], 0)


def prepare_kernel(place, mine, rest, out):
    split_map(mine, rest, place[0], out)


def prepare_parts_kernel(place, mine_p, mine_q, rest_p, rest_q, out):
    split_map((mine_p[...], mine_q[...]), (rest_p[...], rest_q[...]), place[0], out)


def prepare(place, *halves):
    width = halves[0].shape[-1]
    return pl.pallas_call(
        prepare_kernel if len(halves) == 2 else prepare_parts_kernel,
        out_shape=jax.ShapeDtypeStruct((4, width, width), bf16),
        in_specs=[SMEM] + [VMEM] * len(halves),
        name="prepare",
        cost_estimate=pl.CostEstimate(flops=5 * 10**9, bytes_accessed=0, transcendentals=0),
        compiler_params=params(12),
    )(place, *halves)


def mixed(weights, blocks, start, count):
    rows = jnp.concatenate([block[start : start + count] for block in blocks], 0)
    return jnp.dot(weights, rows, precision=lax.Precision.HIGHEST, preferred_element_type=f32)


def mix_own_kernel(place, table, ends, out):
    count = ends.shape[0] // 2
    weights = table[place[2]][:, :count]
    for i in range(2):
        out[i] = mixed(weights, [ends], i * count, count)


def mix_kernel(place, table, own, *refs):
    blocks, outs = refs[:-2], refs[-2:]
    count = blocks[0].shape[0] // 2
    weights = table[place[2]][:, count:]
    for i, out in enumerate(outs):
        out[...] = own[i] + mixed(weights, blocks, i * count, count)


def mix_ends(place, table, ends, blocks):
    rows, width = table.shape[1], ends.shape[1]
    shape = jax.ShapeDtypeStruct((rows, width), f32)
    own = pl.pallas_call(
        mix_own_kernel,
        out_shape=jax.ShapeDtypeStruct((2, rows, width), f32),
        in_specs=[SMEM, VMEM, VMEM],
        name="mix_own",
        compiler_params=params(12),
    )(place, table, ends)
    return pl.pallas_call(
        mix_kernel,
        out_shape=(shape, shape),
        in_specs=[SMEM] + [VMEM] * (2 + len(blocks)),
        name="mix_ends",
        compiler_params=params(12),
    )(place, table, own, *blocks)


def pair_kernel(place, own, ends, beside, total):
    total[...] = ends[...]

    @pl.when(place[1] == 1)
    def _():
        total[...] = carried(beside[...], own) + ends[...]


def pair_total(place, own, ends, beside):
    return pl.pallas_call(
        pair_kernel,
        out_shape=jax.ShapeDtypeStruct(ends.shape, f32),
        in_specs=[SMEM] + [VMEM] * 3,
        name="pair_total",
        compiler_params=params(12),
    )(place, own, ends, beside)


def carry_kernel(pair, place, value, own, partner, start, out):
    out[...] = start[...]

    @pl.when((place[1] == 1) & (place[3] == pair))
    def _():
        out[...] = carried(carried(value[...], partner), own) + start[...]


def carry(pair, place, value, own, partner, start):
    return pl.pallas_call(
        functools.partial(carry_kernel, pair),
        out_shape=jax.ShapeDtypeStruct(value.shape, f32),
        in_specs=[SMEM] + [VMEM] * 4,
        name="carry",
        compiler_params=params(12),
    )(place, value, own, partner, start)


def sweep_kernel(order, place, inverse, coupling, right, state, partner, beside, middle, middle_ends, *refs):
    arrivals, (out, at_group) = refs[:-2], refs[-2:]
    tiles, width, _ = inverse.shape
    local = state.shape[0]
    half = tiles // 2
    core, upper = place[0], place[1]

    inflow = jnp.zeros(at_group.shape, f32)
    for i in range(len(arrivals) // 2):
        arrived = jnp.where(upper == 1, arrivals[2 * i + 1][...], arrivals[2 * i][...])
        inflow = jnp.where(place[3] == i + 1, arrived, inflow)
    at_group[...] = inflow

    @pl.when(upper == 1)
    def _():
        at_group[...] = carried(inflow, partner) + beside[...]

    starts = [at_group[...]]
    starts.append(carried(starts[0], middle) + middle_ends[...])
    a = [start[:local] for start in starts]
    w = [start[local:] for start in starts]
    for k in range(half):
        steps = [order[k], order[k + half]]
        here = [right[tile] for tile in steps]
        turned = [tall_dot(jnp.concatenate([a[s], w[s]], 0), coupling[tile]) for s, tile in enumerate(steps)]
        a = [tall_dot(here[s][:local] - turned[s][:local], inverse[tile]) for s, tile in enumerate(steps)]
        w = [tall_dot(here[s][local:] - a[s] - turned[s][local:], inverse[tile]) for s, tile in enumerate(steps)]
        for s, tile in enumerate(steps):
            for i in range(local):
                out[i, pl.ds(tile, 1), :] = state[i, pl.ds(tile, 1), :] + w[s][i : i + 1]


def sweep(order, place, inverse, coupling, right, state, *rest):
    local, _, width = state.shape
    return pl.pallas_call(
        sweep_kernel,
        out_shape=jax.ShapeDtypeStruct(state.shape, f32),
        in_specs=[SMEM, SMEM] + [VMEM] * (4 + len(rest)),
        scratch_shapes=[pltpu.VMEM((2 * local, width), f32)],
        name="sweep",
        compiler_params=params(24),
    )(order, place, inverse, coupling, right, state, *rest)


def after(value, *others):
    return lax.optimization_barrier((value, *others))[0]


def on_device(state, forcing, inverse, coupling, order):
    local, tiles, width = state.shape
    groups = lax.axis_size("axial")
    devices = lax.axis_size("inst")
    me, group = lax.axis_index("inst"), lax.axis_index("axial")
    place = jnp.stack([me % CORES, group % 2, me, group // 2]).astype(jnp.int32)
    right_table, chain_table = mixing_tables(devices, local)

    def over_inst(value, bit):
        return lax.ppermute(value, "inst", [(i, i ^ bit) for i in range(devices)])

    def over_pair(value):
        return lax.ppermute(value, "axial", [(g, g ^ 1) for g in range(groups)])

    def next_pair(value, pair, target):
        bit = (2 * pair + 1) ^ (2 * pair + 2 + target)
        if groups & (groups - 1):
            return lax.ppermute(value, "axial", [(2 * pair + 1, 2 * pair + 2 + target)])
        return lax.ppermute(value, "axial", [(g, g ^ bit) for g in range(groups)])

    def with_rest(value):
        return [value, over_inst(value, 1)]

    whole, whole_p, whole_q, middle, ends, packed = chain(order, place, inverse, coupling, state, forcing)

    blocks = [over_inst(ends, s) for s in range(1, devices)]
    partner_p = over_pair(whole_p)
    own = prepare(place, *with_rest(whole))
    ends, middle_ends = mix_ends(place, jnp.asarray(chain_table), ends, blocks)
    beside = after(over_pair(ends), own)
    partner_q = over_pair(after(whole_q, ends))
    packed, middle = after(packed, ends), after(middle, ends)
    packs = [packed] + [over_inst(packed, s) for s in range(CORES, devices, CORES)]
    middle = with_rest(middle)
    partner_p = with_rest(after(partner_p, beside))
    total = pair_total(place, own, ends, beside)
    middle = prepare(place, after(middle[0], total), middle[1])
    partner_q = with_rest(after(partner_q, total))
    partner = prepare(place, partner_p[0], partner_q[0], partner_p[1], partner_q[1])

    arrivals = []
    leaving = total
    for pair in range(groups // 2 - 1):
        if pair:
            leaving = carry(pair, place, arrivals[-1], own, partner, total)
        arrivals += [next_pair(leaving, pair, 0), next_pair(leaving, pair, 1)]
        if not pair:
            arrivals[-1] = after(arrivals[-1], middle, *packs[1:])
        if pair == min(1, groups // 2 - 2):
            packs = [after(pack, leaving) for pack in packs]
            packs = [block for pack in packs for block in (pack, over_inst(pack, 1))]
            right = right_sides(place, jnp.asarray(right_table), packs)
    if groups > 2:
        arrivals[-1] = after(arrivals[-1], right)
    return sweep(order, place, inverse, coupling, right, state, partner, beside, middle, middle_ends, *arrivals)


def solution(mesh):
    return jax.shard_map(
        on_device,
        mesh=mesh,
        in_specs=(
            P("inst", "axial", None),
            P("inst", "axial", None),
            P("axial", None, None),
            P("axial", None, None),
            P("axial"),
        ),
        out_specs=P("inst", "axial", None),
        check_vma=False,
    )
```

```python
import functools

import jax
import jax.numpy as jnp
import numpy as np
from jax import lax
from jax.experimental import pallas as pl
from jax.experimental.pallas import tpu as pltpu
from jax.sharding import PartitionSpec as P

NT = (((1,), (1,)), ((), ()))
NN = (((1,), (0,)), ((), ()))
bf16 = jnp.bfloat16
f32 = jnp.float32
SMEM = pl.BlockSpec(memory_space=pltpu.SMEM)
VMEM = pl.BlockSpec(memory_space=pltpu.VMEM)
HBM = pl.BlockSpec(memory_space=pltpu.HBM)
CORES = 2


def params(mebibytes):
    return pltpu.CompilerParams(vmem_limit_bytes=mebibytes << 20)


def batches(count):
    edges = [0]
    while edges[-1] < count:
        edges.append(min(count, max(1, 2 * edges[-1])))
    return dict(zip(edges, edges[1:]))


def mixing(period):
    distance = np.arange(period)[:, None] - np.arange(period)[None, :]
    angles = np.pi * distance / period
    sine = np.where(distance == 0, 1.0, np.sin(angles))
    parity = 1.0 - 2.0 * (distance % 2)
    derivative = np.where(distance == 0, 0.0, 0.5 * parity * np.cos(angles) / sine)
    mix = derivative * (2.0 / period) + np.eye(period)
    return mix, mix @ mix


def mixing_tables(devices, local):
    period = devices * local
    mix, twice = mixing(period)
    eye, none = np.eye(period), np.zeros((period, period))
    rights, chains = [], []
    for i in range(devices):
        rows = np.arange(local) + i * local
        right, chain = [], []
        for s in range(devices):
            columns = np.arange(local) + (i ^ s) * local
            cut = lambda upper, lower: np.concatenate([upper[rows][:, columns], lower[rows][:, columns]], 0)
            right += [cut(mix, 2 * eye), cut(-twice, -2 * mix)]
            chain += [cut(mix, 2 * eye), cut(-twice, -2 * mix), cut(none, -mix), cut(none, twice)]
        rights.append(np.concatenate(right, 1))
        chains.append(np.concatenate(chain, 1))
    rights, chains = np.stack(rights).astype(np.float32), np.stack(chains).astype(np.float32)
    high = rights.astype(bf16)
    low = (rights - high.astype(np.float32)).astype(bf16)
    return np.concatenate([high, low, high], 2), chains


def split(value):
    high = value.astype(bf16)
    return high, (value - high.astype(f32)).astype(bf16)


def block_dot(value, matrix):
    rows, width = value.shape
    main = width // 256 * 256
    high, low = split(value)
    if not main or 2 * (width - main) > 256:
        return tall_dot(value, matrix)
    both = jnp.concatenate([high[:, :main], low[:, :main]], 0)
    both = lax.dot_general(both, matrix[:, :main], NT, preferred_element_type=f32)
    both = both[:rows] + both[rows:]
    if width == main:
        return both
    rest = jnp.concatenate([high[:, main:], low[:, main:]], 1)
    twice = jnp.concatenate([matrix[:, main:], matrix[:, main:]], 1)
    return both + lax.dot_general(rest, twice, NT, preferred_element_type=f32)


def tall_dot(value, matrix):
    rows = value.shape[0]
    both = lax.dot_general(jnp.concatenate(split(value), 0), matrix, NT, preferred_element_type=f32)
    return both[:rows] + both[rows:]


def chain_kernel(order, place, inverse_hbm, coupling_hbm, state, forcing, whole, lead, trail, middle, ends, packed,
                 inverse, coupling, both, inverse_sem, coupling_sem):
    tiles, width, _ = inverse.shape
    local = state.shape[0]
    part = width // CORES
    rows = part + 2 * local
    half = tiles // 2
    runs = batches(tiles)

    def fetch(k):
        tile = order[k]
        return (
            pltpu.make_async_copy(coupling_hbm.at[tile], coupling.at[k], coupling_sem.at[k]),
            pltpu.make_async_copy(inverse_hbm.at[tile], inverse.at[k], inverse_sem.at[k]),
        )

    for k in range(tiles):
        for copy in fetch(k):
            copy.start()

    def with_terms(k, turned):
        tile = order[k]
        terms = [array[i, pl.ds(tile, 1), :] for array in (forcing, state) for i in range(local)]
        terms = jnp.concatenate(terms, 0)
        packed[tile] = terms
        return jnp.concatenate([-turned[:part], terms - turned[part:]], 0)

    def keep_first(out, offset):
        out[0] = both[:part]
        ends[offset : offset + 2 * local] = both[part:rows]

    def keep_second(out, offset):
        out[1] = both[rows : rows + part]
        ends[offset + 2 * local : offset + 4 * local] = both[rows + part :]

    ids = lax.broadcasted_iota(jnp.int32, (rows, width), 0)
    columns = lax.broadcasted_iota(jnp.int32, (rows, width), 1)
    first = jnp.where((ids < part) & (columns == ids + place[0] * part), 1.0, 0.0)
    second = None
    for k in range(tiles + 1):
        for j in range(k, runs.get(k, k)):
            for copy in fetch(j):
                copy.wait()
        ahead = with_terms(k, block_dot(first, coupling[k])) if k < tiles else None
        behind = None
        if k > 0:
            behind = first if k == 1 else first - block_dot(second, coupling[k - 1])
        if k < tiles:
            first = block_dot(ahead, inverse[k])
            both[:rows] = first
        if k > 0:
            second = block_dot(behind, inverse[k - 1])
            both[rows:] = second
        if k == half - 1:
            keep_first(middle, 4 * local)
        if k == half:
            keep_second(middle, 4 * local)
    keep_first(whole, 0)
    keep_second(whole, 0)
    kept = lead.shape[0] - part
    lead[:part] = both[:part]
    lead[part:] = both[rows : rows + kept]
    trail[...] = both[rows + kept : rows + part]


def chain(order, place, inverse, coupling, state, forcing):
    local, tiles, width = state.shape
    part = width // CORES
    trailing = part // 32 * 16
    half = jax.ShapeDtypeStruct((2, part, width), f32)
    return pl.pallas_call(
        chain_kernel,
        out_shape=(
            half,
            jax.ShapeDtypeStruct((2 * part - trailing, width), f32),
            jax.ShapeDtypeStruct((trailing, width), f32),
            half,
            jax.ShapeDtypeStruct((8 * local, width), f32),
            jax.ShapeDtypeStruct((tiles, 2 * local, width), f32),
        ),
        in_specs=[SMEM, SMEM, HBM, HBM, VMEM, VMEM],
        scratch_shapes=[
            pltpu.VMEM((tiles, width, width), bf16),
            pltpu.VMEM((tiles, width, width), bf16),
            pltpu.VMEM((2 * (part + 2 * local), width), f32),
            pltpu.SemaphoreType.DMA((tiles,)),
            pltpu.SemaphoreType.DMA((tiles,)),
        ],
        name="chain",
        compiler_params=params(60),
    )(order, place, inverse, coupling, state, forcing)


def right_kernel(place, table, *refs):
    blocks, out = refs[:-1], refs[-1]
    weights = table[place[2]]
    for tile in range(out.shape[0]):
        high, low = split(jnp.concatenate([block[tile] for block in blocks], 0))
        out[tile] = lax.dot_general(weights, jnp.concatenate([high, high, low], 0), NN, preferred_element_type=f32)


def right_sides(place, table, blocks):
    return pl.pallas_call(
        right_kernel,
        out_shape=jax.ShapeDtypeStruct(blocks[0].shape, f32),
        in_specs=[SMEM] + [VMEM] * (1 + len(blocks)),
        name="right_sides",
        compiler_params=params(12),
    )(place, table, *blocks)


def split_half(source, start, high, low):
    rows = source.shape[0]
    start = pl.multiple_of(start, 16)
    high[pl.ds(start, rows), :], low[pl.ds(start, rows), :] = split(source)


def times(value, high, low):
    upper, lower = split(value)
    rows = value.shape[0]
    both = lax.dot_general(jnp.concatenate([upper, lower], 0), high, NN, preferred_element_type=f32)
    return both[:rows] + both[rows:] + lax.dot_general(upper, low, NN, preferred_element_type=f32)


def carried(value, parts):
    rows = value.shape[0] // 2
    p_high, p_low, q_high, q_low = (ref[i] for ref in parts for i in range(ref.shape[0]))
    moved = times(value, p_high, p_low)
    return jnp.concatenate([moved[:rows], moved[rows:] - times(value[:rows], q_high, q_low)], 0)


def prepare_kernel(place, mine, rest, out):
    rows = mine.shape[1]
    for i in range(2):
        split_half(mine[i], place[0] * rows, out.at[2 * i], out.at[2 * i + 1])
        split_half(rest[i], (1 - place[0]) * rows, out.at[2 * i], out.at[2 * i + 1])


def prepare_p_kernel(place, lead, lead_rest, out):
    rows = out.shape[1] // CORES
    split_half(lead[:rows], place[0] * rows, out.at[0], out.at[1])
    split_half(lead_rest[:rows], (1 - place[0]) * rows, out.at[0], out.at[1])


def prepare_q_kernel(place, lead, lead_rest, trail, trail_rest, out):
    rows = out.shape[1] // CORES
    for first, last, half in ((lead, trail, place[0]), (lead_rest, trail_rest, 1 - place[0])):
        split_half(jnp.concatenate([first[rows:], last[...]], 0), half * rows, out.at[0], out.at[1])


def prepare(place, *halves):
    width = halves[0].shape[-1]
    kernel = prepare_q_kernel if len(halves) == 4 else prepare_kernel if halves[0].ndim == 3 else prepare_p_kernel
    return pl.pallas_call(
        kernel,
        out_shape=jax.ShapeDtypeStruct((4 if kernel is prepare_kernel else 2, width, width), bf16),
        in_specs=[SMEM] + [VMEM] * len(halves),
        name="prepare",
        cost_estimate=pl.CostEstimate(flops=5 * 10**9, bytes_accessed=0, transcendentals=0),
        compiler_params=params(12),
    )(place, *halves)


def mixed(weights, blocks, start, count):
    rows = jnp.concatenate([block[start : start + count] for block in blocks], 0)
    return jnp.dot(weights, rows, precision=lax.Precision.HIGHEST, preferred_element_type=f32)


def mix_own_kernel(place, table, ends, out):
    count = ends.shape[0] // 2
    weights = table[place[2]][:, :count]
    for i in range(2):
        out[i] = mixed(weights, [ends], i * count, count)


def mix_kernel(place, table, own, *refs):
    blocks, outs = refs[:-2], refs[-2:]
    count = blocks[0].shape[0] // 2
    weights = table[place[2]][:, count:]
    for i, out in enumerate(outs):
        out[...] = own[i] + mixed(weights, blocks, i * count, count)


def mix_ends(place, table, ends, blocks):
    rows, width = table.shape[1], ends.shape[1]
    shape = jax.ShapeDtypeStruct((rows, width), f32)
    own = pl.pallas_call(
        mix_own_kernel,
        out_shape=jax.ShapeDtypeStruct((2, rows, width), f32),
        in_specs=[SMEM, VMEM, VMEM],
        name="mix_own",
        compiler_params=params(12),
    )(place, table, ends)
    return pl.pallas_call(
        mix_kernel,
        out_shape=(shape, shape),
        in_specs=[SMEM] + [VMEM] * (2 + len(blocks)),
        name="mix_ends",
        compiler_params=params(12),
    )(place, table, own, *blocks)


def pair_kernel(place, own, ends, beside, total):
    total[...] = ends[...]

    @pl.when(place[1] == 1)
    def _():
        total[...] = carried(beside[...], [own]) + ends[...]


def pair_total(place, own, ends, beside):
    return pl.pallas_call(
        pair_kernel,
        out_shape=jax.ShapeDtypeStruct(ends.shape, f32),
        in_specs=[SMEM] + [VMEM] * 3,
        name="pair_total",
        compiler_params=params(12),
    )(place, own, ends, beside)


def carry_kernel(pair, place, own, partner_p, partner_q, ends, beside, *refs):
    arrivals, out = refs[:-1], refs[-1]
    own, partner = [own], [partner_p, partner_q]
    out[...] = ends[...]

    @pl.when((place[1] == 1) & (place[3] == pair))
    def _():
        out[...] = carried(carried(arrivals[0][...], partner) + beside[...], own) + ends[...]

    @pl.when((place[1] == 0) & (place[3] == pair))
    def _():
        out[...] = carried(carried(arrivals[-1][...], own) + ends[...], partner) + beside[...]


def carry(pair, place, own, partner, ends, beside, arrivals):
    return pl.pallas_call(
        functools.partial(carry_kernel, pair),
        out_shape=jax.ShapeDtypeStruct(ends.shape, f32),
        in_specs=[SMEM] + [VMEM] * (5 + len(arrivals)),
        name="carry",
        compiler_params=params(12),
    )(place, own, *partner, ends, beside, *arrivals)


def sweep_kernel(order, place, inverse, coupling, right, state, partner_p, partner_q, beside, middle, middle_ends, *refs):
    arrivals, (out, at_group) = refs[:-2], refs[-2:]
    tiles, width, _ = inverse.shape
    local = state.shape[0]
    half = tiles // 2
    core, upper = place[0], place[1]

    inflow = jnp.zeros(at_group.shape, f32)
    for i, arrived in enumerate(arrivals[1:]):
        inflow = jnp.where(place[3] == i + 1, arrived[...], inflow)
    if arrivals:
        inflow = jnp.where((place[3] == 1) & (upper == 1), arrivals[0][...], inflow)
    at_group[...] = inflow

    @pl.when(upper == 1)
    def _():
        at_group[...] = carried(inflow, [partner_p, partner_q]) + beside[...]

    starts = [at_group[...]]
    starts.append(carried(starts[0], [middle]) + middle_ends[...])
    a = [start[:local] for start in starts]
    w = [start[local:] for start in starts]
    for k in range(half):
        steps = [order[k], order[k + half]]
        here = [right[tile] for tile in steps]
        turned = [tall_dot(jnp.concatenate([a[s], w[s]], 0), coupling[tile]) for s, tile in enumerate(steps)]
        a = [tall_dot(here[s][:local] - turned[s][:local], inverse[tile]) for s, tile in enumerate(steps)]
        w = [tall_dot(here[s][local:] - a[s] - turned[s][local:], inverse[tile]) for s, tile in enumerate(steps)]
        for s, tile in enumerate(steps):
            for i in range(local):
                out[i, pl.ds(tile, 1), :] = state[i, pl.ds(tile, 1), :] + w[s][i : i + 1]


def sweep(order, place, inverse, coupling, right, state, *rest):
    local, _, width = state.shape
    return pl.pallas_call(
        sweep_kernel,
        out_shape=jax.ShapeDtypeStruct(state.shape, f32),
        in_specs=[SMEM, SMEM] + [VMEM] * (4 + len(rest)),
        scratch_shapes=[pltpu.VMEM((2 * local, width), f32)],
        name="sweep",
        compiler_params=params(24),
    )(order, place, inverse, coupling, right, state, *rest)


def after(value, *others):
    return lax.optimization_barrier((value, *others))[0]


def on_device(state, forcing, inverse, coupling, order):
    local, tiles, width = state.shape
    groups = lax.axis_size("axial")
    devices = lax.axis_size("inst")
    me, group = lax.axis_index("inst"), lax.axis_index("axial")
    place = jnp.stack([me % CORES, group % 2, me, group // 2]).astype(jnp.int32)
    right_table, chain_table = mixing_tables(devices, local)

    def over_inst(value, bit):
        return lax.ppermute(value, "inst", [(i, i ^ bit) for i in range(devices)])

    def over_pair(value):
        return lax.ppermute(value, "axial", [(g, g ^ 1) for g in range(groups)])

    def swapped(value, source, target):
        if groups & (groups - 1):
            return lax.ppermute(value, "axial", [(source, target)])
        return lax.ppermute(value, "axial", [(g, g ^ source ^ target) for g in range(groups)])

    def with_rest(value):
        return [value, over_inst(value, 1)]

    whole, lead, trail, middle, ends, packed = chain(order, place, inverse, coupling, state, forcing)

    blocks = [over_inst(ends, s) for s in range(1, devices)]
    lead = over_pair(lead)
    own = prepare(place, *with_rest(whole))
    ends, middle_ends = mix_ends(place, jnp.asarray(chain_table), ends, blocks)
    beside = after(over_pair(ends), own)
    trail = over_pair(after(trail, ends))
    packed, middle = after(packed, ends), after(middle, ends)
    packs = [packed] + [over_inst(packed, s) for s in range(CORES, devices, CORES)]
    middle = with_rest(middle)
    total = pair_total(place, own, ends, beside)
    middle = prepare(place, after(middle[0], total), middle[1])
    lead = with_rest(after(lead, beside))
    trail = with_rest(after(trail, total))
    partner = prepare(place, *lead), prepare(place, *lead, *trail)

    arrivals = []
    if groups > 2:
        arrivals = [swapped(total, 1, 3), swapped(total, 1, 2)]
        arrivals[0] = after(arrivals[0], middle, *packs[1:])
    leaving = total
    for pair in range(1, groups // 2 - 1):
        came = arrivals if pair == 1 else arrivals[-1:]
        leaving = carry(pair, place, own, partner, ends, beside, came)
        arrivals.append(swapped(leaving, 2 * pair, 2 * pair + 2))
        if pair == 1:
            packs = [after(pack, leaving) for pack in packs]
    packs = [block for pack in packs for block in (pack, over_inst(pack, 1))]
    right = right_sides(place, jnp.asarray(right_table), packs)
    if arrivals:
        arrivals[-1] = after(arrivals[-1], right)
    return sweep(order, place, inverse, coupling, right, state, *partner, beside, middle, middle_ends, *arrivals)


def solution(mesh):
    return jax.shard_map(
        on_device,
        mesh=mesh,
        in_specs=(
            P("inst", "axial", None),
            P("inst", "axial", None),
            P("axial", None, None),
            P("axial", None, None),
            P("axial"),
        ),
        out_specs=P("inst", "axial", None),
        check_vma=False,
    )
```

```python
import functools

import jax
import jax.numpy as jnp
import numpy as np
from jax import lax
from jax.experimental import pallas as pl
from jax.experimental.pallas import tpu as pltpu
from jax.sharding import PartitionSpec as P

NT = (((1,), (1,)), ((), ()))
NN = (((1,), (0,)), ((), ()))
bf16 = jnp.bfloat16
f32 = jnp.float32
SMEM = pl.BlockSpec(memory_space=pltpu.SMEM)
VMEM = pl.BlockSpec(memory_space=pltpu.VMEM)
HBM = pl.BlockSpec(memory_space=pltpu.HBM)
CORES = 2


def params(mebibytes):
    return pltpu.CompilerParams(vmem_limit_bytes=mebibytes << 20)


def batches(count):
    edges = [0]
    while edges[-1] < count:
        edges.append(min(count, max(1, 2 * edges[-1])))
    return dict(zip(edges, edges[1:]))


def mixing(period):
    distance = np.arange(period)[:, None] - np.arange(period)[None, :]
    angles = np.pi * distance / period
    sine = np.where(distance == 0, 1.0, np.sin(angles))
    parity = 1.0 - 2.0 * (distance % 2)
    derivative = np.where(distance == 0, 0.0, 0.5 * parity * np.cos(angles) / sine)
    mix = derivative * (2.0 / period) + np.eye(period)
    return mix, mix @ mix


def mixing_tables(devices, local):
    period = devices * local
    mix, twice = mixing(period)
    eye, none = np.eye(period), np.zeros((period, period))
    rights, chains = [], []
    for i in range(devices):
        rows = np.arange(local) + i * local
        right, chain = [], []
        for s in range(devices):
            columns = np.arange(local) + (i ^ s) * local
            cut = lambda upper, lower: np.concatenate([upper[rows][:, columns], lower[rows][:, columns]], 0)
            right += [cut(mix, 2 * eye), cut(-twice, -2 * mix)]
            chain += [cut(mix, 2 * eye), cut(-twice, -2 * mix), cut(none, -mix), cut(none, twice)]
        rights.append(np.concatenate(right, 1))
        chains.append(np.concatenate(chain, 1))
    rights, chains = np.stack(rights).astype(np.float32), np.stack(chains).astype(np.float32)
    high = rights.astype(bf16)
    low = (rights - high.astype(np.float32)).astype(bf16)
    return np.concatenate([high, low, high], 2), chains


def split(value):
    high = value.astype(bf16)
    return high, (value - high.astype(f32)).astype(bf16)


def block_dot(value, matrix):
    rows, width = value.shape
    main = width // 256 * 256
    high, low = split(value)
    if not main or 2 * (width - main) > 256:
        return tall_dot(value, matrix)
    both = jnp.concatenate([high[:, :main], low[:, :main]], 0)
    both = lax.dot_general(both, matrix[:, :main], NT, preferred_element_type=f32)
    both = both[:rows] + both[rows:]
    if width == main:
        return both
    rest = jnp.concatenate([high[:, main:], low[:, main:]], 1)
    twice = jnp.concatenate([matrix[:, main:], matrix[:, main:]], 1)
    return both + lax.dot_general(rest, twice, NT, preferred_element_type=f32)


def tall_dot(value, matrix):
    rows = value.shape[0]
    both = lax.dot_general(jnp.concatenate(split(value), 0), matrix, NT, preferred_element_type=f32)
    return both[:rows] + both[rows:]


def chain_kernel(order, place, inverse_hbm, coupling_hbm, state, forcing, whole, middle, ends, last_ends, packed,
                 inverse, coupling, both, inverse_sem, coupling_sem):
    tiles, width, _ = inverse.shape
    local = state.shape[0]
    part = width // CORES
    rows = part + 2 * local
    half = tiles // 2
    runs = batches(tiles)

    def fetch(k):
        tile = order[k]
        return (
            pltpu.make_async_copy(coupling_hbm.at[tile], coupling.at[k], coupling_sem.at[k]),
            pltpu.make_async_copy(inverse_hbm.at[tile], inverse.at[k], inverse_sem.at[k]),
        )

    for k in range(tiles):
        for copy in fetch(k):
            copy.start()

    def with_terms(k, turned):
        tile = order[k]
        terms = [array[i, pl.ds(tile, 1), :] for array in (forcing, state) for i in range(local)]
        terms = jnp.concatenate(terms, 0)
        packed[tile] = terms
        return jnp.concatenate([-turned[:part], terms - turned[part:]], 0)

    def keep_first(out, offset):
        out[0] = both[:part]
        ends[offset : offset + 2 * local] = both[part:rows]

    def keep_second(out, offset):
        out[1] = both[rows : rows + part]
        ends[offset + 2 * local : offset + 4 * local] = both[rows + part :]

    ids = lax.broadcasted_iota(jnp.int32, (rows, width), 0)
    columns = lax.broadcasted_iota(jnp.int32, (rows, width), 1)
    first = jnp.where((ids < part) & (columns == ids + place[0] * part), 1.0, 0.0)
    second = None
    for k in range(tiles + 1):
        for j in range(k, runs.get(k, k)):
            for copy in fetch(j):
                copy.wait()
        ahead = with_terms(k, block_dot(first, coupling[k])) if k < tiles else None
        behind = None
        if k > 0:
            behind = first if k == 1 else first - block_dot(second, coupling[k - 1])
        if k < tiles:
            first = block_dot(ahead, inverse[k])
            both[:rows] = first
        if k > 0:
            second = block_dot(behind, inverse[k - 1])
            both[rows:] = second
        if k == half - 1:
            keep_first(middle, 4 * local)
        if k == half:
            keep_second(middle, 4 * local)
    keep_first(whole, 0)
    keep_second(whole, 0)
    last_ends[: 2 * local] = both[part:rows]
    last_ends[2 * local :] = both[rows + part :]


def chain(order, place, inverse, coupling, state, forcing):
    local, tiles, width = state.shape
    part = width // CORES
    half = jax.ShapeDtypeStruct((2, part, width), f32)
    return pl.pallas_call(
        chain_kernel,
        out_shape=(
            half,
            half,
            jax.ShapeDtypeStruct((8 * local, width), f32),
            jax.ShapeDtypeStruct((4 * local, width), f32),
            jax.ShapeDtypeStruct((tiles, 2 * local, width), f32),
        ),
        in_specs=[SMEM, SMEM, HBM, HBM, VMEM, VMEM],
        scratch_shapes=[
            pltpu.VMEM((tiles, width, width), bf16),
            pltpu.VMEM((tiles, width, width), bf16),
            pltpu.VMEM((2 * (part + 2 * local), width), f32),
            pltpu.SemaphoreType.DMA((tiles,)),
            pltpu.SemaphoreType.DMA((tiles,)),
        ],
        name="chain",
        compiler_params=params(60),
    )(order, place, inverse, coupling, state, forcing)


def right_kernel(place, table, *refs):
    blocks, out = refs[:-1], refs[-1]
    weights = table[place[2]]
    for tile in range(out.shape[0]):
        high, low = split(jnp.concatenate([block[tile] for block in blocks], 0))
        out[tile] = lax.dot_general(weights, jnp.concatenate([high, high, low], 0), NN, preferred_element_type=f32)


def right_sides(place, table, blocks):
    return pl.pallas_call(
        right_kernel,
        out_shape=jax.ShapeDtypeStruct(blocks[0].shape, f32),
        in_specs=[SMEM] + [VMEM] * (1 + len(blocks)),
        name="right_sides",
        compiler_params=params(12),
    )(place, table, *blocks)


def split_half(source, start, high, low):
    rows = source.shape[0]
    start = pl.multiple_of(start, 16)
    high[pl.ds(start, rows), :], low[pl.ds(start, rows), :] = split(source)


def times(value, high, low):
    upper, lower = split(value)
    rows = value.shape[0]
    both = lax.dot_general(jnp.concatenate([upper, lower], 0), high, NN, preferred_element_type=f32)
    return both[:rows] + both[rows:] + lax.dot_general(upper, low, NN, preferred_element_type=f32)


def carried(value, parts):
    rows = value.shape[0] // 2
    p_high, p_low, q_high, q_low = (parts[i] for i in range(4))
    moved = times(value, p_high, p_low)
    return jnp.concatenate([moved[:rows], moved[rows:] - times(value[:rows], q_high, q_low)], 0)


def prepare_kernel(place, mine, rest, out):
    rows = mine.shape[1]
    for i in range(2):
        split_half(mine[i], place[0] * rows, out.at[2 * i], out.at[2 * i + 1])
        split_half(rest[i], (1 - place[0]) * rows, out.at[2 * i], out.at[2 * i + 1])


def prepare(place, mine, rest, cost=0):
    width = mine.shape[2]
    return pl.pallas_call(
        prepare_kernel,
        out_shape=jax.ShapeDtypeStruct((4, width, width), bf16),
        in_specs=[SMEM, VMEM, VMEM],
        name="prepare",
        cost_estimate=pl.CostEstimate(flops=cost, bytes_accessed=0, transcendentals=0),
        compiler_params=params(12),
    )(place, mine, rest)


def mixed(weights, blocks, start, count):
    rows = jnp.concatenate([block[start : start + count] for block in blocks], 0)
    return jnp.dot(weights, rows, precision=lax.Precision.HIGHEST, preferred_element_type=f32)


def mix_kernel(place, table, *refs):
    blocks, outs = refs[:-2], refs[-2:]
    count = blocks[0].shape[0] // 2
    for i, out in enumerate(outs):
        out[...] = mixed(table[place[2]], blocks, i * count, count)


def mix_ends(place, table, blocks):
    shape = jax.ShapeDtypeStruct((table.shape[1], blocks[0].shape[1]), f32)
    return pl.pallas_call(
        mix_kernel,
        out_shape=(shape, shape),
        in_specs=[SMEM] + [VMEM] * (1 + len(blocks)),
        name="mix_ends",
        compiler_params=params(12),
    )(place, table, *blocks)


def pair_kernel(place, table, own, ends, *refs):
    blocks, (beside, total) = refs[:-2], refs[-2:]
    came = mixed(table[place[2]], blocks, 0, blocks[0].shape[0])
    beside[...] = came
    total[...] = ends[...]

    @pl.when(place[1] == 1)
    def _():
        total[...] = carried(came, own) + ends[...]


def pair_total(place, table, own, ends, blocks):
    shape = jax.ShapeDtypeStruct(ends.shape, f32)
    return pl.pallas_call(
        pair_kernel,
        out_shape=(shape, shape),
        in_specs=[SMEM] + [VMEM] * (3 + len(blocks)),
        name="pair_total",
        compiler_params=params(12),
    )(place, table, own, ends, *blocks)


def carry_kernel(pair, place, own, partner, ends, beside, *refs):
    arrivals, out = refs[:-1], refs[-1]
    out[...] = ends[...]

    @pl.when((place[1] == 1) & (place[3] == pair))
    def _():
        out[...] = carried(carried(arrivals[0][...], partner) + beside[...], own) + ends[...]

    @pl.when((place[1] == 0) & (place[3] == pair))
    def _():
        out[...] = carried(carried(arrivals[-1][...], own) + ends[...], partner) + beside[...]


def carry(pair, place, own, partner, ends, beside, arrivals):
    return pl.pallas_call(
        functools.partial(carry_kernel, pair),
        out_shape=jax.ShapeDtypeStruct(ends.shape, f32),
        in_specs=[SMEM] + [VMEM] * (4 + len(arrivals)),
        name="carry",
        compiler_params=params(12),
    )(place, own, partner, ends, beside, *arrivals)


def sweep_kernel(order, place, inverse, coupling, right, state, partner, beside, middle, middle_ends, *refs):
    arrivals, (out, at_group) = refs[:-2], refs[-2:]
    tiles, width, _ = inverse.shape
    local = state.shape[0]
    half = tiles // 2
    core, upper = place[0], place[1]

    inflow = jnp.zeros(at_group.shape, f32)
    for i, arrived in enumerate(arrivals[1:]):
        inflow = jnp.where(place[3] == i + 1, arrived[...], inflow)
    if arrivals:
        inflow = jnp.where((place[3] == 1) & (upper == 1), arrivals[0][...], inflow)
    at_group[...] = inflow

    @pl.when(upper == 1)
    def _():
        at_group[...] = carried(inflow, partner) + beside[...]

    starts = [at_group[...]]
    starts.append(carried(starts[0], middle) + middle_ends[...])
    a = [start[:local] for start in starts]
    w = [start[local:] for start in starts]
    for k in range(half):
        steps = [order[k], order[k + half]]
        here = [right[tile] for tile in steps]
        turned = [tall_dot(jnp.concatenate([a[s], w[s]], 0), coupling[tile]) for s, tile in enumerate(steps)]
        a = [tall_dot(here[s][:local] - turned[s][:local], inverse[tile]) for s, tile in enumerate(steps)]
        w = [tall_dot(here[s][local:] - a[s] - turned[s][local:], inverse[tile]) for s, tile in enumerate(steps)]
        for s, tile in enumerate(steps):
            for i in range(local):
                out[i, pl.ds(tile, 1), :] = state[i, pl.ds(tile, 1), :] + w[s][i : i + 1]


def sweep(order, place, inverse, coupling, right, state, *rest):
    local, _, width = state.shape
    return pl.pallas_call(
        sweep_kernel,
        out_shape=jax.ShapeDtypeStruct(state.shape, f32),
        in_specs=[SMEM, SMEM] + [VMEM] * (4 + len(rest)),
        scratch_shapes=[pltpu.VMEM((2 * local, width), f32)],
        name="sweep",
        compiler_params=params(24),
    )(order, place, inverse, coupling, right, state, *rest)


def after(value, *others):
    return lax.optimization_barrier((value, *others))[0]


def on_device(state, forcing, inverse, coupling, order):
    local, tiles, width = state.shape
    groups = lax.axis_size("axial")
    devices = lax.axis_size("inst")
    me, group = lax.axis_index("inst"), lax.axis_index("axial")
    place = jnp.stack([me % CORES, group % 2, me, group // 2]).astype(jnp.int32)
    right_table, chain_table = mixing_tables(devices, local)

    def over_inst(value, bit):
        return lax.ppermute(value, "inst", [(i, i ^ bit) for i in range(devices)])

    def over_pair(value):
        return lax.ppermute(value, "axial", [(g, g ^ 1) for g in range(groups)])

    def swapped(value, source, target):
        if groups & (groups - 1):
            return lax.ppermute(value, "axial", [(source, target)])
        return lax.ppermute(value, "axial", [(g, g ^ source ^ target) for g in range(groups)])

    def with_rest(value):
        return [value, over_inst(value, 1)]

    whole, middle, ends, last_ends, packed = chain(order, place, inverse, coupling, state, forcing)
    chain_table = jnp.asarray(chain_table)

    beside = over_pair(last_ends)
    blocks = [over_inst(ends, s) for s in range(1, devices)]
    partner = over_pair(whole)
    own = prepare(place, *with_rest(whole), 5 * 10**9)
    ends, middle_ends = mix_ends(place, chain_table, [ends] + blocks)
    beside = after(beside, ends)
    blocks = [beside] + [over_inst(beside, s) for s in range(1, devices)]
    packed, middle = after(packed, ends), after(middle, ends)
    packs = [packed] + [over_inst(packed, s) for s in range(CORES, devices, CORES)]
    packs = [block for pack in packs for block in (pack, over_inst(pack, 1))]
    middle = with_rest(middle)
    beside, total = pair_total(place, chain_table, own, ends, blocks)
    middle = prepare(place, after(middle[0], total), middle[1], 5 * 10**9)
    partner = prepare(place, *with_rest(after(partner, total)))

    arrivals = []
    if groups > 2:
        arrivals = [swapped(total, 1, 3), swapped(total, 1, 2)]
        arrivals[0] = after(arrivals[0], middle, *packs[1:])
    leaving = total
    for pair in range(1, groups // 2 - 1):
        came = arrivals if pair == 1 else arrivals[-1:]
        leaving = carry(pair, place, own, partner, ends, beside, came)
        arrivals.append(swapped(leaving, 2 * pair, 2 * pair + 2))
    right = right_sides(place, jnp.asarray(right_table), packs)
    if arrivals:
        arrivals[-1] = after(arrivals[-1], right)
    return sweep(order, place, inverse, coupling, right, state, partner, beside, middle, middle_ends, *arrivals)


def solution(mesh):
    return jax.shard_map(
        on_device,
        mesh=mesh,
        in_specs=(
            P("inst", "axial", None),
            P("inst", "axial", None),
            P("axial", None, None),
            P("axial", None, None),
            P("axial"),
        ),
        out_specs=P("inst", "axial", None),
        check_vma=False,
    )
```

```python
import functools

import jax
import jax.numpy as jnp
import numpy as np
from jax import lax
from jax.experimental import pallas as pl
from jax.experimental.pallas import tpu as pltpu
from jax.sharding import PartitionSpec as P

NT = (((1,), (1,)), ((), ()))
NN = (((1,), (0,)), ((), ()))
bf16 = jnp.bfloat16
f32 = jnp.float32
SMEM = pl.BlockSpec(memory_space=pltpu.SMEM)
VMEM = pl.BlockSpec(memory_space=pltpu.VMEM)
HBM = pl.BlockSpec(memory_space=pltpu.HBM)
CORES = 2


def params(mebibytes):
    return pltpu.CompilerParams(vmem_limit_bytes=mebibytes << 20)


def batches(count):
    edges = [0]
    while edges[-1] < count:
        edges.append(min(count, max(1, 2 * edges[-1])))
    return dict(zip(edges, edges[1:]))


def mixing(period):
    distance = np.arange(period)[:, None] - np.arange(period)[None, :]
    angles = np.pi * distance / period
    sine = np.where(distance == 0, 1.0, np.sin(angles))
    parity = 1.0 - 2.0 * (distance % 2)
    derivative = np.where(distance == 0, 0.0, 0.5 * parity * np.cos(angles) / sine)
    mix = derivative * (2.0 / period) + np.eye(period)
    return mix, mix @ mix


def mixing_tables(devices, local):
    period = devices * local
    mix, twice = mixing(period)
    eye, none = np.eye(period), np.zeros((period, period))
    rights, chains = [], []
    for i in range(devices):
        rows = np.arange(local) + i * local
        right, chain = [], []
        for s in range(devices):
            columns = np.arange(local) + (i ^ s) * local
            cut = lambda upper, lower: np.concatenate([upper[rows][:, columns], lower[rows][:, columns]], 0)
            right += [cut(mix, 2 * eye), cut(-twice, -2 * mix)]
            chain += [cut(mix, 2 * eye), cut(-twice, -2 * mix), cut(none, -mix), cut(none, twice)]
        rights.append(np.concatenate(right, 1))
        chains.append(np.concatenate(chain, 1))
    rights, chains = np.stack(rights).astype(np.float32), np.stack(chains).astype(np.float32)
    high = rights.astype(bf16)
    low = (rights - high.astype(np.float32)).astype(bf16)
    return np.concatenate([high, low, high], 2), chains


def split(value):
    high = value.astype(bf16)
    return high, (value - high.astype(f32)).astype(bf16)


def block_dot(value, matrix):
    rows, width = value.shape
    main = width // 256 * 256
    high, low = split(value)
    if not main or 2 * (width - main) > 256:
        return tall_dot(value, matrix)
    both = jnp.concatenate([high[:, :main], low[:, :main]], 0)
    both = lax.dot_general(both, matrix[:, :main], NT, preferred_element_type=f32)
    both = both[:rows] + both[rows:]
    if width == main:
        return both
    rest = jnp.concatenate([high[:, main:], low[:, main:]], 1)
    twice = jnp.concatenate([matrix[:, main:], matrix[:, main:]], 1)
    return both + lax.dot_general(rest, twice, NT, preferred_element_type=f32)


def tall_dot(value, matrix):
    rows = value.shape[0]
    both = lax.dot_general(jnp.concatenate(split(value), 0), matrix, NT, preferred_element_type=f32)
    return both[:rows] + both[rows:]


def chain_kernel(order, place, inverse_hbm, coupling_hbm, state, forcing, whole, middle, ends, last_ends, packed,
                 inverse, coupling, both, inverse_sem, coupling_sem):
    tiles, width, _ = inverse.shape
    local = state.shape[0]
    part = width // CORES
    rows = part + 2 * local
    half = tiles // 2
    runs = batches(tiles)

    def fetch(k):
        tile = order[k]
        return (
            pltpu.make_async_copy(coupling_hbm.at[tile], coupling.at[k], coupling_sem.at[k]),
            pltpu.make_async_copy(inverse_hbm.at[tile], inverse.at[k], inverse_sem.at[k]),
        )

    for k in range(tiles):
        for copy in fetch(k):
            copy.start()

    def with_terms(k, turned):
        tile = order[k]
        terms = [array[i, pl.ds(tile, 1), :] for array in (forcing, state) for i in range(local)]
        terms = jnp.concatenate(terms, 0)
        packed[tile] = terms
        return jnp.concatenate([-turned[:part], terms - turned[part:]], 0)

    def keep_first(out, offset):
        out[0] = both[:part]
        ends[offset : offset + 2 * local] = both[part:rows]

    def keep_second(out, offset):
        out[1] = both[rows : rows + part]
        ends[offset + 2 * local : offset + 4 * local] = both[rows + part :]

    ids = lax.broadcasted_iota(jnp.int32, (rows, width), 0)
    columns = lax.broadcasted_iota(jnp.int32, (rows, width), 1)
    first = jnp.where((ids < part) & (columns == ids + place[0] * part), 1.0, 0.0)
    second = None
    for k in range(tiles + 1):
        for j in range(k, runs.get(k, k)):
            for copy in fetch(j):
                copy.wait()
        ahead = with_terms(k, block_dot(first, coupling[k])) if k < tiles else None
        behind = None
        if k > 0:
            behind = first if k == 1 else first - block_dot(second, coupling[k - 1])
        if k < tiles:
            first = block_dot(ahead, inverse[k])
            both[:rows] = first
        if k > 0:
            second = block_dot(behind, inverse[k - 1])
            both[rows:] = second
        if k == half - 1:
            keep_first(middle, 4 * local)
        if k == half:
            keep_second(middle, 4 * local)
    keep_first(whole, 0)
    keep_second(whole, 0)
    last_ends[: 2 * local] = both[part:rows]
    last_ends[2 * local :] = both[rows + part :]


def chain(order, place, inverse, coupling, state, forcing):
    local, tiles, width = state.shape
    part = width // CORES
    half = jax.ShapeDtypeStruct((2, part, width), f32)
    return pl.pallas_call(
        chain_kernel,
        out_shape=(
            half,
            half,
            jax.ShapeDtypeStruct((8 * local, width), f32),
            jax.ShapeDtypeStruct((4 * local, width), f32),
            jax.ShapeDtypeStruct((tiles, 2 * local, width), f32),
        ),
        in_specs=[SMEM, SMEM, HBM, HBM, VMEM, VMEM],
        scratch_shapes=[
            pltpu.VMEM((tiles, width, width), bf16),
            pltpu.VMEM((tiles, width, width), bf16),
            pltpu.VMEM((2 * (part + 2 * local), width), f32),
            pltpu.SemaphoreType.DMA((tiles,)),
            pltpu.SemaphoreType.DMA((tiles,)),
        ],
        name="chain",
        compiler_params=params(60),
    )(order, place, inverse, coupling, state, forcing)


def right_kernel(place, table, *refs):
    blocks, out = refs[:-1], refs[-1]
    weights = table[place[2]]
    for tile in range(out.shape[0]):
        high, low = split(jnp.concatenate([block[tile] for block in blocks], 0))
        out[tile] = lax.dot_general(weights, jnp.concatenate([high, high, low], 0), NN, preferred_element_type=f32)


def right_sides(place, table, blocks):
    return pl.pallas_call(
        right_kernel,
        out_shape=jax.ShapeDtypeStruct(blocks[0].shape, f32),
        in_specs=[SMEM] + [VMEM] * (1 + len(blocks)),
        name="right_sides",
        compiler_params=params(12),
    )(place, table, *blocks)


def split_half(source, start, high, low):
    rows = source.shape[0]
    start = pl.multiple_of(start, 16)
    high[pl.ds(start, rows), :], low[pl.ds(start, rows), :] = split(source)


def times(value, high, low):
    upper, lower = split(value)
    rows = value.shape[0]
    both = lax.dot_general(jnp.concatenate([upper, lower], 0), high, NN, preferred_element_type=f32)
    return both[:rows] + both[rows:] + lax.dot_general(upper, low, NN, preferred_element_type=f32)


def carried(value, parts):
    rows = value.shape[0] // 2
    p_high, p_low, q_high, q_low = (parts[i] for i in range(4))
    moved = times(value, p_high, p_low)
    return jnp.concatenate([moved[:rows], moved[rows:] - times(value[:rows], q_high, q_low)], 0)


def prepare_kernel(place, mine, rest, out):
    rows = mine.shape[1]
    for i in range(2):
        split_half(mine[i], place[0] * rows, out.at[2 * i], out.at[2 * i + 1])
        split_half(rest[i], (1 - place[0]) * rows, out.at[2 * i], out.at[2 * i + 1])


def prepare(place, mine, rest, cost=0):
    width = mine.shape[2]
    return pl.pallas_call(
        prepare_kernel,
        out_shape=jax.ShapeDtypeStruct((4, width, width), bf16),
        in_specs=[SMEM, VMEM, VMEM],
        name="prepare",
        cost_estimate=pl.CostEstimate(flops=cost, bytes_accessed=0, transcendentals=0),
        compiler_params=params(12),
    )(place, mine, rest)


def mixed(weights, blocks, start, count):
    rows = jnp.concatenate([block[start : start + count] for block in blocks], 0)
    return jnp.dot(weights, rows, precision=lax.Precision.HIGHEST, preferred_element_type=f32)


def mix_kernel(place, table, *refs):
    blocks, outs = refs[:-2], refs[-2:]
    count = blocks[0].shape[0] // 2
    for i, out in enumerate(outs):
        out[...] = mixed(table[place[2]], blocks, i * count, count)


def mix_ends(place, table, blocks):
    shape = jax.ShapeDtypeStruct((table.shape[1], blocks[0].shape[1]), f32)
    return pl.pallas_call(
        mix_kernel,
        out_shape=(shape, shape),
        in_specs=[SMEM] + [VMEM] * (1 + len(blocks)),
        name="mix_ends",
        compiler_params=params(12),
    )(place, table, *blocks)


def pair_kernel(place, table, own, ends, *refs):
    blocks, (beside, total) = refs[:-2], refs[-2:]
    came = mixed(table[place[2]], blocks, 0, blocks[0].shape[0])
    beside[...] = came
    total[...] = ends[...]

    @pl.when(place[1] == 1)
    def _():
        total[...] = carried(came, own) + ends[...]


def pair_total(place, table, own, ends, blocks):
    shape = jax.ShapeDtypeStruct(ends.shape, f32)
    return pl.pallas_call(
        pair_kernel,
        out_shape=(shape, shape),
        in_specs=[SMEM] + [VMEM] * (3 + len(blocks)),
        name="pair_total",
        compiler_params=params(12),
    )(place, table, own, ends, *blocks)


def carry_kernel(pair, place, own, partner, ends, beside, *refs):
    arrivals, out = refs[:-1], refs[-1]
    out[...] = ends[...]

    @pl.when((place[1] == 1) & (place[3] == pair))
    def _():
        out[...] = carried(carried(arrivals[0][...], partner) + beside[...], own) + ends[...]

    @pl.when((place[1] == 0) & (place[3] == pair))
    def _():
        out[...] = carried(carried(arrivals[-1][...], own) + ends[...], partner) + beside[...]


def carry(pair, place, own, partner, ends, beside, arrivals):
    return pl.pallas_call(
        functools.partial(carry_kernel, pair),
        out_shape=jax.ShapeDtypeStruct(ends.shape, f32),
        in_specs=[SMEM] + [VMEM] * (4 + len(arrivals)),
        name="carry",
        compiler_params=params(12),
    )(place, own, partner, ends, beside, *arrivals)


def sweep_kernel(order, place, inverse, coupling, right, state, partner, beside, middle, middle_ends, *refs):
    arrivals, (out, at_group) = refs[:-2], refs[-2:]
    tiles, width, _ = inverse.shape
    local = state.shape[0]
    half = tiles // 2
    core, upper = place[0], place[1]

    inflow = jnp.zeros(at_group.shape, f32)
    for i, arrived in enumerate(arrivals[1:]):
        inflow = jnp.where(place[3] == i + 1, arrived[...], inflow)
    if arrivals:
        inflow = jnp.where((place[3] == 1) & (upper == 1), arrivals[0][...], inflow)
    at_group[...] = inflow

    @pl.when(upper == 1)
    def _():
        at_group[...] = carried(inflow, partner) + beside[...]

    starts = [at_group[...]]
    starts.append(carried(starts[0], middle) + middle_ends[...])
    a = [start[:local] for start in starts]
    w = [start[local:] for start in starts]
    for k in range(half):
        steps = [order[k], order[k + half]]
        here = [right[tile] for tile in steps]
        turned = [tall_dot(jnp.concatenate([a[s], w[s]], 0), coupling[tile]) for s, tile in enumerate(steps)]
        a = [tall_dot(here[s][:local] - turned[s][:local], inverse[tile]) for s, tile in enumerate(steps)]
        w = [tall_dot(here[s][local:] - a[s] - turned[s][local:], inverse[tile]) for s, tile in enumerate(steps)]
        for s, tile in enumerate(steps):
            for i in range(local):
                out[i, pl.ds(tile, 1), :] = state[i, pl.ds(tile, 1), :] + w[s][i : i + 1]


def sweep(order, place, inverse, coupling, right, state, *rest):
    local, _, width = state.shape
    return pl.pallas_call(
        sweep_kernel,
        out_shape=jax.ShapeDtypeStruct(state.shape, f32),
        in_specs=[SMEM, SMEM] + [VMEM] * (4 + len(rest)),
        scratch_shapes=[pltpu.VMEM((2 * local, width), f32)],
        name="sweep",
        compiler_params=params(24),
    )(order, place, inverse, coupling, right, state, *rest)


def after(value, *others):
    return lax.optimization_barrier((value, *others))[0]


def on_device(state, forcing, inverse, coupling, order):
    local, tiles, width = state.shape
    groups = lax.axis_size("axial")
    devices = lax.axis_size("inst")
    me, group = lax.axis_index("inst"), lax.axis_index("axial")
    place = jnp.stack([me % CORES, group % 2, me, group // 2]).astype(jnp.int32)
    right_table, chain_table = mixing_tables(devices, local)

    def over_inst(value, bit):
        return lax.ppermute(value, "inst", [(i, i ^ bit) for i in range(devices)])

    def over_pair(value):
        return lax.ppermute(value, "axial", [(g, g ^ 1) for g in range(groups)])

    def swapped(value, source, target):
        if groups & (groups - 1):
            return lax.ppermute(value, "axial", [(source, target)])
        return lax.ppermute(value, "axial", [(g, g ^ source ^ target) for g in range(groups)])

    def with_rest(value):
        return [value, over_inst(value, 1)]

    whole, middle, ends, last_ends, packed = chain(order, place, inverse, coupling, state, forcing)
    chain_table = jnp.asarray(chain_table)

    beside = over_pair(last_ends)
    blocks = [over_inst(ends, s) for s in range(1, devices)]
    partner = over_pair(whole)
    own = prepare(place, *with_rest(whole), 5 * 10**9)
    ends, middle_ends = mix_ends(place, chain_table, [ends] + blocks)
    beside = after(beside, ends)
    blocks = [beside] + [over_inst(beside, s) for s in range(1, devices)]
    packed, middle = after(packed, ends), after(middle, ends)
    packs = [packed] + [over_inst(packed, s) for s in range(CORES, devices, CORES)]
    middle = with_rest(middle)
    beside, total = pair_total(place, chain_table, own, ends, blocks)
    middle = prepare(place, after(middle[0], total), middle[1], 5 * 10**9)
    partner = prepare(place, *with_rest(after(partner, total)))

    arrivals = []
    if groups > 2:
        arrivals = [swapped(total, 1, 3), swapped(total, 1, 2)]
        arrivals[0] = after(arrivals[0], middle, *packs[1:])
    leaving = total
    for pair in range(1, groups // 2 - 1):
        came = arrivals if pair == 1 else arrivals[-1:]
        leaving = carry(pair, place, own, partner, ends, beside, came)
        arrivals.append(swapped(leaving, 2 * pair, 2 * pair + 2))
        if pair == 1:
            packs = [after(pack, leaving) for pack in packs]
    packs = [block for pack in packs for block in (pack, over_inst(pack, 1))]
    right = right_sides(place, jnp.asarray(right_table), packs)
    if arrivals:
        arrivals[-1] = after(arrivals[-1], right)
    return sweep(order, place, inverse, coupling, right, state, partner, beside, middle, middle_ends, *arrivals)


def solution(mesh):
    return jax.shard_map(
        on_device,
        mesh=mesh,
        in_specs=(
            P("inst", "axial", None),
            P("inst", "axial", None),
            P("axial", None, None),
            P("axial", None, None),
            P("axial"),
        ),
        out_specs=P("inst", "axial", None),
        check_vma=False,
    )
```

```python
import functools

import jax
import jax.numpy as jnp
import numpy as np
from jax import lax
from jax.experimental import pallas as pl
from jax.experimental.pallas import tpu as pltpu
from jax.sharding import PartitionSpec as P

NT = (((1,), (1,)), ((), ()))
NN = (((1,), (0,)), ((), ()))
bf16 = jnp.bfloat16
f32 = jnp.float32
SMEM = pl.BlockSpec(memory_space=pltpu.SMEM)
VMEM = pl.BlockSpec(memory_space=pltpu.VMEM)
HBM = pl.BlockSpec(memory_space=pltpu.HBM)
CORES = 2


def params(mebibytes):
    return pltpu.CompilerParams(vmem_limit_bytes=mebibytes << 20)


def batches(count):
    edges = [0]
    while edges[-1] < count:
        edges.append(min(count, max(1, 2 * edges[-1])))
    return dict(zip(edges, edges[1:]))


def mixing(period):
    distance = np.arange(period)[:, None] - np.arange(period)[None, :]
    angles = np.pi * distance / period
    sine = np.where(distance == 0, 1.0, np.sin(angles))
    parity = 1.0 - 2.0 * (distance % 2)
    derivative = np.where(distance == 0, 0.0, 0.5 * parity * np.cos(angles) / sine)
    mix = derivative * (2.0 / period) + np.eye(period)
    return mix, mix @ mix


def mixing_tables(devices, local):
    period = devices * local
    mix, twice = mixing(period)
    eye, none = np.eye(period), np.zeros((period, period))
    rights, chains = [], []
    for i in range(devices):
        rows = np.arange(local) + i * local
        right, chain = [], []
        for s in range(devices):
            columns = np.arange(local) + (i ^ s) * local
            cut = lambda upper, lower: np.concatenate([upper[rows][:, columns], lower[rows][:, columns]], 0)
            right += [cut(mix, 2 * eye), cut(-twice, -2 * mix)]
            chain += [cut(mix, 2 * eye), cut(-twice, -2 * mix), cut(none, -mix), cut(none, twice)]
        rights.append(np.concatenate(right, 1))
        chains.append(np.concatenate(chain, 1))
    rights, chains = np.stack(rights).astype(np.float32), np.stack(chains).astype(np.float32)
    high = rights.astype(bf16)
    low = (rights - high.astype(np.float32)).astype(bf16)
    return np.concatenate([high, low, high], 2), chains


def split(value):
    high = value.astype(bf16)
    return high, (value - high.astype(f32)).astype(bf16)


def block_dot(value, matrix):
    rows, width = value.shape
    main = width // 256 * 256
    high, low = split(value)
    if not main or 2 * (width - main) > 256:
        return tall_dot(value, matrix)
    both = jnp.concatenate([high[:, :main], low[:, :main]], 0)
    both = lax.dot_general(both, matrix[:, :main], NT, preferred_element_type=f32)
    both = both[:rows] + both[rows:]
    if width == main:
        return both
    rest = jnp.concatenate([high[:, main:], low[:, main:]], 1)
    twice = jnp.concatenate([matrix[:, main:], matrix[:, main:]], 1)
    return both + lax.dot_general(rest, twice, NT, preferred_element_type=f32)


def tall_dot(value, matrix):
    rows = value.shape[0]
    both = lax.dot_general(jnp.concatenate(split(value), 0), matrix, NT, preferred_element_type=f32)
    return both[:rows] + both[rows:]


def chain_kernel(order, place, inverse_hbm, coupling_hbm, state, forcing, whole, middle, ends, last_ends, packed,
                 inverse, coupling, both, inverse_sem, coupling_sem):
    tiles, width, _ = inverse.shape
    local = state.shape[0]
    part = width // CORES
    rows = part + 2 * local
    half = tiles // 2
    runs = batches(tiles)

    def fetch(k):
        tile = order[k]
        return (
            pltpu.make_async_copy(coupling_hbm.at[tile], coupling.at[k], coupling_sem.at[k]),
            pltpu.make_async_copy(inverse_hbm.at[tile], inverse.at[k], inverse_sem.at[k]),
        )

    for k in range(tiles):
        for copy in fetch(k):
            copy.start()

    def with_terms(k, turned):
        tile = order[k]
        terms = [array[i, pl.ds(tile, 1), :] for array in (forcing, state) for i in range(local)]
        terms = jnp.concatenate(terms, 0)
        packed[tile] = terms
        return jnp.concatenate([-turned[:part], terms - turned[part:]], 0)

    def keep_first(out, offset):
        out[0] = both[:part]
        ends[offset : offset + 2 * local] = both[part:rows]

    def keep_second(out, offset):
        out[1] = both[rows : rows + part]
        ends[offset + 2 * local : offset + 4 * local] = both[rows + part :]

    ids = lax.broadcasted_iota(jnp.int32, (rows, width), 0)
    columns = lax.broadcasted_iota(jnp.int32, (rows, width), 1)
    first = jnp.where((ids < part) & (columns == ids + place[0] * part), 1.0, 0.0)
    second = None
    for k in range(tiles + 1):
        for j in range(k, runs.get(k, k)):
            for copy in fetch(j):
                copy.wait()
        ahead = with_terms(k, block_dot(first, coupling[k])) if k < tiles else None
        behind = None
        if k > 0:
            behind = first if k == 1 else first - block_dot(second, coupling[k - 1])
        if k < tiles:
            first = block_dot(ahead, inverse[k])
            both[:rows] = first
        if k > 0:
            second = block_dot(behind, inverse[k - 1])
            both[rows:] = second
        if k == half - 1:
            keep_first(middle, 4 * local)
        if k == half:
            keep_second(middle, 4 * local)
    keep_first(whole, 0)
    keep_second(whole, 0)
    last_ends[: 2 * local] = both[part:rows]
    last_ends[2 * local :] = both[rows + part :]


def chain(order, place, inverse, coupling, state, forcing):
    local, tiles, width = state.shape
    part = width // CORES
    half = jax.ShapeDtypeStruct((2, part, width), f32)
    return pl.pallas_call(
        chain_kernel,
        out_shape=(
            half,
            half,
            jax.ShapeDtypeStruct((8 * local, width), f32),
            jax.ShapeDtypeStruct((4 * local, width), f32),
            jax.ShapeDtypeStruct((tiles, 2 * local, width), f32),
        ),
        in_specs=[SMEM, SMEM, HBM, HBM, VMEM, VMEM],
        scratch_shapes=[
            pltpu.VMEM((tiles, width, width), bf16),
            pltpu.VMEM((tiles, width, width), bf16),
            pltpu.VMEM((2 * (part + 2 * local), width), f32),
            pltpu.SemaphoreType.DMA((tiles,)),
            pltpu.SemaphoreType.DMA((tiles,)),
        ],
        name="chain",
        compiler_params=params(60),
    )(order, place, inverse, coupling, state, forcing)


def right_kernel(place, table, *refs):
    blocks, out = refs[:-1], refs[-1]
    weights = table[place[2]]
    for tile in range(out.shape[0]):
        high, low = split(jnp.concatenate([block[tile] for block in blocks], 0))
        out[tile] = lax.dot_general(weights, jnp.concatenate([high, high, low], 0), NN, preferred_element_type=f32)


def right_sides(place, table, blocks):
    return pl.pallas_call(
        right_kernel,
        out_shape=jax.ShapeDtypeStruct(blocks[0].shape, f32),
        in_specs=[SMEM] + [VMEM] * (1 + len(blocks)),
        name="right_sides",
        compiler_params=params(12),
    )(place, table, *blocks)


def split_half(source, start, high, low):
    rows = source.shape[0]
    start = pl.multiple_of(start, 16)
    high[pl.ds(start, rows), :], low[pl.ds(start, rows), :] = split(source)


def times(value, high, low):
    upper, lower = split(value)
    rows = value.shape[0]
    both = lax.dot_general(jnp.concatenate([upper, lower], 0), high, NN, preferred_element_type=f32)
    return both[:rows] + both[rows:] + lax.dot_general(upper, low, NN, preferred_element_type=f32)


def carried(value, parts):
    rows = value.shape[0] // 2
    p_high, p_low, q_high, q_low = (parts[i] for i in range(4))
    moved = times(value, p_high, p_low)
    return jnp.concatenate([moved[:rows], moved[rows:] - times(value[:rows], q_high, q_low)], 0)


def prepare_kernel(place, mine, rest, out):
    rows = mine.shape[1]
    for i in range(2):
        split_half(mine[i], place[0] * rows, out.at[2 * i], out.at[2 * i + 1])
        split_half(rest[i], (1 - place[0]) * rows, out.at[2 * i], out.at[2 * i + 1])


def prepare(place, mine, rest, cost=0):
    width = mine.shape[2]
    return pl.pallas_call(
        prepare_kernel,
        out_shape=jax.ShapeDtypeStruct((4, width, width), bf16),
        in_specs=[SMEM, VMEM, VMEM],
        name="prepare",
        cost_estimate=pl.CostEstimate(flops=cost, bytes_accessed=0, transcendentals=0),
        compiler_params=params(12),
    )(place, mine, rest)


def mixed(weights, blocks, start, count):
    rows = jnp.concatenate([block[start : start + count] for block in blocks], 0)
    return jnp.dot(weights, rows, precision=lax.Precision.HIGHEST, preferred_element_type=f32)


def mix_kernel(place, table, *refs):
    blocks, outs = refs[:-2], refs[-2:]
    count = blocks[0].shape[0] // 2
    for i, out in enumerate(outs):
        out[...] = mixed(table[place[2]], blocks, i * count, count)


def mix_ends(place, table, blocks):
    shape = jax.ShapeDtypeStruct((table.shape[1], blocks[0].shape[1]), f32)
    return pl.pallas_call(
        mix_kernel,
        out_shape=(shape, shape),
        in_specs=[SMEM] + [VMEM] * (1 + len(blocks)),
        name="mix_ends",
        compiler_params=params(12),
    )(place, table, *blocks)


def pair_kernel(place, table, own, ends, *refs):
    blocks, (beside, total) = refs[:-2], refs[-2:]
    came = mixed(table[place[2]], blocks, 0, blocks[0].shape[0])
    beside[...] = came
    total[...] = ends[...]

    @pl.when(place[1] == 1)
    def _():
        total[...] = carried(came, own) + ends[...]


def pair_total(place, table, own, ends, blocks):
    shape = jax.ShapeDtypeStruct(ends.shape, f32)
    return pl.pallas_call(
        pair_kernel,
        out_shape=(shape, shape),
        in_specs=[SMEM] + [VMEM] * (3 + len(blocks)),
        name="pair_total",
        compiler_params=params(12),
    )(place, table, own, ends, *blocks)


def carry_kernel(pair, place, own, partner, ends, beside, *refs):
    arrivals, out = refs[:-1], refs[-1]
    out[...] = ends[...]

    @pl.when((place[1] == 1) & (place[3] == pair))
    def _():
        out[...] = carried(carried(arrivals[0][...], partner) + beside[...], own) + ends[...]

    @pl.when((place[1] == 0) & (place[3] == pair))
    def _():
        out[...] = carried(carried(arrivals[-1][...], own) + ends[...], partner) + beside[...]


def carry(pair, place, own, partner, ends, beside, arrivals):
    return pl.pallas_call(
        functools.partial(carry_kernel, pair),
        out_shape=jax.ShapeDtypeStruct(ends.shape, f32),
        in_specs=[SMEM] + [VMEM] * (4 + len(arrivals)),
        name="carry",
        compiler_params=params(12),
    )(place, own, partner, ends, beside, *arrivals)


def sweep_kernel(order, place, inverse, coupling, right, state, partner, beside, middle, middle_ends, *refs):
    arrivals, (out, at_group) = refs[:-2], refs[-2:]
    tiles, width, _ = inverse.shape
    local = state.shape[0]
    half = tiles // 2
    core, upper = place[0], place[1]

    inflow = jnp.zeros(at_group.shape, f32)
    for i, arrived in enumerate(arrivals[1:]):
        inflow = jnp.where(place[3] == i + 1, arrived[...], inflow)
    if arrivals:
        inflow = jnp.where((place[3] == 1) & (upper == 1), arrivals[0][...], inflow)
    at_group[...] = inflow

    @pl.when(upper == 1)
    def _():
        at_group[...] = carried(inflow, partner) + beside[...]

    starts = [at_group[...]]
    starts.append(carried(starts[0], middle) + middle_ends[...])
    a = [start[:local] for start in starts]
    w = [start[local:] for start in starts]
    for k in range(half):
        steps = [order[k], order[k + half]]
        here = [right[tile] for tile in steps]
        turned = [tall_dot(jnp.concatenate([a[s], w[s]], 0), coupling[tile]) for s, tile in enumerate(steps)]
        a = [tall_dot(here[s][:local] - turned[s][:local], inverse[tile]) for s, tile in enumerate(steps)]
        w = [tall_dot(here[s][local:] - a[s] - turned[s][local:], inverse[tile]) for s, tile in enumerate(steps)]
        for s, tile in enumerate(steps):
            for i in range(local):
                out[i, pl.ds(tile, 1), :] = state[i, pl.ds(tile, 1), :] + w[s][i : i + 1]


def sweep(order, place, inverse, coupling, right, state, *rest):
    local, _, width = state.shape
    return pl.pallas_call(
        sweep_kernel,
        out_shape=jax.ShapeDtypeStruct(state.shape, f32),
        in_specs=[SMEM, SMEM] + [VMEM] * (4 + len(rest)),
        scratch_shapes=[pltpu.VMEM((2 * local, width), f32)],
        name="sweep",
        compiler_params=params(24),
    )(order, place, inverse, coupling, right, state, *rest)


def after(value, *others):
    return lax.optimization_barrier((value, *others))[0]


def on_device(state, forcing, inverse, coupling, order):
    local, tiles, width = state.shape
    groups = lax.axis_size("axial")
    devices = lax.axis_size("inst")
    me, group = lax.axis_index("inst"), lax.axis_index("axial")
    place = jnp.stack([me % CORES, group % 2, me, group // 2]).astype(jnp.int32)
    right_table, chain_table = mixing_tables(devices, local)

    def over_inst(value, bit):
        return lax.ppermute(value, "inst", [(i, i ^ bit) for i in range(devices)])

    def over_pair(value):
        return lax.ppermute(value, "axial", [(g, g ^ 1) for g in range(groups)])

    def swapped(value, source, target):
        if groups & (groups - 1):
            return lax.ppermute(value, "axial", [(source, target)])
        return lax.ppermute(value, "axial", [(g, g ^ source ^ target) for g in range(groups)])

    def with_rest(value):
        return [value, over_inst(value, 1)]

    whole, middle, ends, last_ends, packed = chain(order, place, inverse, coupling, state, forcing)
    chain_table = jnp.asarray(chain_table)

    beside = over_pair(last_ends)
    blocks = [over_inst(ends, s) for s in range(1, devices)]
    first_block = blocks[0]
    partner = over_pair(whole)
    own = prepare(place, *with_rest(whole), 5 * 10**9)
    ends, middle_ends = mix_ends(place, chain_table, [ends] + blocks)
    beside = after(beside, blocks[0])
    blocks = [beside] + [over_inst(beside, s) for s in range(1, devices)]
    packed, middle = after(packed, first_block), after(middle, ends)
    packs = [packed] + [over_inst(packed, s) for s in range(CORES, devices, CORES)]
    middle = with_rest(middle)
    beside, total = pair_total(place, chain_table, own, ends, blocks)
    middle = prepare(place, after(middle[0], total), middle[1], 5 * 10**9)
    partner = prepare(place, *with_rest(after(partner, total)))

    arrivals = []
    if groups > 2:
        arrivals = [swapped(total, 1, 3), swapped(total, 1, 2)]
        arrivals[0] = after(arrivals[0], middle)
    leaving = total
    for pair in range(1, groups // 2 - 1):
        came = arrivals if pair == 1 else arrivals[-1:]
        leaving = carry(pair, place, own, partner, ends, beside, came)
        arrivals.append(swapped(leaving, 2 * pair, 2 * pair + 2))
        if pair == 1:
            packs = [after(pack, leaving) for pack in packs]
    packs = [block for pack in packs for block in (pack, over_inst(pack, 1))]
    right = right_sides(place, jnp.asarray(right_table), packs)
    if arrivals:
        arrivals[-1] = after(arrivals[-1], right)
    return sweep(order, place, inverse, coupling, right, state, partner, beside, middle, middle_ends, *arrivals)


def solution(mesh):
    return jax.shard_map(
        on_device,
        mesh=mesh,
        in_specs=(
            P("inst", "axial", None),
            P("inst", "axial", None),
            P("axial", None, None),
            P("axial", None, None),
            P("axial"),
        ),
        out_specs=P("inst", "axial", None),
        check_vma=False,
    )
```

```python
import functools

import jax
import jax.numpy as jnp
import numpy as np
from jax import lax
from jax.experimental import pallas as pl
from jax.experimental.pallas import tpu as pltpu
from jax.sharding import PartitionSpec as P

NT = (((1,), (1,)), ((), ()))
NN = (((1,), (0,)), ((), ()))
bf16 = jnp.bfloat16
f32 = jnp.float32
SMEM = pl.BlockSpec(memory_space=pltpu.SMEM)
VMEM = pl.BlockSpec(memory_space=pltpu.VMEM)
HBM = pl.BlockSpec(memory_space=pltpu.HBM)
CORES = 2


def params(mebibytes):
    return pltpu.CompilerParams(vmem_limit_bytes=mebibytes << 20)


def whereabouts():
    me, group = lax.axis_index("inst"), lax.axis_index("axial")
    return me % CORES, group % 2, me, group // 2


def batches(count):
    edges = [0]
    while edges[-1] < count:
        edges.append(min(count, max(1, 2 * edges[-1])))
    return dict(zip(edges, edges[1:]))


def mixing(period):
    distance = np.arange(period)[:, None] - np.arange(period)[None, :]
    angles = np.pi * distance / period
    sine = np.where(distance == 0, 1.0, np.sin(angles))
    parity = 1.0 - 2.0 * (distance % 2)
    derivative = np.where(distance == 0, 0.0, 0.5 * parity * np.cos(angles) / sine)
    mix = derivative * (2.0 / period) + np.eye(period)
    return mix, mix @ mix


def mixing_tables(devices, local):
    period = devices * local
    mix, twice = mixing(period)
    eye, none = np.eye(period), np.zeros((period, period))
    rights, chains = [], []
    for i in range(devices):
        rows = np.arange(local) + i * local
        right, chain = [], []
        for s in range(devices):
            columns = np.arange(local) + (i ^ s) * local
            cut = lambda upper, lower: np.concatenate([upper[rows][:, columns], lower[rows][:, columns]], 0)
            right += [cut(mix, 2 * eye), cut(-twice, -2 * mix)]
            chain += [cut(mix, 2 * eye), cut(-twice, -2 * mix), cut(none, -mix), cut(none, twice)]
        rights.append(np.concatenate(right, 1))
        chains.append(np.concatenate(chain, 1))
    rights, chains = np.stack(rights).astype(np.float32), np.stack(chains).astype(np.float32)
    high = rights.astype(bf16)
    low = (rights - high.astype(np.float32)).astype(bf16)
    return np.concatenate([high, low, high], 2), chains


def split(value):
    high = value.astype(bf16)
    return high, (value - high.astype(f32)).astype(bf16)


def block_dot(value, matrix):
    rows, width = value.shape
    main = width // 256 * 256
    high, low = split(value)
    if not main or 2 * (width - main) > 256:
        return tall_dot(value, matrix)
    both = jnp.concatenate([high[:, :main], low[:, :main]], 0)
    both = lax.dot_general(both, matrix[:, :main], NT, preferred_element_type=f32)
    both = both[:rows] + both[rows:]
    if width == main:
        return both
    rest = jnp.concatenate([high[:, main:], low[:, main:]], 1)
    twice = jnp.concatenate([matrix[:, main:], matrix[:, main:]], 1)
    return both + lax.dot_general(rest, twice, NT, preferred_element_type=f32)


def tall_dot(value, matrix):
    rows = value.shape[0]
    both = lax.dot_general(jnp.concatenate(split(value), 0), matrix, NT, preferred_element_type=f32)
    return both[:rows] + both[rows:]


def chain_kernel(order, inverse_hbm, coupling_hbm, state_hbm, forcing_hbm, whole, middle, ends, last_ends, packed,
                 inverse, coupling, state, forcing, both, inverse_sem, coupling_sem, extra_sem):
    place = whereabouts()
    tiles, width, _ = inverse.shape
    local = state.shape[0]
    part = width // CORES
    rows = part + 2 * local
    half = tiles // 2
    runs = batches(tiles)

    def fetch(k):
        tile = order[k]
        return (
            pltpu.make_async_copy(coupling_hbm.at[tile], coupling.at[k], coupling_sem.at[k]),
            pltpu.make_async_copy(inverse_hbm.at[tile], inverse.at[k], inverse_sem.at[k]),
        )

    extras = (
        pltpu.make_async_copy(state_hbm, state, extra_sem.at[0]),
        pltpu.make_async_copy(forcing_hbm, forcing, extra_sem.at[1]),
    )
    for copy in fetch(0) + extras:
        copy.start()
    for k in range(1, tiles):
        for copy in fetch(k):
            copy.start()

    def with_terms(k, turned):
        tile = order[k]
        terms = [array[i, pl.ds(tile, 1), :] for array in (forcing, state) for i in range(local)]
        terms = jnp.concatenate(terms, 0)
        packed[tile] = terms
        return jnp.concatenate([-turned[:part], terms - turned[part:]], 0)

    def keep_first(out, offset):
        out[0] = both[:part]
        ends[offset : offset + 2 * local] = both[part:rows]

    def keep_second(out, offset):
        out[1] = both[rows : rows + part]
        ends[offset + 2 * local : offset + 4 * local] = both[rows + part :]

    ids = lax.broadcasted_iota(jnp.int32, (rows, width), 0)
    columns = lax.broadcasted_iota(jnp.int32, (rows, width), 1)
    first = jnp.where((ids < part) & (columns == ids + place[0] * part), 1.0, 0.0)
    second = None
    for k in range(tiles + 1):
        for j in range(k, runs.get(k, k)):
            for copy in fetch(j) + (() if j else extras):
                copy.wait()
        ahead = with_terms(k, block_dot(first, coupling[k])) if k < tiles else None
        behind = None
        if k > 0:
            behind = first if k == 1 else first - block_dot(second, coupling[k - 1])
        if k < tiles:
            first = block_dot(ahead, inverse[k])
            both[:rows] = first
        if k > 0:
            second = block_dot(behind, inverse[k - 1])
            both[rows:] = second
        if k == half - 1:
            keep_first(middle, 4 * local)
        if k == half:
            keep_second(middle, 4 * local)
    keep_first(whole, 0)
    keep_second(whole, 0)
    last_ends[: 2 * local] = both[part:rows]
    last_ends[2 * local :] = both[rows + part :]


def chain(order, inverse, coupling, state, forcing):
    local, tiles, width = state.shape
    part = width // CORES
    half = jax.ShapeDtypeStruct((2, part, width), f32)
    return pl.pallas_call(
        chain_kernel,
        out_shape=(
            half,
            half,
            jax.ShapeDtypeStruct((8 * local, width), f32),
            jax.ShapeDtypeStruct((4 * local, width), f32),
            jax.ShapeDtypeStruct((tiles, 2 * local, width), f32),
        ),
        in_specs=[SMEM, HBM, HBM, HBM, HBM],
        scratch_shapes=[
            pltpu.VMEM((tiles, width, width), bf16),
            pltpu.VMEM((tiles, width, width), bf16),
            pltpu.VMEM((local, tiles, width), f32),
            pltpu.VMEM((local, tiles, width), f32),
            pltpu.VMEM((2 * (part + 2 * local), width), f32),
            pltpu.SemaphoreType.DMA((tiles,)),
            pltpu.SemaphoreType.DMA((tiles,)),
            pltpu.SemaphoreType.DMA((2,)),
        ],
        name="chain",
        compiler_params=params(60),
    )(order, inverse, coupling, state, forcing)


def right_kernel(table, *refs):
    place = whereabouts()
    blocks, out = refs[:-1], refs[-1]
    weights = table[place[2]]
    for tile in range(out.shape[0]):
        high, low = split(jnp.concatenate([block[tile] for block in blocks], 0))
        out[tile] = lax.dot_general(weights, jnp.concatenate([high, high, low], 0), NN, preferred_element_type=f32)


def right_sides(table, blocks):
    return pl.pallas_call(
        right_kernel,
        out_shape=jax.ShapeDtypeStruct(blocks[0].shape, f32),
        in_specs=[VMEM] * (1 + len(blocks)),
        name="right_sides",
        compiler_params=params(12),
    )(table, *blocks)


def split_half(source, start, high, low):
    rows = source.shape[0]
    start = pl.multiple_of(start, 16)
    high[pl.ds(start, rows), :], low[pl.ds(start, rows), :] = split(source)


def times(value, high, low):
    upper, lower = split(value)
    rows = value.shape[0]
    both = lax.dot_general(jnp.concatenate([upper, lower], 0), high, NN, preferred_element_type=f32)
    return both[:rows] + both[rows:] + lax.dot_general(upper, low, NN, preferred_element_type=f32)


def carried(value, parts):
    rows = value.shape[0] // 2
    p_high, p_low, q_high, q_low = (parts[i] for i in range(4))
    moved = times(value, p_high, p_low)
    return jnp.concatenate([moved[:rows], moved[rows:] - times(value[:rows], q_high, q_low)], 0)


def prepare_kernel(mine, rest, out):
    place = whereabouts()
    rows = mine.shape[1]
    for i in range(2):
        split_half(mine[i], place[0] * rows, out.at[2 * i], out.at[2 * i + 1])
        split_half(rest[i], (1 - place[0]) * rows, out.at[2 * i], out.at[2 * i + 1])


def prepare(mine, rest, cost=0):
    width = mine.shape[2]
    return pl.pallas_call(
        prepare_kernel,
        out_shape=jax.ShapeDtypeStruct((4, width, width), bf16),
        in_specs=[VMEM, VMEM],
        name="prepare",
        cost_estimate=pl.CostEstimate(flops=cost, bytes_accessed=0, transcendentals=0),
        compiler_params=params(12),
    )(mine, rest)


def mixed(weights, blocks, start, count):
    rows = jnp.concatenate([block[start : start + count] for block in blocks], 0)
    return jnp.dot(weights, rows, precision=lax.Precision.HIGHEST, preferred_element_type=f32)


def mix_kernel(table, *refs):
    place = whereabouts()
    blocks, outs = refs[:-2], refs[-2:]
    count = blocks[0].shape[0] // 2
    for i, out in enumerate(outs):
        out[...] = mixed(table[place[2]], blocks, i * count, count)


def mix_ends(table, blocks):
    shape = jax.ShapeDtypeStruct((table.shape[1], blocks[0].shape[1]), f32)
    return pl.pallas_call(
        mix_kernel,
        out_shape=(shape, shape),
        in_specs=[VMEM] * (1 + len(blocks)),
        name="mix_ends",
        compiler_params=params(12),
    )(table, *blocks)


def pair_kernel(table, own, ends, *refs):
    place = whereabouts()
    blocks, (beside, total) = refs[:-2], refs[-2:]
    came = mixed(table[place[2]], blocks, 0, blocks[0].shape[0])
    beside[...] = came
    total[...] = ends[...]

    @pl.when(place[1] == 1)
    def _():
        total[...] = carried(came, own) + ends[...]


def pair_total(table, own, ends, blocks):
    shape = jax.ShapeDtypeStruct(ends.shape, f32)
    return pl.pallas_call(
        pair_kernel,
        out_shape=(shape, shape),
        in_specs=[VMEM] * (3 + len(blocks)),
        name="pair_total",
        compiler_params=params(12),
    )(table, own, ends, *blocks)


def carry_kernel(pair, own, partner, ends, beside, *refs):
    place = whereabouts()
    arrivals, out = refs[:-1], refs[-1]
    out[...] = ends[...]

    @pl.when((place[1] == 1) & (place[3] == pair))
    def _():
        out[...] = carried(carried(arrivals[0][...], partner) + beside[...], own) + ends[...]

    @pl.when((place[1] == 0) & (place[3] == pair))
    def _():
        out[...] = carried(carried(arrivals[-1][...], own) + ends[...], partner) + beside[...]


def carry(pair, own, partner, ends, beside, arrivals):
    return pl.pallas_call(
        functools.partial(carry_kernel, pair),
        out_shape=jax.ShapeDtypeStruct(ends.shape, f32),
        in_specs=[VMEM] * (4 + len(arrivals)),
        name="carry",
        compiler_params=params(12),
    )(own, partner, ends, beside, *arrivals)


def sweep_kernel(order, inverse, coupling, right, state, partner, beside, middle, middle_ends, *refs):
    place = whereabouts()
    arrivals, (out, at_group) = refs[:-2], refs[-2:]
    tiles, width, _ = inverse.shape
    local = state.shape[0]
    half = tiles // 2
    core, upper = place[0], place[1]

    inflow = jnp.zeros(at_group.shape, f32)
    for i, arrived in enumerate(arrivals[1:]):
        inflow = jnp.where(place[3] == i + 1, arrived[...], inflow)
    if arrivals:
        inflow = jnp.where((place[3] == 1) & (upper == 1), arrivals[0][...], inflow)
    at_group[...] = inflow

    @pl.when(upper == 1)
    def _():
        at_group[...] = carried(inflow, partner) + beside[...]

    starts = [at_group[...]]
    starts.append(carried(starts[0], middle) + middle_ends[...])
    a = [start[:local] for start in starts]
    w = [start[local:] for start in starts]
    for k in range(half):
        steps = [order[k], order[k + half]]
        here = [right[tile] for tile in steps]
        turned = [tall_dot(jnp.concatenate([a[s], w[s]], 0), coupling[tile]) for s, tile in enumerate(steps)]
        a = [tall_dot(here[s][:local] - turned[s][:local], inverse[tile]) for s, tile in enumerate(steps)]
        w = [tall_dot(here[s][local:] - a[s] - turned[s][local:], inverse[tile]) for s, tile in enumerate(steps)]
        for s, tile in enumerate(steps):
            for i in range(local):
                out[i, pl.ds(tile, 1), :] = state[i, pl.ds(tile, 1), :] + w[s][i : i + 1]


def sweep(order, inverse, coupling, right, state, *rest):
    local, _, width = state.shape
    return pl.pallas_call(
        sweep_kernel,
        out_shape=jax.ShapeDtypeStruct(state.shape, f32),
        in_specs=[SMEM] + [VMEM] * (4 + len(rest)),
        scratch_shapes=[pltpu.VMEM((2 * local, width), f32)],
        name="sweep",
        compiler_params=params(24),
    )(order, inverse, coupling, right, state, *rest)


def after(value, *others):
    return lax.optimization_barrier((value, *others))[0]


def on_device(state, forcing, inverse, coupling, order):
    local, tiles, width = state.shape
    groups = lax.axis_size("axial")
    devices = lax.axis_size("inst")
    right_table, chain_table = mixing_tables(devices, local)

    def over_inst(value, bit):
        return lax.ppermute(value, "inst", [(i, i ^ bit) for i in range(devices)])

    def over_pair(value):
        return lax.ppermute(value, "axial", [(g, g ^ 1) for g in range(groups)])

    def swapped(value, source, target):
        if groups & (groups - 1):
            return lax.ppermute(value, "axial", [(source, target)])
        return lax.ppermute(value, "axial", [(g, g ^ source ^ target) for g in range(groups)])

    def with_rest(value):
        return [value, over_inst(value, 1)]

    whole, middle, ends, last_ends, packed = chain(order, inverse, coupling, state, forcing)
    chain_table = jnp.asarray(chain_table)

    beside = over_pair(last_ends)
    blocks = [over_inst(ends, s) for s in range(1, devices)]
    first_block = blocks[0]
    partner = over_pair(whole)
    own = prepare(*with_rest(whole), 5 * 10**9)
    ends, middle_ends = mix_ends(chain_table, [ends] + blocks)
    beside = after(beside, blocks[0])
    blocks = [beside] + [over_inst(beside, s) for s in range(1, devices)]
    packed, middle = after(packed, first_block), after(middle, ends)
    packs = [packed] + [over_inst(packed, s) for s in range(CORES, devices, CORES)]
    middle = with_rest(middle)
    beside, total = pair_total(chain_table, own, ends, blocks)
    middle = prepare(after(middle[0], total), middle[1], 5 * 10**9)
    partner = prepare(*with_rest(after(partner, total)))

    arrivals = []
    if groups > 2:
        arrivals = [swapped(total, 1, 3), swapped(total, 1, 2)]
        arrivals[0] = after(arrivals[0], middle)
    leaving = total
    for pair in range(1, groups // 2 - 1):
        came = arrivals if pair == 1 else arrivals[-1:]
        leaving = carry(pair, own, partner, ends, beside, came)
        arrivals.append(swapped(leaving, 2 * pair, 2 * pair + 2))
        if pair == 1:
            packs = [after(pack, leaving) for pack in packs]
    packs = [block for pack in packs for block in (pack, over_inst(pack, 1))]
    right = right_sides(jnp.asarray(right_table), packs)
    if arrivals:
        arrivals[-1] = after(arrivals[-1], right)
    return sweep(order, inverse, coupling, right, state, partner, beside, middle, middle_ends, *arrivals)


def solution(mesh):
    return jax.shard_map(
        on_device,
        mesh=mesh,
        in_specs=(
            P("inst", "axial", None),
            P("inst", "axial", None),
            P("axial", None, None),
            P("axial", None, None),
            P("axial"),
        ),
        out_specs=P("inst", "axial", None),
        check_vma=False,
    )
```

```python
import functools

import jax
import jax.numpy as jnp
import numpy as np
from jax import lax
from jax.experimental import pallas as pl
from jax.experimental.pallas import tpu as pltpu
from jax.sharding import PartitionSpec as P

NT = (((1,), (1,)), ((), ()))
NN = (((1,), (0,)), ((), ()))
bf16 = jnp.bfloat16
f32 = jnp.float32
SMEM = pl.BlockSpec(memory_space=pltpu.SMEM)
VMEM = pl.BlockSpec(memory_space=pltpu.VMEM)
HBM = pl.BlockSpec(memory_space=pltpu.HBM)
CORES = 2


def params(mebibytes):
    return pltpu.CompilerParams(vmem_limit_bytes=mebibytes << 20)


def whereabouts():
    me, group = lax.axis_index("inst"), lax.axis_index("axial")
    return me % CORES, group % 2, me, group // 2


def batches(count):
    edges = [0]
    while edges[-1] < count:
        edges.append(min(count, max(1, 2 * edges[-1])))
    return dict(zip(edges, edges[1:]))


def mixing(period):
    distance = np.arange(period)[:, None] - np.arange(period)[None, :]
    angles = np.pi * distance / period
    sine = np.where(distance == 0, 1.0, np.sin(angles))
    parity = 1.0 - 2.0 * (distance % 2)
    derivative = np.where(distance == 0, 0.0, 0.5 * parity * np.cos(angles) / sine)
    mix = derivative * (2.0 / period) + np.eye(period)
    return mix, mix @ mix


def mixing_tables(devices, local):
    period = devices * local
    mix, twice = mixing(period)
    eye, none = np.eye(period), np.zeros((period, period))
    rights, chains = [], []
    for i in range(devices):
        rows = np.arange(local) + i * local
        right, chain = [], []
        for s in range(devices):
            columns = np.arange(local) + (i ^ s) * local
            cut = lambda upper, lower: np.concatenate([upper[rows][:, columns], lower[rows][:, columns]], 0)
            right += [cut(mix, 2 * eye), cut(-twice, -2 * mix)]
            chain += [cut(mix, 2 * eye), cut(-twice, -2 * mix), cut(none, -mix), cut(none, twice)]
        rights.append(np.concatenate(right, 1))
        chains.append(np.concatenate(chain, 1))
    rights, chains = np.stack(rights).astype(np.float32), np.stack(chains).astype(np.float32)
    high = rights.astype(bf16)
    low = (rights - high.astype(np.float32)).astype(bf16)
    return np.concatenate([high, low, high], 2), chains


def split(value):
    high = value.astype(bf16)
    return high, (value - high.astype(f32)).astype(bf16)


def block_dot(value, matrix):
    rows, width = value.shape
    main = width // 256 * 256
    high, low = split(value)
    if not main or 2 * (width - main) > 256:
        return tall_dot(value, matrix)
    both = jnp.concatenate([high[:, :main], low[:, :main]], 0)
    both = lax.dot_general(both, matrix[:, :main], NT, preferred_element_type=f32)
    both = both[:rows] + both[rows:]
    if width == main:
        return both
    rest = jnp.concatenate([high[:, main:], low[:, main:]], 1)
    twice = jnp.concatenate([matrix[:, main:], matrix[:, main:]], 1)
    return both + lax.dot_general(rest, twice, NT, preferred_element_type=f32)


def tall_dot(value, matrix):
    rows = value.shape[0]
    both = lax.dot_general(jnp.concatenate(split(value), 0), matrix, NT, preferred_element_type=f32)
    return both[:rows] + both[rows:]


def chain_kernel(order, inverse_hbm, coupling_hbm, state, forcing, whole, middle, ends, last_ends, packed,
                 inverse, coupling, both, inverse_sem, coupling_sem):
    place = whereabouts()
    tiles, width, _ = inverse.shape
    local = state.shape[0]
    part = width // CORES
    rows = part + 2 * local
    half = tiles // 2
    runs = batches(tiles)

    def fetch(k):
        tile = order[k]
        return (
            pltpu.make_async_copy(coupling_hbm.at[tile], coupling.at[k], coupling_sem.at[k]),
            pltpu.make_async_copy(inverse_hbm.at[tile], inverse.at[k], inverse_sem.at[k]),
        )

    for k in range(tiles):
        for copy in fetch(k):
            copy.start()

    def with_terms(k, turned):
        tile = order[k]
        terms = [array[i, pl.ds(tile, 1), :] for array in (forcing, state) for i in range(local)]
        terms = jnp.concatenate(terms, 0)
        packed[tile] = terms
        return jnp.concatenate([-turned[:part], terms - turned[part:]], 0)

    def keep_first(out, offset):
        out[0] = both[:part]
        ends[offset : offset + 2 * local] = both[part:rows]

    def keep_second(out, offset):
        out[1] = both[rows : rows + part]
        ends[offset + 2 * local : offset + 4 * local] = both[rows + part :]

    ids = lax.broadcasted_iota(jnp.int32, (rows, width), 0)
    columns = lax.broadcasted_iota(jnp.int32, (rows, width), 1)
    first = jnp.where((ids < part) & (columns == ids + place[0] * part), 1.0, 0.0)
    second = None
    for k in range(tiles + 1):
        for j in range(k, runs.get(k, k)):
            for copy in fetch(j):
                copy.wait()
        ahead = with_terms(k, block_dot(first, coupling[k])) if k < tiles else None
        behind = None
        if k > 0:
            behind = first if k == 1 else first - block_dot(second, coupling[k - 1])
        if k < tiles:
            first = block_dot(ahead, inverse[k])
            both[:rows] = first
        if k > 0:
            second = block_dot(behind, inverse[k - 1])
            both[rows:] = second
        if k == half - 1:
            keep_first(middle, 4 * local)
        if k == half:
            keep_second(middle, 4 * local)
    keep_first(whole, 0)
    keep_second(whole, 0)
    last_ends[: 2 * local] = both[part:rows]
    last_ends[2 * local :] = both[rows + part :]


def chain(order, inverse, coupling, state, forcing):
    local, tiles, width = state.shape
    part = width // CORES
    half = jax.ShapeDtypeStruct((2, part, width), f32)
    return pl.pallas_call(
        chain_kernel,
        out_shape=(
            half,
            half,
            jax.ShapeDtypeStruct((8 * local, width), f32),
            jax.ShapeDtypeStruct((4 * local, width), f32),
            jax.ShapeDtypeStruct((tiles, 2 * local, width), f32),
        ),
        in_specs=[SMEM, HBM, HBM, VMEM, VMEM],
        scratch_shapes=[
            pltpu.VMEM((tiles, width, width), bf16),
            pltpu.VMEM((tiles, width, width), bf16),
            pltpu.VMEM((2 * (part + 2 * local), width), f32),
            pltpu.SemaphoreType.DMA((tiles,)),
            pltpu.SemaphoreType.DMA((tiles,)),
        ],
        name="chain",
        compiler_params=params(60),
    )(order, inverse, coupling, state, forcing)


def right_kernel(table, *refs):
    place = whereabouts()
    blocks, out = refs[:-1], refs[-1]
    weights = table[place[2]]
    for tile in range(out.shape[0]):
        high, low = split(jnp.concatenate([block[tile] for block in blocks], 0))
        out[tile] = lax.dot_general(weights, jnp.concatenate([high, high, low], 0), NN, preferred_element_type=f32)


def right_sides(table, blocks):
    return pl.pallas_call(
        right_kernel,
        out_shape=jax.ShapeDtypeStruct(blocks[0].shape, f32),
        in_specs=[VMEM] * (1 + len(blocks)),
        name="right_sides",
        compiler_params=params(12),
    )(table, *blocks)


def split_half(source, start, high, low):
    rows = source.shape[0]
    start = pl.multiple_of(start, 16)
    high[pl.ds(start, rows), :], low[pl.ds(start, rows), :] = split(source)


def times(value, high, low):
    upper, lower = split(value)
    rows = value.shape[0]
    both = lax.dot_general(jnp.concatenate([upper, lower], 0), high, NN, preferred_element_type=f32)
    return both[:rows] + both[rows:] + lax.dot_general(upper, low, NN, preferred_element_type=f32)


def carried(value, parts):
    rows = value.shape[0] // 2
    p_high, p_low, q_high, q_low = (parts[i] for i in range(4))
    moved = times(value, p_high, p_low)
    return jnp.concatenate([moved[:rows], moved[rows:] - times(value[:rows], q_high, q_low)], 0)


def prepare_kernel(mine, rest, out):
    place = whereabouts()
    rows = mine.shape[1]
    for i in range(2):
        split_half(mine[i], place[0] * rows, out.at[2 * i], out.at[2 * i + 1])
        split_half(rest[i], (1 - place[0]) * rows, out.at[2 * i], out.at[2 * i + 1])


def prepare(mine, rest, cost=0):
    width = mine.shape[2]
    return pl.pallas_call(
        prepare_kernel,
        out_shape=jax.ShapeDtypeStruct((4, width, width), bf16),
        in_specs=[VMEM, VMEM],
        name="prepare",
        cost_estimate=pl.CostEstimate(flops=cost, bytes_accessed=0, transcendentals=0),
        compiler_params=params(12),
    )(mine, rest)


def mixed(weights, blocks, start, count):
    rows = jnp.concatenate([block[start : start + count] for block in blocks], 0)
    return jnp.dot(weights, rows, precision=lax.Precision.HIGHEST, preferred_element_type=f32)


def mix_kernel(table, *refs):
    place = whereabouts()
    blocks, outs = refs[:-2], refs[-2:]
    count = blocks[0].shape[0] // 2
    for i, out in enumerate(outs):
        out[...] = mixed(table[place[2]], blocks, i * count, count)


def mix_ends(table, blocks):
    shape = jax.ShapeDtypeStruct((table.shape[1], blocks[0].shape[1]), f32)
    return pl.pallas_call(
        mix_kernel,
        out_shape=(shape, shape),
        in_specs=[VMEM] * (1 + len(blocks)),
        name="mix_ends",
        compiler_params=params(12),
    )(table, *blocks)


def pair_kernel(table, own, ends, *refs):
    place = whereabouts()
    blocks, (beside, total) = refs[:-2], refs[-2:]
    came = mixed(table[place[2]], blocks, 0, blocks[0].shape[0])
    beside[...] = came
    total[...] = ends[...]

    @pl.when(place[1] == 1)
    def _():
        total[...] = carried(came, own) + ends[...]


def pair_total(table, own, ends, blocks):
    shape = jax.ShapeDtypeStruct(ends.shape, f32)
    return pl.pallas_call(
        pair_kernel,
        out_shape=(shape, shape),
        in_specs=[VMEM] * (3 + len(blocks)),
        name="pair_total",
        compiler_params=params(12),
    )(table, own, ends, *blocks)


def carry_kernel(pair, own, partner, ends, beside, *refs):
    place = whereabouts()
    arrivals, out = refs[:-1], refs[-1]
    out[...] = ends[...]

    @pl.when((place[1] == 1) & (place[3] == pair))
    def _():
        out[...] = carried(carried(arrivals[0][...], partner) + beside[...], own) + ends[...]

    @pl.when((place[1] == 0) & (place[3] == pair))
    def _():
        out[...] = carried(carried(arrivals[-1][...], own) + ends[...], partner) + beside[...]


def carry(pair, own, partner, ends, beside, arrivals):
    return pl.pallas_call(
        functools.partial(carry_kernel, pair),
        out_shape=jax.ShapeDtypeStruct(ends.shape, f32),
        in_specs=[VMEM] * (4 + len(arrivals)),
        name="carry",
        compiler_params=params(12),
    )(own, partner, ends, beside, *arrivals)


def sweep_kernel(order, inverse, coupling, right, state, partner, beside, middle, middle_ends, *refs):
    place = whereabouts()
    arrivals, (out, at_group) = refs[:-2], refs[-2:]
    tiles, width, _ = inverse.shape
    local = state.shape[0]
    half = tiles // 2
    core, upper = place[0], place[1]

    inflow = jnp.zeros(at_group.shape, f32)
    for i, arrived in enumerate(arrivals[1:]):
        inflow = jnp.where(place[3] == i + 1, arrived[...], inflow)
    if arrivals:
        inflow = jnp.where((place[3] == 1) & (upper == 1), arrivals[0][...], inflow)
    at_group[...] = inflow

    @pl.when(upper == 1)
    def _():
        at_group[...] = carried(inflow, partner) + beside[...]

    starts = [at_group[...]]
    starts.append(carried(starts[0], middle) + middle_ends[...])
    a = [start[:local] for start in starts]
    w = [start[local:] for start in starts]
    for k in range(half):
        steps = [order[k], order[k + half]]
        here = [right[tile] for tile in steps]
        turned = [tall_dot(jnp.concatenate([a[s], w[s]], 0), coupling[tile]) for s, tile in enumerate(steps)]
        a = [tall_dot(here[s][:local] - turned[s][:local], inverse[tile]) for s, tile in enumerate(steps)]
        w = [tall_dot(here[s][local:] - a[s] - turned[s][local:], inverse[tile]) for s, tile in enumerate(steps)]
        for s, tile in enumerate(steps):
            for i in range(local):
                out[i, pl.ds(tile, 1), :] = state[i, pl.ds(tile, 1), :] + w[s][i : i + 1]


def sweep(order, inverse, coupling, right, state, *rest):
    local, _, width = state.shape
    return pl.pallas_call(
        sweep_kernel,
        out_shape=jax.ShapeDtypeStruct(state.shape, f32),
        in_specs=[SMEM] + [VMEM] * (4 + len(rest)),
        scratch_shapes=[pltpu.VMEM((2 * local, width), f32)],
        name="sweep",
        compiler_params=params(24),
    )(order, inverse, coupling, right, state, *rest)


def after(value, *others):
    return lax.optimization_barrier((value, *others))[0]


def on_device(state, forcing, inverse, coupling, order):
    local, tiles, width = state.shape
    groups = lax.axis_size("axial")
    devices = lax.axis_size("inst")
    right_table, chain_table = mixing_tables(devices, local)

    def over_inst(value, bit):
        return lax.ppermute(value, "inst", [(i, i ^ bit) for i in range(devices)])

    def over_pair(value):
        return lax.ppermute(value, "axial", [(g, g ^ 1) for g in range(groups)])

    def swapped(value, source, target):
        if groups & (groups - 1):
            return lax.ppermute(value, "axial", [(source, target)])
        return lax.ppermute(value, "axial", [(g, g ^ source ^ target) for g in range(groups)])

    def with_rest(value):
        return [value, over_inst(value, 1)]

    whole, middle, ends, last_ends, packed = chain(order, inverse, coupling, state, forcing)
    chain_table = jnp.asarray(chain_table)

    beside = over_pair(last_ends)
    blocks = [over_inst(ends, s) for s in range(1, devices)]
    first_block = blocks[0]
    partner = over_pair(whole)
    own = prepare(*with_rest(whole), 5 * 10**9)
    ends, middle_ends = mix_ends(chain_table, [ends] + blocks)
    beside = after(beside, blocks[0])
    blocks = [beside] + [over_inst(beside, s) for s in range(1, devices)]
    packed, middle = after(packed, first_block), after(middle, ends)
    packs = [packed] + [over_inst(packed, s) for s in range(CORES, devices, CORES)]
    middle = with_rest(middle)
    beside, total = pair_total(chain_table, own, ends, blocks)
    middle = prepare(after(middle[0], total), middle[1], 5 * 10**9)
    partner = prepare(*with_rest(after(partner, total)))

    arrivals = []
    if groups > 2:
        arrivals = [swapped(total, 1, 3), swapped(total, 1, 2)]
        arrivals[0] = after(arrivals[0], middle)
    leaving = total
    for pair in range(1, groups // 2 - 1):
        came = arrivals if pair == 1 else arrivals[-1:]
        leaving = carry(pair, own, partner, ends, beside, came)
        arrivals.append(swapped(leaving, 2 * pair, 2 * pair + 2))
        if pair == 1:
            packs = [after(pack, leaving) for pack in packs]
    packs = [block for pack in packs for block in (pack, over_inst(pack, 1))]
    right = right_sides(jnp.asarray(right_table), packs)
    if arrivals:
        arrivals[-1] = after(arrivals[-1], right)
    return sweep(order, inverse, coupling, right, state, partner, beside, middle, middle_ends, *arrivals)


def solution(mesh):
    return jax.shard_map(
        on_device,
        mesh=mesh,
        in_specs=(
            P("inst", "axial", None),
            P("inst", "axial", None),
            P("axial", None, None),
            P("axial", None, None),
            P("axial"),
        ),
        out_specs=P("inst", "axial", None),
        check_vma=False,
    )
```

```python
import functools

import jax
import jax.numpy as jnp
import numpy as np
from jax import lax
from jax.experimental import pallas as pl
from jax.experimental.pallas import tpu as pltpu
from jax.sharding import PartitionSpec as P

NT = (((1,), (1,)), ((), ()))
NN = (((1,), (0,)), ((), ()))
bf16 = jnp.bfloat16
f32 = jnp.float32
SMEM = pl.BlockSpec(memory_space=pltpu.SMEM)
VMEM = pl.BlockSpec(memory_space=pltpu.VMEM)
HBM = pl.BlockSpec(memory_space=pltpu.HBM)
CORES = 2


def params(mebibytes):
    return pltpu.CompilerParams(vmem_limit_bytes=mebibytes << 20)


def whereabouts():
    me, group = lax.axis_index("inst"), lax.axis_index("axial")
    return me % CORES, group % 2, me, group // 2


def batches(count):
    edges = [0]
    while edges[-1] < count:
        edges.append(min(count, max(1, 2 * edges[-1])))
    return dict(zip(edges, edges[1:]))


def mixing(period):
    distance = np.arange(period)[:, None] - np.arange(period)[None, :]
    angles = np.pi * distance / period
    sine = np.where(distance == 0, 1.0, np.sin(angles))
    parity = 1.0 - 2.0 * (distance % 2)
    derivative = np.where(distance == 0, 0.0, 0.5 * parity * np.cos(angles) / sine)
    mix = derivative * (2.0 / period) + np.eye(period)
    return mix, mix @ mix


def mixing_tables(devices, local):
    period = devices * local
    mix, twice = mixing(period)
    eye, none = np.eye(period), np.zeros((period, period))
    rights, chains = [], []
    for i in range(devices):
        rows = np.arange(local) + i * local
        right, chain = [], []
        for s in range(devices):
            columns = np.arange(local) + (i ^ s) * local
            cut = lambda upper, lower: np.concatenate([upper[rows][:, columns], lower[rows][:, columns]], 0)
            right += [cut(mix, 2 * eye), cut(-twice, -2 * mix)]
            chain += [cut(mix, 2 * eye), cut(-twice, -2 * mix), cut(none, -mix), cut(none, twice)]
        rights.append(np.concatenate(right, 1))
        chains.append(np.concatenate(chain, 1))
    rights, chains = np.stack(rights).astype(np.float32), np.stack(chains).astype(np.float32)
    high = rights.astype(bf16)
    low = (rights - high.astype(np.float32)).astype(bf16)
    return np.concatenate([high, low, high], 2), chains


def split(value):
    high = value.astype(bf16)
    return high, (value - high.astype(f32)).astype(bf16)


def block_dot(value, matrix):
    rows, width = value.shape
    main = width // 256 * 256
    high, low = split(value)
    if not main or 2 * (width - main) > 256:
        return tall_dot(value, matrix)
    both = jnp.concatenate([high[:, :main], low[:, :main]], 0)
    both = lax.dot_general(both, matrix[:, :main], NT, preferred_element_type=f32)
    both = both[:rows] + both[rows:]
    if width == main:
        return both
    rest = jnp.concatenate([high[:, main:], low[:, main:]], 1)
    twice = jnp.concatenate([matrix[:, main:], matrix[:, main:]], 1)
    return both + lax.dot_general(rest, twice, NT, preferred_element_type=f32)


def tall_dot(value, matrix):
    rows = value.shape[0]
    both = lax.dot_general(jnp.concatenate(split(value), 0), matrix, NT, preferred_element_type=f32)
    return both[:rows] + both[rows:]


def chain_kernel(order, inverse_hbm, coupling_hbm, state, forcing, whole, middle, ends, last_ends, packed,
                 inverse, coupling, both, inverse_sem, coupling_sem):
    place = whereabouts()
    tiles, width, _ = inverse.shape
    local = state.shape[0]
    part = width // CORES
    rows = part + 2 * local
    half = tiles // 2
    runs = batches(tiles)

    def fetch(k):
        tile = order[k]
        return (
            pltpu.make_async_copy(coupling_hbm.at[tile], coupling.at[k], coupling_sem.at[k]),
            pltpu.make_async_copy(inverse_hbm.at[tile], inverse.at[k], inverse_sem.at[k]),
        )

    for k in range(tiles):
        for copy in fetch(k):
            copy.start()

    def with_terms(k, turned):
        tile = order[k]
        terms = [array[i, pl.ds(tile, 1), :] for array in (forcing, state) for i in range(local)]
        terms = jnp.concatenate(terms, 0)
        packed[tile] = terms
        return jnp.concatenate([-turned[:part], terms - turned[part:]], 0)

    def keep_first(out, offset):
        out[0] = both[:part]
        ends[offset : offset + 2 * local] = both[part:rows]

    def keep_second(out, offset):
        out[1] = both[rows : rows + part]
        ends[offset + 2 * local : offset + 4 * local] = both[rows + part :]

    ids = lax.broadcasted_iota(jnp.int32, (rows, width), 0)
    columns = lax.broadcasted_iota(jnp.int32, (rows, width), 1)
    first = jnp.where((ids < part) & (columns == ids + place[0] * part), 1.0, 0.0)
    second = None
    for k in range(tiles + 1):
        for j in range(k, runs.get(k, k)):
            for copy in fetch(j):
                copy.wait()
        ahead = None
        if k == 0:
            ahead = with_terms(k, lax.dot_general(first.astype(bf16), coupling[k], NT, preferred_element_type=f32))
        elif k < tiles:
            ahead = with_terms(k, block_dot(first, coupling[k]))
        behind = None
        if k > 0:
            behind = first if k == 1 else first - block_dot(second, coupling[k - 1])
        if k < tiles:
            first = block_dot(ahead, inverse[k])
            both[:rows] = first
        if k > 0:
            second = block_dot(behind, inverse[k - 1])
            both[rows:] = second
        if k == half - 1:
            keep_first(middle, 4 * local)
        if k == half:
            keep_second(middle, 4 * local)
    keep_first(whole, 0)
    keep_second(whole, 0)
    last_ends[: 2 * local] = both[part:rows]
    last_ends[2 * local :] = both[rows + part :]


def chain(order, inverse, coupling, state, forcing):
    local, tiles, width = state.shape
    part = width // CORES
    half = jax.ShapeDtypeStruct((2, part, width), f32)
    return pl.pallas_call(
        chain_kernel,
        out_shape=(
            half,
            half,
            jax.ShapeDtypeStruct((8 * local, width), f32),
            jax.ShapeDtypeStruct((4 * local, width), f32),
            jax.ShapeDtypeStruct((tiles, 2 * local, width), f32),
        ),
        in_specs=[SMEM, HBM, HBM, VMEM, VMEM],
        scratch_shapes=[
            pltpu.VMEM((tiles, width, width), bf16),
            pltpu.VMEM((tiles, width, width), bf16),
            pltpu.VMEM((2 * (part + 2 * local), width), f32),
            pltpu.SemaphoreType.DMA((tiles,)),
            pltpu.SemaphoreType.DMA((tiles,)),
        ],
        name="chain",
        compiler_params=params(60),
    )(order, inverse, coupling, state, forcing)


def right_kernel(table, *refs):
    place = whereabouts()
    blocks, out = refs[:-1], refs[-1]
    weights = table[place[2]]
    for tile in range(out.shape[0]):
        high, low = split(jnp.concatenate([block[tile] for block in blocks], 0))
        out[tile] = lax.dot_general(weights, jnp.concatenate([high, high, low], 0), NN, preferred_element_type=f32)


def right_sides(table, blocks):
    return pl.pallas_call(
        right_kernel,
        out_shape=jax.ShapeDtypeStruct(blocks[0].shape, f32),
        in_specs=[VMEM] * (1 + len(blocks)),
        name="right_sides",
        compiler_params=params(12),
    )(table, *blocks)


def split_half(source, start, high, low):
    rows = source.shape[0]
    start = pl.multiple_of(start, 16)
    high[pl.ds(start, rows), :], low[pl.ds(start, rows), :] = split(source)


def times(value, high, low):
    upper, lower = split(value)
    rows = value.shape[0]
    both = lax.dot_general(jnp.concatenate([upper, lower], 0), high, NN, preferred_element_type=f32)
    return both[:rows] + both[rows:] + lax.dot_general(upper, low, NN, preferred_element_type=f32)


def carried(value, parts):
    rows = value.shape[0] // 2
    p_high, p_low, q_high, q_low = (parts[i] for i in range(4))
    moved = times(value, p_high, p_low)
    return jnp.concatenate([moved[:rows], moved[rows:] - times(value[:rows], q_high, q_low)], 0)


def prepare_kernel(mine, rest, out):
    place = whereabouts()
    rows = mine.shape[1]
    for i in range(2):
        split_half(mine[i], place[0] * rows, out.at[2 * i], out.at[2 * i + 1])
        split_half(rest[i], (1 - place[0]) * rows, out.at[2 * i], out.at[2 * i + 1])


def prepare(mine, rest, cost=0):
    width = mine.shape[2]
    return pl.pallas_call(
        prepare_kernel,
        out_shape=jax.ShapeDtypeStruct((4, width, width), bf16),
        in_specs=[VMEM, VMEM],
        name="prepare",
        cost_estimate=pl.CostEstimate(flops=cost, bytes_accessed=0, transcendentals=0),
        compiler_params=params(12),
    )(mine, rest)


def mixed(weights, blocks, start, count):
    rows = jnp.concatenate([block[start : start + count] for block in blocks], 0)
    return jnp.dot(weights, rows, precision=lax.Precision.HIGHEST, preferred_element_type=f32)


def mix_kernel(table, *refs):
    place = whereabouts()
    blocks, outs = refs[:-2], refs[-2:]
    count = blocks[0].shape[0] // 2
    for i, out in enumerate(outs):
        out[...] = mixed(table[place[2]], blocks, i * count, count)


def mix_ends(table, blocks):
    shape = jax.ShapeDtypeStruct((table.shape[1], blocks[0].shape[1]), f32)
    return pl.pallas_call(
        mix_kernel,
        out_shape=(shape, shape),
        in_specs=[VMEM] * (1 + len(blocks)),
        name="mix_ends",
        compiler_params=params(12),
    )(table, *blocks)


def pair_kernel(table, own, ends, *refs):
    place = whereabouts()
    blocks, (beside, total) = refs[:-2], refs[-2:]
    came = mixed(table[place[2]], blocks, 0, blocks[0].shape[0])
    beside[...] = came
    total[...] = ends[...]

    @pl.when(place[1] == 1)
    def _():
        total[...] = carried(came, own) + ends[...]


def pair_total(table, own, ends, blocks):
    shape = jax.ShapeDtypeStruct(ends.shape, f32)
    return pl.pallas_call(
        pair_kernel,
        out_shape=(shape, shape),
        in_specs=[VMEM] * (3 + len(blocks)),
        name="pair_total",
        compiler_params=params(12),
    )(table, own, ends, *blocks)


def carry_kernel(pair, own, partner, ends, beside, *refs):
    place = whereabouts()
    arrivals, out = refs[:-1], refs[-1]
    out[...] = ends[...]

    @pl.when((place[1] == 1) & (place[3] == pair))
    def _():
        out[...] = carried(carried(arrivals[0][...], partner) + beside[...], own) + ends[...]

    @pl.when((place[1] == 0) & (place[3] == pair))
    def _():
        out[...] = carried(carried(arrivals[-1][...], own) + ends[...], partner) + beside[...]


def carry(pair, own, partner, ends, beside, arrivals):
    return pl.pallas_call(
        functools.partial(carry_kernel, pair),
        out_shape=jax.ShapeDtypeStruct(ends.shape, f32),
        in_specs=[VMEM] * (4 + len(arrivals)),
        name="carry",
        compiler_params=params(12),
    )(own, partner, ends, beside, *arrivals)


def sweep_kernel(order, inverse, coupling, right, state, partner, beside, middle, middle_ends, *refs):
    place = whereabouts()
    arrivals, (out, at_group) = refs[:-2], refs[-2:]
    tiles, width, _ = inverse.shape
    local = state.shape[0]
    half = tiles // 2
    core, upper = place[0], place[1]

    inflow = jnp.zeros(at_group.shape, f32)
    for i, arrived in enumerate(arrivals[1:]):
        inflow = jnp.where(place[3] == i + 1, arrived[...], inflow)
    if arrivals:
        inflow = jnp.where((place[3] == 1) & (upper == 1), arrivals[0][...], inflow)
    at_group[...] = inflow

    @pl.when(upper == 1)
    def _():
        at_group[...] = carried(inflow, partner) + beside[...]

    starts = [at_group[...]]
    starts.append(carried(starts[0], middle) + middle_ends[...])
    a = [start[:local] for start in starts]
    w = [start[local:] for start in starts]
    for k in range(half):
        steps = [order[k], order[k + half]]
        here = [right[tile] for tile in steps]
        turned = [tall_dot(jnp.concatenate([a[s], w[s]], 0), coupling[tile]) for s, tile in enumerate(steps)]
        a = [tall_dot(here[s][:local] - turned[s][:local], inverse[tile]) for s, tile in enumerate(steps)]
        w = [tall_dot(here[s][local:] - a[s] - turned[s][local:], inverse[tile]) for s, tile in enumerate(steps)]
        for s, tile in enumerate(steps):
            for i in range(local):
                out[i, pl.ds(tile, 1), :] = state[i, pl.ds(tile, 1), :] + w[s][i : i + 1]


def sweep(order, inverse, coupling, right, state, *rest):
    local, _, width = state.shape
    return pl.pallas_call(
        sweep_kernel,
        out_shape=jax.ShapeDtypeStruct(state.shape, f32),
        in_specs=[SMEM] + [VMEM] * (4 + len(rest)),
        scratch_shapes=[pltpu.VMEM((2 * local, width), f32)],
        name="sweep",
        compiler_params=params(24),
    )(order, inverse, coupling, right, state, *rest)


def after(value, *others):
    return lax.optimization_barrier((value, *others))[0]


def on_device(state, forcing, inverse, coupling, order):
    local, tiles, width = state.shape
    groups = lax.axis_size("axial")
    devices = lax.axis_size("inst")
    right_table, chain_table = mixing_tables(devices, local)

    def over_inst(value, bit):
        return lax.ppermute(value, "inst", [(i, i ^ bit) for i in range(devices)])

    def over_pair(value):
        return lax.ppermute(value, "axial", [(g, g ^ 1) for g in range(groups)])

    def swapped(value, source, target):
        if groups & (groups - 1):
            return lax.ppermute(value, "axial", [(source, target)])
        return lax.ppermute(value, "axial", [(g, g ^ source ^ target) for g in range(groups)])

    def with_rest(value):
        return [value, over_inst(value, 1)]

    whole, middle, ends, last_ends, packed = chain(order, inverse, coupling, state, forcing)
    chain_table = jnp.asarray(chain_table)

    beside = over_pair(last_ends)
    blocks = [over_inst(ends, s) for s in range(1, devices)]
    first_block = blocks[0]
    partner = over_pair(whole)
    own = prepare(*with_rest(whole), 5 * 10**9)
    ends, middle_ends = mix_ends(chain_table, [ends] + blocks)
    beside = after(beside, blocks[0])
    blocks = [beside] + [over_inst(beside, s) for s in range(1, devices)]
    packed, middle = after(packed, first_block), after(middle, ends)
    packs = [packed] + [over_inst(packed, s) for s in range(CORES, devices, CORES)]
    middle = with_rest(middle)
    beside, total = pair_total(chain_table, own, ends, blocks)
    middle = prepare(after(middle[0], total), middle[1], 5 * 10**9)
    partner = prepare(*with_rest(after(partner, total)))

    arrivals = []
    if groups > 2:
        arrivals = [swapped(total, 1, 3), swapped(total, 1, 2)]
        arrivals[0] = after(arrivals[0], middle)
    leaving = total
    for pair in range(1, groups // 2 - 1):
        came = arrivals if pair == 1 else arrivals[-1:]
        leaving = carry(pair, own, partner, ends, beside, came)
        arrivals.append(swapped(leaving, 2 * pair, 2 * pair + 2))
        if pair == 1:
            packs = [after(pack, leaving) for pack in packs]
    packs = [block for pack in packs for block in (pack, over_inst(pack, 1))]
    right = right_sides(jnp.asarray(right_table), packs)
    if arrivals:
        arrivals[-1] = after(arrivals[-1], right)
    return sweep(order, inverse, coupling, right, state, partner, beside, middle, middle_ends, *arrivals)


def solution(mesh):
    return jax.shard_map(
        on_device,
        mesh=mesh,
        in_specs=(
            P("inst", "axial", None),
            P("inst", "axial", None),
            P("axial", None, None),
            P("axial", None, None),
            P("axial"),
        ),
        out_specs=P("inst", "axial", None),
        check_vma=False,
    )
```
